32 devices in a mesh: seq: 16 (over z, y, core), fsdp: 2 (over x).
Axes of the slice: x: 2, y: 2, z: 4, core: 2. Of those that a mesh axis runs over, the one named last changes fastest.
Arguments:
- tokens: bfloat16 [4096, 1024], P(('seq', 'fsdp')), may hold values from -6 to 6
- norm1_gain: bfloat16 [1024], P('seq'), may hold values from 0.5 to 1.5
- w_qkv: bfloat16 [1024, 3, 1024], P('seq', None, 'fsdp'), may hold values from -0.1875 to 0.1875
- w_attn_out: bfloat16 [1024, 1024], P('fsdp', 'seq'), may hold values from -2 to 2
- norm2_gain: bfloat16 [1024], P('seq'), may hold values from 0.5 to 1.5
- w_in: bfloat16 [1024, 2, 2624], P('seq', None, 'fsdp'), may hold values from -0.1875 to 0.1875
- w_down: bfloat16 [2624, 1024], P('fsdp', 'seq'), may hold values from -0.125 to 0.125
- cotangent: bfloat16 [4096, 1024], P(('seq', 'fsdp')), may hold values from -6 to 6
Outputs:
- output: bfloat16 [4096, 1024], P(('seq', 'fsdp'))
- grad_tokens: bfloat16 [4096, 1024], P(('seq', 'fsdp'))
- grad_norm1_gain: float32 [1024], P('seq')
- grad_w_qkv: float32 [1024, 3, 1024], P('seq', None, 'fsdp')
- grad_w_attn_out: float32 [1024, 1024], P('fsdp', 'seq')
- grad_norm2_gain: float32 [1024], P('seq')
- grad_w_in: float32 [1024, 2, 2624], P('seq', None, 'fsdp')
- grad_w_down: float32 [2624, 1024], P('fsdp', 'seq')
The draws below stay inside these ranges and needn't reach their ends.
All inputs are finite; a program needn't handle non-finite values.
Results may differ from the reference program's by a relative error of at most 0.019.
Values may be sent and summed in bfloat16 or wider, within the bound.
No kernel may reach another device: no remote copies, remote signals or barrier semaphores. Data moves between devices by JAX's collectives and lax.ppermute only.
A program may use at most 128 MiB of HBM per device.

```python
import jax
import jax.numpy as jnp
from jax import lax

D = 1024
HD = 64
FF = 2624
HALF = 64
TOKENS = 4096


def spiked(values, stream_key, source, target, blocks, factor):
    def block_of(position):
        return (jnp.arange(values.shape[position]) // (values.shape[position] // blocks)).reshape((-1,) + (1,) * (values.ndim - 1 - position))

    one_side = jax.random.permutation(stream_key, blocks)[block_of(target)]
    far = (block_of(target) + blocks // 2) % blocks
    return jnp.where((block_of(source) == one_side) | (block_of(source) == far), factor * values, values)


def steps_of(rng, extent, split, low, high):
    loudness = 1.0
    for axis_at, blocks in split:
        heights = jax.random.uniform(jax.random.fold_in(jax.random.fold_in(rng, 6), axis_at), (blocks,), jnp.float32, low / len(split), high / len(split))
        loudness = loudness * jnp.repeat(jnp.exp(heights), extent[axis_at] // blocks).reshape((-1,) + (1,) * (len(extent) - 1 - axis_at))
    return loudness


def gaussian(key, shape, deviation, reach, pieces=(), kind=jnp.bfloat16):
    drawn = deviation * jax.random.normal(key, shape, jnp.float32)
    if pieces:
        drawn = drawn * steps_of(key, shape, pieces, -0.22, 0.18)
    return jnp.clip(drawn, -reach, reach).astype(kind)


def heavy_noise(rng, shape, width, most, split, heavy, held_as=jnp.bfloat16):
    array = width * jax.random.normal(rng, shape, jnp.float32)
    if split:
        array = array * steps_of(rng, shape, split, -0.22, 0.18)
    return jnp.clip(spiked(array, jax.random.fold_in(rng, 3), *heavy), -most, most).astype(held_as)


def setup_inputs(seed: int = 0) -> dict:
    splits = jax.random.split(jax.random.key(seed), 9)
    tokens = heavy_noise(splits[0], (TOKENS, D), 1.0, 6.0, ((0, 32),), (0, 1, 32, 2.75))
    norm1_gain = jnp.clip(1.0 + 0.1 * jax.random.normal(splits[1], (D,), jnp.float32), 0.5, 1.5).astype(jnp.bfloat16)
    w_qkv = gaussian(splits[2], (D, 3, D), D ** -0.5, 0.1875, ((0, 16), (2, 2)))
    w_attn_out = gaussian(splits[3], (D, D), (D // (2 * HALF)) ** -0.5, 2.0, ((0, 2), (1, 16)))
    norm2_gain = jnp.clip(1.0 + 0.1 * jax.random.normal(splits[4], (D,), jnp.float32), 0.5, 1.5).astype(jnp.bfloat16)
    w_in = gaussian(splits[5], (D, 2, FF), D ** -0.5, 0.1875, ((0, 16), (2, 2)))
    w_down = gaussian(splits[6], (FF, D), FF ** -0.5, 0.125, ((0, 2), (1, 16)))
    cotangent = heavy_noise(splits[7], (TOKENS, D), 1.0, 6.0, ((0, 32),), (0, 1, 32, 2.75))
    return dict(tokens=tokens, norm1_gain=norm1_gain, w_qkv=w_qkv, w_attn_out=w_attn_out, norm2_gain=norm2_gain, w_in=w_in, w_down=w_down, cotangent=cotangent)


@jax.custom_vjp
def low(v):
    return lax.optimization_barrier(v.astype(jnp.bfloat16)).astype(jnp.float32)

@jax.custom_vjp
def low_back(v):
    return v

def low_keep(v):
    return (low(v), None)

def low_pass(kept, grad):
    return (grad,)

def back_keep(v):
    return (v, None)

def back_low(kept, grad):
    return (low(grad),)
low.defvjp(low_keep, low_pass)
low_back.defvjp(back_keep, back_low)
EPSILON = 1e-05
THETA = 10000.0
HIGHEST = lax.Precision.HIGHEST

def layer_norm(values, gain):
    average = lax.optimization_barrier(jnp.mean(values, axis=-1, keepdims=True))
    centered = values - average
    inverse = lax.rsqrt(lax.optimization_barrier(jnp.mean(centered * centered, axis=-1, keepdims=True)) + EPSILON)
    return centered * inverse * gain

def rotary_tables(positions, head_size):
    half_size = head_size // 2
    frequency = THETA ** (-(jnp.arange(half_size, dtype=jnp.float32) * 2.0) / head_size)
    angles = positions.astype(jnp.float32)[:, None] * frequency[None, :]
    return (jnp.cos(angles)[:, None, :], jnp.sin(angles)[:, None, :])

def rotate(values, cosine_table, sine_table):
    half_size = values.shape[-1] // 2
    first_half = values[..., :half_size]
    second_half = values[..., half_size:]
    return jnp.concatenate([first_half * cosine_table - second_half * sine_table, second_half * cosine_table + first_half * sine_table], axis=-1)

def layer_forward(tokens, norm1_gain, w_qkv, w_attn_out, norm2_gain, w_in, w_down):
    total_rows = tokens.shape[0]
    model_width = tokens.shape[1]
    heads_count = model_width // HD
    ff_width = w_down.shape[0]
    score_scale = 1.0 / HD ** 0.5
    qkv_matrix = w_qkv.reshape(model_width, 3 * model_width)
    in_matrix = w_in.reshape(model_width, 2 * ff_width)
    low_one = low(layer_norm(tokens, norm1_gain))
    qkv = low_back(jnp.dot(low_one, qkv_matrix, precision=HIGHEST))
    positions = jnp.arange(total_rows, dtype=jnp.int32)
    cosine_table, sine_table = rotary_tables(positions, HD)
    queries = low(rotate(qkv[:, :model_width].reshape(total_rows, heads_count, HD), cosine_table, sine_table))
    keys = low(rotate(qkv[:, model_width:2 * model_width].reshape(total_rows, heads_count, HD), cosine_table, sine_table))
    values = low(qkv[:, 2 * model_width:].reshape(total_rows, heads_count, HD))
    keys_pad = jnp.pad(keys, ((HALF, HALF), (0, 0), (0, 0)))
    values_pad = jnp.pad(values, ((HALF, HALF), (0, 0), (0, 0)))

    def attend(block_index):
        first_row = (block_index * 512).astype(jnp.int32)
        query_part = lax.dynamic_slice_in_dim(queries, first_row, 512, 0)
        key_part = lax.dynamic_slice_in_dim(keys_pad, first_row, 512 + 2 * HALF, 0)
        value_part = lax.dynamic_slice_in_dim(values_pad, first_row, 512 + 2 * HALF, 0)
        scores = jnp.einsum('qhd,khd->hqk', query_part, key_part, precision=HIGHEST) * score_scale
        scores = low_back(scores)
        query_pos = first_row + jnp.arange(512, dtype=jnp.int32)
        key_pos = first_row - HALF + jnp.arange(512 + 2 * HALF, dtype=jnp.int32)
        offset = key_pos[None, :] - query_pos[:, None]
        inside = (jnp.abs(offset) <= HALF) & (key_pos[None, :] >= 0) & (key_pos[None, :] < total_rows)
        softmax_rows = low(jax.nn.softmax(jnp.where(inside[None], scores, -1e+30), axis=-1))
        return jnp.einsum('hqk,khd->qhd', softmax_rows, value_part, precision=HIGHEST)
    context = lax.map(jax.checkpoint(attend), jnp.arange(total_rows // 512, dtype=jnp.int32))
    context = low(low_back(context.reshape(total_rows, model_width)))
    residual = tokens + low_back(jnp.dot(context, w_attn_out, precision=HIGHEST))
    low_two = low(layer_norm(residual, norm2_gain))
    projected = low_back(jnp.dot(low_two, in_matrix, precision=HIGHEST))
    hidden = low(jax.nn.gelu(projected[:, :ff_width], approximate=False) * projected[:, ff_width:])
    return residual + jnp.dot(hidden, w_down, precision=HIGHEST)

def reference(tokens, norm1_gain, w_qkv, w_attn_out, norm2_gain, w_in, w_down, cotangent):
    output, pullback = jax.vjp(layer_forward, tokens.astype(jnp.float32), norm1_gain.astype(jnp.float32), w_qkv.astype(jnp.float32), w_attn_out.astype(jnp.float32), norm2_gain.astype(jnp.float32), w_in.astype(jnp.float32), w_down.astype(jnp.float32))
    gradients = pullback(cotangent.astype(jnp.float32))
    return (output.astype(jnp.bfloat16), gradients[0].astype(jnp.bfloat16), gradients[1], gradients[2], gradients[3], gradients[4], gradients[5], gradients[6])
```

```python
import math

import jax
import jax.numpy as jnp
import numpy as np
from jax import lax
from jax.sharding import PartitionSpec as P

HD = 64
HALF = 64
LANES = 128

EPSILON = 1e-05
THETA = 10000.0
SEQ = "seq"
PAIR = "fsdp"
F32 = jnp.float32
BF16 = jnp.bfloat16


def passed_along(block, axis, distance):
    devices = range(lax.axis_size(axis))
    route = [(i - distance, i) for i in devices if i - distance in devices]
    return lax.ppermute(block, axis, route)


def pair_swap(block):
    return lax.ppermute(block, PAIR, [(0, 1), (1, 0)])


class Ring:
    def __init__(self):
        size = lax.axis_size(SEQ)
        self.chips = size // 2
        rows = self.chips // 2
        order = [2 * z for z in range(rows)] + [2 * z + 1 for z in reversed(range(rows))]
        place = np.argsort(np.array(order))
        self.up, self.down = [], []
        for i in range(size):
            chip, core = divmod(i, 2)
            self.up.append((i, order[(place[chip] + 1) % self.chips] * 2 + core))
            self.down.append((i, order[(place[chip] - 1) % self.chips] * 2 + core))
        self.swap = [(i, i ^ 1) for i in range(size)]
        me = lax.axis_index(SEQ)
        self.core = me % 2
        self.place = jnp.asarray(place, jnp.int32)[me // 2]
        self.order = jnp.asarray(order, jnp.int32)

    def chip_at(self, distance):
        return self.order[(self.place + distance + self.chips) % self.chips]

    def gather(self, block):
        rows, width = block.shape
        whole = jnp.zeros((2 * self.chips * rows, width), block.dtype)

        def put(whole, piece, distance):
            chip = self.chip_at(distance)
            other = lax.ppermute(piece, SEQ, self.swap)
            whole = lax.dynamic_update_slice(whole, piece, ((chip * 2 + self.core) * rows, 0))
            return lax.dynamic_update_slice(whole, other, ((chip * 2 + 1 - self.core) * rows, 0))

        whole = put(whole, block, 0)
        upward = downward = block
        half = self.chips // 2
        for step in range(1, half + 1):
            upward = lax.ppermute(upward, SEQ, self.up)
            if step < self.chips - half:
                downward = lax.ppermute(downward, SEQ, self.down)
                whole = put(whole, downward, step)
            whole = put(whole, upward, -step)
        return whole

    def scatter_sum(self, terms):
        rows, width = terms.shape[0] // (2 * self.chips), terms.shape[1]
        blocks = terms.reshape(self.chips, 2, rows, width)
        away = lax.dynamic_slice_in_dim(blocks, 1 - self.core, 1, 1)
        came = lax.ppermute(away, SEQ, self.swap)[:, 0]
        kept = lax.dynamic_slice_in_dim(blocks, self.core, 1, 1)[:, 0]
        held = (kept.astype(F32) + came.astype(F32)).astype(BF16)

        def at(distance):
            return lax.dynamic_slice_in_dim(held, self.chip_at(distance), 1, 0)[0]

        def joined(a, b):
            return (a.astype(F32) + b.astype(F32)).astype(BF16)

        half = self.chips // 2
        upward = at(half)
        for step in range(1, half + 1):
            upward = lax.ppermute(upward, SEQ, self.up)
            if step < half:
                upward = joined(upward, at(half - step))
        downward = at(half + 1)
        for step in range(1, self.chips - half):
            downward = lax.ppermute(downward, SEQ, self.down)
            if step < self.chips - half - 1:
                downward = joined(downward, at(half + 1 + step))
        return at(0).astype(F32) + upward.astype(F32) + downward.astype(F32)


def norm_rows(values, gain):
    average = jnp.mean(values, axis=-1, keepdims=True)
    centered = values - average
    inverse = lax.rsqrt(jnp.mean(centered * centered, axis=-1, keepdims=True) + EPSILON)
    unit_rows = centered * inverse
    return (unit_rows * gain, unit_rows, inverse)


def norm_back(grad_rows, gain, unit_rows, inverse):
    scaled = grad_rows * gain
    centered_grad = (
        scaled
        - jnp.mean(scaled, axis=-1, keepdims=True)
        - unit_rows * jnp.mean(scaled * unit_rows, axis=-1, keepdims=True)
    )
    return inverse * centered_grad


def rotary_tables(positions, head_size):
    half_size = head_size // 2
    frequency = THETA ** (-(jnp.arange(half_size, dtype=jnp.float32) * 2.0) / head_size)
    angles = positions.astype(jnp.float32)[:, None] * frequency[None, :]
    return (jnp.cos(angles)[:, None, :], jnp.sin(angles)[:, None, :])


def rotate(values, cosine_table, sine_table):
    half_size = values.shape[-1] // 2
    first_half = values[..., :half_size]
    second_half = values[..., half_size:]
    return jnp.concatenate(
        [
            first_half * cosine_table - second_half * sine_table,
            second_half * cosine_table + first_half * sine_table,
        ],
        axis=-1,
    )


def gated(gate_part, up_part):
    return jax.nn.gelu(gate_part, approximate=False) * up_part


def pair_rows(mine):
    other = pair_swap(mine)
    first = lax.axis_index(PAIR) == 0
    return jnp.concatenate([jnp.where(first, mine, other), jnp.where(first, other, mine)], axis=0)


def own_rows(values, row_count):
    return lax.dynamic_slice_in_dim(values, lax.axis_index(PAIR) * row_count, row_count, 0)


def other_rows(values, row_count):
    return lax.dynamic_slice_in_dim(values, (1 - lax.axis_index(PAIR)) * row_count, row_count, 0)


def dot(a, b, over=(1, 0)):
    return lax.dot_general(a, b, (((over[0],), (over[1],)), ((), ())), preferred_element_type=F32)


def padded_to_lanes(values):
    return jnp.pad(values, ((0, 0), (0, -values.shape[1] % LANES)))


def local(tokens, norm1_gain, w_qkv, w_attn_out, norm2_gain, w_in, w_down, cotangent):
    row_count, model_width = tokens.shape
    score_scale = 1.0 / math.sqrt(HD)
    ring = Ring()
    depth, _, width = w_qkv.shape
    units = w_down.shape[0]
    heads_here = width // HD
    gains = padded_to_lanes(jnp.stack([norm1_gain, norm2_gain], axis=1))
    blob_a = jnp.concatenate([w_qkv.reshape(depth, -1), w_attn_out.T, gains], axis=1)
    whole_a = ring.gather(blob_a)
    qkv_matrix = whole_a[:, : 3 * width]
    attn_matrix = whole_a[:, 3 * width : 4 * width]
    gain_columns = whole_a[:, 4 * width :].astype(F32)
    gain_one = gain_columns[:, 0]
    gain_two = gain_columns[:, 1]
    blob_b = jnp.concatenate(
        [padded_to_lanes(w_in[:, 0]), padded_to_lanes(w_in[:, 1]), padded_to_lanes(w_down.T)], axis=1
    )
    units_pad = blob_b.shape[1] // 3
    whole_b = lax.all_gather(blob_b, SEQ, axis=0, tiled=True)
    in_matrix = whole_b[:, : 2 * units_pad]
    down_matrix = whole_b[:, 2 * units_pad :]

    pair_size = lax.axis_size(PAIR)
    work_rows = row_count * pair_size
    work_start = lax.axis_index(SEQ) * work_rows
    all_rows = work_rows * lax.axis_size(SEQ)
    token_float = pair_rows(tokens).astype(F32)
    cot_work = pair_rows(cotangent)

    normed_one, unit_one, inverse_one = norm_rows(token_float, gain_one)
    work_one = normed_one.astype(BF16)
    query_pos = work_start + jnp.arange(work_rows, dtype=jnp.int32)
    key_pos = work_start - HALF + jnp.arange(work_rows + 2 * HALF, dtype=jnp.int32)
    offset = key_pos[None, :] - query_pos[:, None]
    inside = (jnp.abs(offset) <= HALF) & (key_pos[None, :] >= 0) & (key_pos[None, :] < all_rows)
    cosine_table, sine_table = rotary_tables(query_pos, HD)
    qkv = dot(work_one, qkv_matrix)
    queries = rotate(
        qkv[:, :width].reshape(work_rows, heads_here, HD), cosine_table, sine_table
    ).astype(BF16)
    keys_own = rotate(
        qkv[:, width : 2 * width].reshape(work_rows, heads_here, HD), cosine_table, sine_table
    )
    keys_own = keys_own.reshape(work_rows, width).astype(BF16)
    values_own = qkv[:, 2 * width :].astype(BF16)
    kv_own = jnp.concatenate([keys_own, values_own], axis=1)
    from_before = passed_along(kv_own[work_rows - HALF :], SEQ, 1)
    from_after = passed_along(kv_own[:HALF], SEQ, -1)
    padded = jnp.concatenate([from_before, kv_own, from_after], axis=0)
    keys_all = padded[:, :width].reshape(-1, heads_here, HD)
    values_all = padded[:, width:].reshape(-1, heads_here, HD)
    scores = jnp.einsum("qhd,khd->hqk", queries, keys_all, preferred_element_type=F32) * score_scale
    masked = jnp.where(inside[None], scores, -1e30)
    expo = jnp.exp(masked - jnp.max(masked, axis=-1, keepdims=True))
    softmax_rows = expo / jnp.sum(expo, axis=-1, keepdims=True)
    softmax_low = softmax_rows.astype(BF16)
    context = jnp.einsum("hqk,khd->qhd", softmax_low, values_all, preferred_element_type=F32)
    context = context.reshape(work_rows, width).astype(BF16)
    attn_term = dot(context, attn_matrix, (1, 1)).astype(BF16)
    attn_other = pair_swap(attn_term)
    residual = token_float + (attn_term.astype(F32) + attn_other.astype(F32))

    normed_two, unit_two, inverse_two = norm_rows(residual, gain_two)
    work_two = normed_two.astype(BF16)
    projected = dot(work_two, in_matrix)
    hidden, gate_back = jax.vjp(gated, projected[:, :units_pad], projected[:, units_pad:])
    hidden = hidden.astype(BF16)
    grad_hidden = dot(cot_work, down_matrix)
    grad_gate, grad_up = gate_back(grad_hidden)
    grad_proj = jnp.concatenate([grad_gate, grad_up], axis=1).astype(BF16)
    grad_two = dot(grad_proj, in_matrix, (1, 1)).astype(BF16)
    grad_two_other = pair_swap(grad_two)
    grad_low_two = grad_two.astype(F32) + grad_two_other.astype(F32)

    grad_down = dot(cot_work, hidden, (0, 0)).astype(BF16)
    grad_in = dot(work_two, grad_proj, (0, 0)).astype(BF16)
    terms_b = jnp.concatenate([grad_in, grad_down], axis=1)
    share_b = lax.psum_scatter(terms_b, SEQ, scatter_dimension=0, tiled=True).astype(F32)

    down_term = dot(hidden, down_matrix, (1, 1)).astype(BF16)
    down_other = pair_swap(other_rows(down_term, row_count))
    output = (
        own_rows(residual, row_count)
        + (own_rows(down_term, row_count).astype(F32) + down_other.astype(F32))
    ).astype(BF16)

    grad_gain_two = jnp.sum(grad_low_two * unit_two, axis=0)
    grad_residual = cot_work.astype(F32) + norm_back(grad_low_two, gain_two, unit_two, inverse_two)
    grad_res_work = grad_residual.astype(BF16)
    grad_attn = dot(grad_res_work, context, (0, 0)).astype(BF16)
    grad_context = dot(grad_res_work, attn_matrix).astype(BF16).reshape(work_rows, heads_here, HD)
    grad_softmax = jnp.einsum(
        "qhd,khd->hqk", grad_context, values_all, preferred_element_type=F32
    )
    grad_scores = softmax_rows * (
        grad_softmax - jnp.sum(grad_softmax * softmax_rows, axis=-1, keepdims=True)
    )
    grad_scores = grad_scores.astype(BF16)
    grad_queries = (
        jnp.einsum("hqk,khd->qhd", grad_scores, keys_all, preferred_element_type=F32) * score_scale
    )
    grad_keys = (
        jnp.einsum("hqk,qhd->khd", grad_scores, queries, preferred_element_type=F32) * score_scale
    )
    grad_values = jnp.einsum("hqk,qhd->khd", softmax_low, grad_context, preferred_element_type=F32)
    grad_padded = jnp.concatenate(
        [grad_keys.reshape(-1, width), grad_values.reshape(-1, width)], axis=1
    )
    from_next = passed_along(grad_padded[:HALF].astype(BF16), SEQ, -1).astype(F32)
    from_prev = passed_along(grad_padded[work_rows + HALF :].astype(BF16), SEQ, 1).astype(F32)
    grad_kv = jnp.concatenate(
        [
            grad_padded[HALF : 2 * HALF] + from_prev,
            grad_padded[2 * HALF : work_rows],
            grad_padded[work_rows : work_rows + HALF] + from_next,
        ],
        axis=0,
    )
    grad_key_rows = rotate(
        grad_kv[:, :width].reshape(work_rows, heads_here, HD), cosine_table, -sine_table
    )
    grad_query_rows = rotate(grad_queries, cosine_table, -sine_table)
    grad_qkv = jnp.concatenate(
        [
            grad_query_rows.reshape(work_rows, width),
            grad_key_rows.reshape(work_rows, width),
            grad_kv[:, width:],
        ],
        axis=1,
    ).astype(BF16)
    grad_one = dot(grad_qkv, qkv_matrix, (1, 1))
    grad_gain_one = jnp.sum(grad_one * unit_one, axis=0)
    gain_terms = jnp.stack([grad_gain_one, grad_gain_two], axis=1)
    gain_high = gain_terms.astype(BF16)
    gain_rest = (gain_terms - gain_high.astype(F32)).astype(BF16)
    grad_weight = dot(work_one, grad_qkv, (0, 0)).astype(BF16)
    terms_a = jnp.concatenate(
        [grad_weight, grad_attn, padded_to_lanes(jnp.concatenate([gain_high, gain_rest], axis=1))],
        axis=1,
    )
    share_a = ring.scatter_sum(terms_a)

    grad_one = grad_one.astype(BF16)
    one_other = pair_swap(other_rows(grad_one, row_count))
    grad_low_one = own_rows(grad_one, row_count).astype(F32) + one_other.astype(F32)
    grad_tokens = (
        own_rows(grad_residual, row_count)
        + norm_back(
            grad_low_one,
            gain_one,
            own_rows(unit_one, row_count),
            own_rows(inverse_one, row_count),
        )
    ).astype(BF16)

    share_gains = share_a[:, 4 * width : 4 * width + 2] + share_a[:, 4 * width + 2 : 4 * width + 4]
    share_gain_one = share_gains[:, 0]
    share_gain_one = share_gain_one + pair_swap(share_gain_one)
    return (
        output,
        grad_tokens,
        share_gain_one,
        share_a[:, : 3 * width].reshape(depth, 3, width),
        share_a[:, 3 * width : 4 * width].T,
        share_gains[:, 1],
        jnp.stack([share_b[:, :units], share_b[:, units_pad : units_pad + units]], axis=1),
        share_b[:, 2 * units_pad : 2 * units_pad + units].T,
    )


def solution(mesh):
    return jax.shard_map(
        local,
        mesh=mesh,
        in_specs=(
            P((SEQ, PAIR), None),
            P(SEQ),
            P(SEQ, None, PAIR),
            P(PAIR, SEQ),
            P(SEQ),
            P(SEQ, None, PAIR),
            P(PAIR, SEQ),
            P((SEQ, PAIR), None),
        ),
        out_specs=(
            P((SEQ, PAIR), None),
            P((SEQ, PAIR), None),
            P(SEQ),
            P(SEQ, None, PAIR),
            P(PAIR, SEQ),
            P(SEQ),
            P(SEQ, None, PAIR),
            P(PAIR, SEQ),
        ),
        check_vma=False,
    )
```

```python
import functools
import math

import jax
import jax.numpy as jnp
import numpy as np
from jax import lax
from jax.experimental import pallas as pl
from jax.experimental.pallas import tpu as pltpu
from jax.sharding import PartitionSpec as P

HD = 64
HALF = 64
LANES = 128

EPSILON = 1e-05
THETA = 10000.0
SEQ = "seq"
PAIR = "fsdp"
F32 = jnp.float32
BF16 = jnp.bfloat16


def passed_along(block, axis, distance):
    devices = range(lax.axis_size(axis))
    route = [(i - distance, i) for i in devices if i - distance in devices]
    return lax.ppermute(block, axis, route)


def pair_swap(block):
    return lax.ppermute(block, PAIR, [(0, 1), (1, 0)])


class Ring:
    def __init__(self, width):
        size = lax.axis_size(SEQ)
        self.chips = size // 2
        rows = self.chips // 2
        order = [2 * z for z in range(rows)] + [2 * z + 1 for z in reversed(range(rows))]
        place = np.argsort(np.array(order))
        self.up, self.down = [], []
        for i in range(size):
            chip, core = divmod(i, 2)
            self.up.append((i, order[(place[chip] + 1) % self.chips] * 2 + core))
            self.down.append((i, order[(place[chip] - 1) % self.chips] * 2 + core))
        self.swap = [(i, i ^ 1) for i in range(size)]
        me = lax.axis_index(SEQ)
        self.core = me % 2
        self.place = jnp.asarray(place, jnp.int32)[me // 2]
        self.order = jnp.asarray(order, jnp.int32)
        self.half = self.chips // 2
        self.slots = [self.half]
        for step in range(1, self.half):
            self.slots += [self.half + step, self.half - step]
        self.slots.append(0)
        self.short = width == LANES * self.chips

    def chips_at(self, distances):
        steps = jnp.asarray(distances, jnp.int32)
        return self.order[(self.place + steps + self.chips) % self.chips]

    def go(self, block, route):
        return lax.ppermute(block, SEQ, route)

    def gather(self, block):
        if not self.short:
            return lax.all_gather(block, SEQ, axis=0, tiled=True), []
        rows = block.shape[0]
        middle = rows // 2
        upward = downward = block
        got = {0: block}
        marks = []
        for step in range(1, self.half):
            upward = self.go(upward, self.up)
            downward = self.go(downward, self.down)
            got[-step], got[step] = upward, downward
            marks.append(upward)
        low = self.go(upward[:middle], self.up)
        high = self.go(downward[middle:], self.down)
        got[self.half] = jnp.concatenate([low, high], axis=0)
        distances = sorted(got)
        pieces = [got[d] for d in distances]
        others = [self.go(p, self.swap) for p in pieces]
        chips = self.chips_at(distances)
        starts = jnp.concatenate([chips * 2 + self.core, chips * 2 + 1 - self.core])
        return placed(starts, pieces + others), marks

    def scatter_sum(self, kept, away):
        rows = kept.shape[1]
        middle = rows // 2
        early = 3
        came_first = self.go(away[:early], self.swap)
        came_rest = self.go(away[early:], self.swap)

        def at(slot):
            i = self.slots.index(slot)
            came = came_first[i] if i < early else came_rest[i - early]
            return kept[i].astype(F32) + came.astype(F32)

        far = at(self.half).astype(BF16)
        upward = self.go(far[:middle], self.up)
        downward = self.go(far[middle:], self.down)
        for step in range(1, self.half):
            more_up = upward.astype(F32)
            more_down = downward.astype(F32)
            if step == 1:
                more_up = jnp.pad(more_up, ((0, rows - middle), (0, 0)))
                more_down = jnp.pad(more_down, ((middle, 0), (0, 0)))
            upward = self.go((at(self.half - step) + more_up).astype(BF16), self.up)
            downward = self.go((at(self.half + step) + more_down).astype(BF16), self.down)
        return at(0) + upward.astype(F32) + downward.astype(F32)


def placed_kernel(count, rows, starts, *refs):
    pieces, whole, ready = refs[:count], refs[count], refs[count + 1]
    copies = [
        pltpu.make_async_copy(
            pieces[i],
            whole.at[pl.ds(pl.multiple_of(starts[i] * rows, rows), rows), :],
            ready.at[i],
        )
        for i in range(count)
    ]
    for copy in copies:
        copy.start()
    for copy in copies:
        copy.wait()


def placed(starts, pieces):
    count, (rows, width) = len(pieces), pieces[0].shape
    anywhere = pl.BlockSpec(memory_space=pl.ANY)
    return pl.pallas_call(
        functools.partial(placed_kernel, count, rows),
        grid_spec=pltpu.PrefetchScalarGridSpec(
            num_scalar_prefetch=1,
            grid=(),
            in_specs=[anywhere] * count,
            out_specs=pl.BlockSpec(memory_space=pltpu.VMEM),
            scratch_shapes=[pltpu.SemaphoreType.DMA((count,))],
        ),
        compiler_params=pltpu.CompilerParams(vmem_limit_bytes=24 * 1024 * 1024),
        out_shape=jax.ShapeDtypeStruct((count * rows, width), pieces[0].dtype),
        cost_estimate=pl.CostEstimate(
            flops=0, bytes_accessed=4 * count * rows * width, transcendentals=0
        ),
    )(starts, *pieces)


def weight_kernel(chips, core, left_one, left_two, right_one, right_two, *refs):
    kept, away = refs[-2:]
    lower = core[0] == 0
    depth = kept.shape[1]

    def put(block, start, stop):
        kept[0, :, start:stop] = jnp.where(lower, block[:depth], block[depth:]).astype(BF16)
        away[0, :, start:stop] = jnp.where(lower, block[depth:], block[:depth]).astype(BF16)

    base = 0
    for left, right in ((left_one, right_one), (left_two, right_two)):
        width = right.shape[1]
        turned = left[...].T
        for start in range(0, width, 512):
            stop = min(width, start + 512)
            product = jnp.dot(turned, right[:, start:stop], preferred_element_type=F32)
            put(product, base + start, base + stop)
        base += width
    if len(refs) == 3:
        put(refs[0][...].astype(F32), base, base + refs[0].shape[1])


def weight_terms(ring, left_one, right_one, left_two, right_two, extra=None):
    work_rows, width = left_one.shape
    lanes = width // ring.chips
    depth = lanes // 2
    total = right_one.shape[1] + right_two.shape[1]
    more_args, more_specs = [], []
    if extra is not None:
        total += extra.shape[1]
        more_args.append(extra)
        more_specs.append(
            pl.BlockSpec((lanes, extra.shape[1]), lambda i, chips, core: (chips[i], 0))
        )

    def left_map(i, chips, core):
        return (0, chips[i])

    def whole_map(i, chips, core):
        return (0, 0)

    return pl.pallas_call(
        weight_kernel,
        grid_spec=pltpu.PrefetchScalarGridSpec(
            num_scalar_prefetch=2,
            grid=(ring.chips,),
            in_specs=[
                pl.BlockSpec((work_rows, lanes), left_map),
                pl.BlockSpec((work_rows, lanes), left_map),
                pl.BlockSpec(right_one.shape, whole_map),
                pl.BlockSpec(right_two.shape, whole_map),
                *more_specs,
            ],
            out_specs=[
                pl.BlockSpec((1, depth, total), lambda i, chips, core: (i, 0, 0)),
                pl.BlockSpec((1, depth, total), lambda i, chips, core: (i, 0, 0)),
            ],
        ),
        out_shape=[
            jax.ShapeDtypeStruct((ring.chips, depth, total), BF16),
            jax.ShapeDtypeStruct((ring.chips, depth, total), BF16),
        ],
        compiler_params=pltpu.CompilerParams(vmem_limit_bytes=40 * 1024 * 1024),
        cost_estimate=pl.CostEstimate(
            flops=2 * work_rows * width * total,
            bytes_accessed=2 * (width + work_rows) * total,
            transcendentals=0,
        ),
    )(
        ring.chips_at(ring.slots),
        ring.core.reshape(1),
        left_one,
        left_two,
        right_one,
        right_two,
        *more_args,
    )


def summed_terms(ring, *factors):
    if ring.short:
        return ring.scatter_sum(*weight_terms(ring, *factors))
    left_one, right_one, left_two, right_two, *extra = factors
    terms = [dot(left_one, right_one, (0, 0)), dot(left_two, right_two, (0, 0))]
    terms = jnp.concatenate([t.astype(BF16) for t in terms] + extra, axis=1)
    return lax.psum_scatter(terms, SEQ, scatter_dimension=0, tiled=True).astype(F32)


def norm_rows(values, gain):
    average = jnp.mean(values, axis=-1, keepdims=True)
    centered = values - average
    inverse = lax.rsqrt(jnp.mean(centered * centered, axis=-1, keepdims=True) + EPSILON)
    unit_rows = centered * inverse
    return (unit_rows * gain, unit_rows, inverse)


def norm_back(grad_rows, gain, unit_rows, inverse):
    scaled = grad_rows * gain
    centered_grad = (
        scaled
        - jnp.mean(scaled, axis=-1, keepdims=True)
        - unit_rows * jnp.mean(scaled * unit_rows, axis=-1, keepdims=True)
    )
    return inverse * centered_grad


def rotary_tables(positions, head_size):
    half_size = head_size // 2
    frequency = THETA ** (-(jnp.arange(half_size, dtype=jnp.float32) * 2.0) / head_size)
    angles = positions.astype(jnp.float32)[:, None] * frequency[None, :]
    return (jnp.cos(angles)[:, None, :], jnp.sin(angles)[:, None, :])


def rotate(values, cosine_table, sine_table):
    half_size = values.shape[-1] // 2
    first_half = values[..., :half_size]
    second_half = values[..., half_size:]
    return jnp.concatenate(
        [
            first_half * cosine_table - second_half * sine_table,
            second_half * cosine_table + first_half * sine_table,
        ],
        axis=-1,
    )


def gated(gate_part, up_part):
    return jax.nn.gelu(gate_part, approximate=False) * up_part


def pair_rows(mine):
    other = pair_swap(mine)
    first = lax.axis_index(PAIR) == 0
    return jnp.concatenate([jnp.where(first, mine, other), jnp.where(first, other, mine)], axis=0)


def own_rows(values, row_count):
    return lax.dynamic_slice_in_dim(values, lax.axis_index(PAIR) * row_count, row_count, 0)


def other_rows(values, row_count):
    return lax.dynamic_slice_in_dim(values, (1 - lax.axis_index(PAIR)) * row_count, row_count, 0)


def dot(a, b, over=(1, 0)):
    return lax.dot_general(a, b, (((over[0],), (over[1],)), ((), ())), preferred_element_type=F32)


def padded_to_lanes(values):
    return jnp.pad(values, ((0, 0), (0, -values.shape[1] % LANES)))


def local(tokens, norm1_gain, w_qkv, w_attn_out, norm2_gain, w_in, w_down, cotangent):
    row_count, model_width = tokens.shape
    score_scale = 1.0 / math.sqrt(HD)
    ring = Ring(model_width)
    depth, _, width = w_qkv.shape
    units = w_down.shape[0]
    heads_here = width // HD
    gains = padded_to_lanes(jnp.stack([norm1_gain, norm2_gain], axis=1))
    blob_a = jnp.concatenate([w_qkv.reshape(depth, -1), w_attn_out.T, gains], axis=1)
    whole_a, marks = ring.gather(blob_a)
    qkv_matrix = whole_a[:, : 3 * width]
    attn_matrix = whole_a[:, 3 * width : 4 * width]
    gain_columns = whole_a[:, 4 * width :].astype(F32)
    gain_one = gain_columns[:, 0]
    gain_two = gain_columns[:, 1]
    blob_b = jnp.concatenate(
        [padded_to_lanes(w_in[:, 0]), padded_to_lanes(w_in[:, 1]), padded_to_lanes(w_down.T)], axis=1
    )
    units_pad = blob_b.shape[1] // 3
    whole_b, _ = ring.gather(blob_b)
    in_matrix = whole_b[:, : 2 * units_pad]
    down_matrix = whole_b[:, 2 * units_pad :]

    pair_size = lax.axis_size(PAIR)
    work_rows = row_count * pair_size
    work_start = lax.axis_index(SEQ) * work_rows
    all_rows = work_rows * lax.axis_size(SEQ)
    token_float = pair_rows(tokens).astype(F32)
    cot_work = pair_rows(cotangent)

    normed_one, unit_one, inverse_one = norm_rows(token_float, gain_one)
    work_one = normed_one.astype(BF16)
    query_pos = work_start + jnp.arange(work_rows, dtype=jnp.int32)
    key_pos = work_start - HALF + jnp.arange(work_rows + 2 * HALF, dtype=jnp.int32)
    offset = key_pos[None, :] - query_pos[:, None]
    inside = (jnp.abs(offset) <= HALF) & (key_pos[None, :] >= 0) & (key_pos[None, :] < all_rows)
    cosine_table, sine_table = rotary_tables(query_pos, HD)
    qkv = dot(work_one, qkv_matrix)
    queries = rotate(
        qkv[:, :width].reshape(work_rows, heads_here, HD), cosine_table, sine_table
    ).astype(BF16)
    keys_own = rotate(
        qkv[:, width : 2 * width].reshape(work_rows, heads_here, HD), cosine_table, sine_table
    )
    keys_own = keys_own.reshape(work_rows, width).astype(BF16)
    values_own = qkv[:, 2 * width :].astype(BF16)
    kv_own = jnp.concatenate([keys_own, values_own], axis=1)
    from_before = passed_along(kv_own[work_rows - HALF :], SEQ, 1)
    from_after = passed_along(kv_own[:HALF], SEQ, -1)
    padded = jnp.concatenate([from_before, kv_own, from_after], axis=0)
    keys_all = padded[:, :width].reshape(-1, heads_here, HD)
    values_all = padded[:, width:].reshape(-1, heads_here, HD)
    scores = jnp.einsum("qhd,khd->hqk", queries, keys_all, preferred_element_type=F32) * score_scale
    masked = jnp.where(inside[None], scores, -1e30)
    expo = jnp.exp(masked - jnp.max(masked, axis=-1, keepdims=True))
    softmax_rows = expo / jnp.sum(expo, axis=-1, keepdims=True)
    softmax_low = softmax_rows.astype(BF16)
    context = jnp.einsum("hqk,khd->qhd", softmax_low, values_all, preferred_element_type=F32)
    context = context.reshape(work_rows, width).astype(BF16)
    attn_term = dot(context, attn_matrix, (1, 1)).astype(BF16)
    attn_other = pair_swap(attn_term)
    residual = token_float + (attn_term.astype(F32) + attn_other.astype(F32))

    normed_two, unit_two, inverse_two = norm_rows(residual, gain_two)
    work_two = normed_two.astype(BF16)
    projected = dot(work_two, in_matrix)
    hidden, gate_back = jax.vjp(gated, projected[:, :units_pad], projected[:, units_pad:])
    hidden = hidden.astype(BF16)
    grad_hidden = dot(cot_work, down_matrix)
    grad_gate, grad_up = gate_back(grad_hidden)
    grad_proj = jnp.concatenate([grad_gate, grad_up], axis=1).astype(BF16)
    grad_two = dot(grad_proj, in_matrix, (1, 1)).astype(BF16)
    grad_two_other = pair_swap(grad_two)
    grad_low_two = grad_two.astype(F32) + grad_two_other.astype(F32)

    share_b = summed_terms(ring, work_two, grad_proj, cot_work, hidden)

    down_term = dot(hidden, down_matrix, (1, 1)).astype(BF16)
    down_other = pair_swap(other_rows(down_term, row_count))
    output = (
        own_rows(residual, row_count)
        + (own_rows(down_term, row_count).astype(F32) + down_other.astype(F32))
    ).astype(BF16)

    grad_gain_two = jnp.sum(grad_low_two * unit_two, axis=0)
    grad_residual = cot_work.astype(F32) + norm_back(grad_low_two, gain_two, unit_two, inverse_two)
    grad_res_work = grad_residual.astype(BF16)
    grad_context = dot(grad_res_work, attn_matrix).astype(BF16).reshape(work_rows, heads_here, HD)
    grad_softmax = jnp.einsum(
        "qhd,khd->hqk", grad_context, values_all, preferred_element_type=F32
    )
    grad_scores = softmax_rows * (
        grad_softmax - jnp.sum(grad_softmax * softmax_rows, axis=-1, keepdims=True)
    )
    grad_scores = grad_scores.astype(BF16)
    grad_queries = (
        jnp.einsum("hqk,khd->qhd", grad_scores, keys_all, preferred_element_type=F32) * score_scale
    )
    grad_keys = (
        jnp.einsum("hqk,qhd->khd", grad_scores, queries, preferred_element_type=F32) * score_scale
    )
    grad_values = jnp.einsum("hqk,qhd->khd", softmax_low, grad_context, preferred_element_type=F32)
    grad_padded = jnp.concatenate(
        [grad_keys.reshape(-1, width), grad_values.reshape(-1, width)], axis=1
    )
    from_next = passed_along(grad_padded[:HALF].astype(BF16), SEQ, -1).astype(F32)
    from_prev = passed_along(grad_padded[work_rows + HALF :].astype(BF16), SEQ, 1).astype(F32)
    grad_kv = jnp.concatenate(
        [
            grad_padded[HALF : 2 * HALF] + from_prev,
            grad_padded[2 * HALF : work_rows],
            grad_padded[work_rows : work_rows + HALF] + from_next,
        ],
        axis=0,
    )
    grad_key_rows = rotate(
        grad_kv[:, :width].reshape(work_rows, heads_here, HD), cosine_table, -sine_table
    )
    grad_query_rows = rotate(grad_queries, cosine_table, -sine_table)
    grad_qkv = jnp.concatenate(
        [
            grad_query_rows.reshape(work_rows, width),
            grad_key_rows.reshape(work_rows, width),
            grad_kv[:, width:],
        ],
        axis=1,
    ).astype(BF16)
    grad_one = dot(grad_qkv, qkv_matrix, (1, 1))
    grad_gain_one = jnp.sum(grad_one * unit_one, axis=0)
    gain_terms = jnp.stack([grad_gain_one, grad_gain_two], axis=1)
    gain_high = gain_terms.astype(BF16)
    gain_rest = (gain_terms - gain_high.astype(F32)).astype(BF16)
    gain_columns = padded_to_lanes(jnp.concatenate([gain_high, gain_rest], axis=1))
    share_a = summed_terms(ring, work_one, grad_qkv, grad_res_work, context, gain_columns)

    grad_one = grad_one.astype(BF16)
    one_other = pair_swap(other_rows(grad_one, row_count))
    grad_low_one = own_rows(grad_one, row_count).astype(F32) + one_other.astype(F32)
    grad_tokens = (
        own_rows(grad_residual, row_count)
        + norm_back(
            grad_low_one,
            gain_one,
            own_rows(unit_one, row_count),
            own_rows(inverse_one, row_count),
        )
    ).astype(BF16)

    share_gains = share_a[:, 4 * width : 4 * width + 2] + share_a[:, 4 * width + 2 : 4 * width + 4]
    share_gain_one = share_gains[:, 0]
    share_gain_one = share_gain_one + pair_swap(share_gain_one)
    return (
        output,
        grad_tokens,
        share_gain_one,
        share_a[:, : 3 * width].reshape(depth, 3, width),
        share_a[:, 3 * width : 4 * width].T,
        share_gains[:, 1],
        jnp.stack([share_b[:, :units], share_b[:, units_pad : units_pad + units]], axis=1),
        share_b[:, 2 * units_pad : 2 * units_pad + units].T,
    )


def solution(mesh):
    return jax.shard_map(
        local,
        mesh=mesh,
        in_specs=(
            P((SEQ, PAIR), None),
            P(SEQ),
            P(SEQ, None, PAIR),
            P(PAIR, SEQ),
            P(SEQ),
            P(SEQ, None, PAIR),
            P(PAIR, SEQ),
            P((SEQ, PAIR), None),
        ),
        out_specs=(
            P((SEQ, PAIR), None),
            P((SEQ, PAIR), None),
            P(SEQ),
            P(SEQ, None, PAIR),
            P(PAIR, SEQ),
            P(SEQ),
            P(SEQ, None, PAIR),
            P(PAIR, SEQ),
        ),
        check_vma=False,
    )
```

```python
import functools
import math

import jax
import jax.numpy as jnp
import numpy as np
from jax import lax
from jax.experimental import pallas as pl
from jax.experimental.pallas import tpu as pltpu
from jax.sharding import PartitionSpec as P

HD = 64
HALF = 64
LANES = 128

EPSILON = 1e-05
THETA = 10000.0
SEQ = "seq"
PAIR = "fsdp"
F32 = jnp.float32
BF16 = jnp.bfloat16


def passed_along(block, axis, distance):
    devices = range(lax.axis_size(axis))
    route = [(i - distance, i) for i in devices if i - distance in devices]
    return lax.ppermute(block, axis, route)


def pair_swap(block):
    return lax.ppermute(block, PAIR, [(0, 1), (1, 0)])


class Ring:
    def __init__(self, width):
        size = lax.axis_size(SEQ)
        self.chips = size // 2
        rows = self.chips // 2
        order = [2 * z for z in range(rows)] + [2 * z + 1 for z in reversed(range(rows))]
        place = np.argsort(np.array(order))
        self.up, self.down = [], []
        for i in range(size):
            chip, core = divmod(i, 2)
            self.up.append((i, order[(place[chip] + 1) % self.chips] * 2 + core))
            self.down.append((i, order[(place[chip] - 1) % self.chips] * 2 + core))
        self.swap = [(i, i ^ 1) for i in range(size)]
        me = lax.axis_index(SEQ)
        self.core = me % 2
        self.place = jnp.asarray(place, jnp.int32)[me // 2]
        self.order = jnp.asarray(order, jnp.int32)
        self.half = self.chips // 2
        self.slots = [self.half]
        for step in range(1, self.half):
            self.slots += [self.half + step, self.half - step]
        self.slots.append(0)
        self.short = width == LANES * self.chips

    def chips_at(self, distances):
        steps = jnp.asarray(distances, jnp.int32)
        return self.order[(self.place + steps + self.chips) % self.chips]

    def go(self, block, route, name):
        with jax.named_scope(name):
            return lax.ppermute(block, SEQ, route)

    def gather(self, block, name):
        if not self.short:
            whole = lax.all_gather(block, SEQ, axis=0, tiled=True)
            return [whole], jnp.zeros(1, jnp.int32)
        rows = block.shape[0]
        middle = rows // 2
        upward = downward = block
        got = {0: block}
        for step in range(1, self.half):
            upward = self.go(upward, self.up, f"{name}_up_{step}")
            downward = self.go(downward, self.down, f"{name}_down_{step}")
            upward, downward = yield upward, downward
            got[-step], got[step] = upward, downward
        low = self.go(upward[:middle], self.up, f"{name}_up_{self.half}")
        high = self.go(downward[middle:], self.down, f"{name}_down_{self.half}")
        got[self.half] = jnp.concatenate([low, high], axis=0)
        distances = sorted(got, key=abs)
        pieces = [got[d] for d in distances]
        others = [self.go(p, self.swap, f"{name}_cores_{d}") for d, p in zip(distances, pieces)]
        chips = self.chips_at(distances)
        starts = jnp.concatenate([chips * 2 + self.core, chips * 2 + 1 - self.core]) * rows
        return pieces + others, starts

    def scatter_sum(self, kept, away, name):
        rows = kept.shape[1]
        middle = rows // 2
        away = yield away
        early = 3
        came_first = self.go(away[:early], self.swap, f"{name}_cores_early")
        came_rest = self.go(away[early:], self.swap, f"{name}_cores_rest")

        def at(slot):
            i = self.slots.index(slot)
            came = came_first[i] if i < early else came_rest[i - early]
            return kept[i].astype(F32) + came.astype(F32)

        far = at(self.half).astype(BF16)
        upward, downward = far[:middle], far[middle:]
        for step in range(1, self.half):
            upward, downward = yield upward, downward
            more_up = self.go(upward, self.up, f"{name}_up_{step}").astype(F32)
            more_down = self.go(downward, self.down, f"{name}_down_{step}").astype(F32)
            if step == 1:
                more_up = jnp.pad(more_up, ((0, rows - middle), (0, 0)))
                more_down = jnp.pad(more_down, ((middle, 0), (0, 0)))
            upward = (at(self.half - step) + more_up).astype(BF16)
            downward = (at(self.half + step) + more_down).astype(BF16)
        upward, downward = yield upward, downward
        upward = self.go(upward, self.up, f"{name}_up_{self.half}")
        downward = self.go(downward, self.down, f"{name}_down_{self.half}")
        return at(0) + upward.astype(F32) + downward.astype(F32)


class Stepped:
    def __init__(self, steps):
        self.steps, self.state, self.result = steps, None, None
        self.advance()

    def advance(self):
        try:
            if self.state is not None:
                self.state = lax.optimization_barrier(self.state)
            self.state = self.steps.send(self.state)
        except StopIteration as end:
            self.steps, self.state, self.result = None, None, end.value

    def ride(self, value):
        if self.steps is not None:
            value, self.state = lax.optimization_barrier((value, self.state))
            self.advance()
        return value

    def step(self):
        if self.steps is not None:
            self.advance()

    def beside(self, other):
        if self.steps is not None and other.steps is not None:
            self.state, other.state = lax.optimization_barrier((self.state, other.state))
            self.advance()
            other.advance()

    def finish(self):
        while self.steps is not None:
            self.advance()
        return self.result


VMEM = pl.BlockSpec(memory_space=pltpu.VMEM)
ANY = pl.BlockSpec(memory_space=pl.ANY)
SMEM = pl.BlockSpec(memory_space=pltpu.SMEM)
MIB = 1024 * 1024


def shape_of(rows, columns, kind):
    return jax.ShapeDtypeStruct((rows, columns), kind)


def call(kernel, args, specs, outs, scratch=(), flops=0, moved=0, room=48):
    return pl.pallas_call(
        kernel,
        in_specs=specs,
        out_specs=[VMEM] * len(outs),
        out_shape=outs,
        scratch_shapes=list(scratch),
        compiler_params=pltpu.CompilerParams(vmem_limit_bytes=room * MIB),
        cost_estimate=pl.CostEstimate(flops=flops, bytes_accessed=moved, transcendentals=0),
    )(*args)


def placing(starts, pieces, whole, ready):
    copies = []
    for i, piece in enumerate(pieces):
        rows = piece.shape[0]
        start = pl.multiple_of(starts[i], rows)
        copies.append(
            pltpu.make_async_copy(piece, whole.at[pl.ds(start, rows), :], ready.at[i])
        )
    return copies


def lane_of(rows, width):
    return lax.broadcasted_iota(jnp.int32, (rows, width), 1)


def halves_swapped(values):
    width = values.shape[1]
    lane = lane_of(*values.shape)
    ahead = pltpu.roll(values, width - HD // 2, 1)
    behind = pltpu.roll(values, HD // 2, 1)
    return jnp.where(lane % HD < HD // 2, ahead, behind)


def turned_by(values, cosine, sine):
    copies = values.shape[1] // LANES
    cosine = jnp.concatenate([cosine] * copies, axis=1)
    sine = jnp.concatenate([sine] * copies, axis=1)
    return values * cosine + halves_swapped(values) * sine


def unit_of(values):
    average = jnp.mean(values, axis=-1, keepdims=True)
    centered = values - average
    inverse = lax.rsqrt(jnp.mean(centered * centered, axis=-1, keepdims=True) + EPSILON)
    return centered * inverse, inverse


def first_kernel(count, width, starts, tokens, cosine, sine, *refs):
    pieces = refs[:count]
    whole, matrix, gains, work, queries, keys_values, first, last, ready = refs[count:]
    copies = placing(starts, pieces, whole, ready)
    for copy in copies:
        copy.start()
    unit, _ = unit_of(tokens[...].astype(F32))
    for copy in copies:
        copy.wait()
    matrix[...] = whole[:, 3 * width : 4 * width]
    gains[...] = whole[:, 4 * width :].astype(F32).T[:8]
    work[...] = (unit * gains[0:1, :]).astype(BF16)
    rows = work.shape[0]
    for start in range(0, 3 * width, 256):
        part = dot(work[...], whole[:, start : start + 256])
        if start < 2 * width:
            part = turned_by(part, cosine[...], sine[...])
        part = part.astype(BF16)
        if start < width:
            queries[:, start : start + 256] = part
        else:
            at = slice(start - width, start - width + 256)
            keys_values[:, at] = part
            first[:, at] = part[:HALF]
            last[:, at] = part[rows - HALF :]


def window(seq, tile, tiles):
    row = lax.broadcasted_iota(jnp.int32, (2 * LANES, 2 * LANES), 0) % LANES
    column = lax.broadcasted_iota(jnp.int32, (2 * LANES, 2 * LANES), 1)
    ahead = column - row
    inside = (ahead >= 0) & (ahead <= 2 * HALF)
    if tile == 0:
        inside &= (seq[0] > 0) | (column >= HALF)
    if tile == tiles - 1:
        inside &= (seq[0] < seq[1] - 1) | (column < 2 * LANES - HALF)
    return inside


def heads_apart(pair):
    lane = lane_of(*pair.shape)
    zero = jnp.zeros_like(pair)
    return jnp.concatenate(
        [jnp.where(lane < HD, pair, zero), jnp.where(lane < HD, zero, pair)], axis=0
    )


def heads_joined(apart):
    rows = apart.shape[0] // 2
    return jnp.where(lane_of(rows, apart.shape[1]) < HD, apart[:rows], apart[rows:])


def shares_of(apart, keys, inside):
    scores = dot(apart, keys, (1, 1)) * (1.0 / math.sqrt(HD))
    scores = jnp.where(inside, scores, -1e30)
    expo = jnp.exp(scores - jnp.max(scores, axis=-1, keepdims=True))
    return expo / jnp.sum(expo, axis=-1, keepdims=True)


def joined_rows(before, own, after, whole):
    rows = own.shape[0]
    whole[:HALF] = before[...]
    whole[HALF : HALF + rows] = own[...]
    whole[HALF + rows :] = after[...]


def attend_kernel(seq, queries, own, before, after, matrix, context, term, keys_values):
    rows, width = queries.shape
    joined_rows(before, own, after, keys_values)
    tiles = rows // LANES
    for tile in range(tiles):
        inside = window(seq, tile, tiles)
        at = slice(tile * LANES, tile * LANES + LANES)
        reach = slice(tile * LANES, tile * LANES + 2 * LANES)
        for start in range(0, width, LANES):
            columns = slice(start, start + LANES)
            apart = heads_apart(queries[at, columns])
            shares = shares_of(apart, keys_values[reach, columns], inside)
            values = keys_values[reach, width + start : width + start + LANES]
            context[at, columns] = heads_joined(dot(shares.astype(BF16), values)).astype(BF16)
    term[...] = dot(context[...], matrix[...], (1, 1)).astype(BF16)


def hidden_kernel(count, starts, tokens, term, term_other, gains, cot, *refs):
    pieces = refs[:count]
    residual, work, hidden, grad_proj, grad_two, down, whole, ready = refs[count:]
    copies = placing(starts, pieces, whole, ready)
    for copy in copies:
        copy.start()
    added = term[...].astype(F32) + term_other[...].astype(F32)
    residual[...] = tokens[...].astype(F32) + added
    unit, _ = unit_of(residual[...])
    work[...] = (unit * gains[1:2, :]).astype(BF16)
    for copy in copies:
        copy.wait()
    units = hidden.shape[1]
    for start in range(0, units, 256):
        stop = min(units, start + 256)
        gate = dot(work[...], whole[:, start:stop])
        up = dot(work[...], whole[:, units + start : units + stop])
        back = dot(cot[...], whole[:, 2 * units + start : 2 * units + stop])
        share = 0.5 + 0.5 * lax.erf(gate * (1.0 / math.sqrt(2.0)))
        bell = jnp.exp(-0.5 * gate * gate) * (1.0 / math.sqrt(2.0 * math.pi))
        gelu = gate * share
        hidden[:, start:stop] = (gelu * up).astype(BF16)
        grad_proj[:, start:stop] = (back * up * (share + gate * bell)).astype(BF16)
        grad_proj[:, units + start : units + stop] = (back * gelu).astype(BF16)
    grad_two[...] = dot(grad_proj[...], whole[:, : 2 * units], (1, 1)).astype(BF16)
    down[...] = dot(hidden[...], whole[:, 2 * units :], (1, 1)).astype(BF16)


def attend_back_kernel(
    seq, residual, gains, grad_two, grad_two_other, cot, matrix, queries, own, before, after,
    cosine, sine, grad_residual, grad_low, gain_two, grad_queries, grad_own, to_before, to_after,
    keys_values, grad_all,
):
    rows, width = queries.shape
    joined_rows(before, own, after, keys_values)
    unit, inverse = unit_of(residual[...])
    grad = grad_two[...].astype(F32) + grad_two_other[...].astype(F32)
    gain_two[...] = jnp.broadcast_to(jnp.sum(grad * unit, axis=0, keepdims=True), gain_two.shape)
    scaled = grad * gains[1:2, :]
    middle = jnp.mean(scaled, axis=-1, keepdims=True)
    along = jnp.mean(scaled * unit, axis=-1, keepdims=True)
    total = cot[...].astype(F32) + inverse * (scaled - middle - unit * along)
    grad_residual[...] = total
    grad_low[...] = total.astype(BF16)
    grad_context = dot(grad_low[...], matrix[...]).astype(BF16)
    grad_all[...] = jnp.zeros_like(grad_all)
    scale = 1.0 / math.sqrt(HD)
    tiles = rows // LANES
    for tile in range(tiles):
        inside = window(seq, tile, tiles)
        at = slice(tile * LANES, tile * LANES + LANES)
        reach = slice(tile * LANES, tile * LANES + 2 * LANES)
        for start in range(0, width, LANES):
            columns = slice(start, start + LANES)
            beside = slice(width + start, width + start + LANES)
            apart = heads_apart(queries[at, columns])
            keys = keys_values[reach, columns]
            shares = shares_of(apart, keys, inside)
            grad_apart = heads_apart(grad_context[at, columns])
            grad_shares = dot(grad_apart, keys_values[reach, beside], (1, 1))
            lost = jnp.sum(grad_shares * shares, axis=-1, keepdims=True)
            grad_scores = (shares * (grad_shares - lost)).astype(BF16)
            grad_here = heads_joined(dot(grad_scores, keys)) * scale
            grad_queries[at, columns] = turned_by(grad_here, cosine[at], -sine[at]).astype(BF16)
            grad_all[reach, columns] += dot(grad_scores, apart, (0, 0)) * scale
            grad_all[reach, beside] += dot(shares.astype(BF16), grad_apart, (0, 0))
    to_before[...] = grad_all[:HALF].astype(BF16)
    grad_own[...] = grad_all[HALF : HALF + rows]
    to_after[...] = grad_all[HALF + rows :].astype(BF16)


def last_kernel(
    grad_queries, grad_own, from_before, from_after, cosine, sine, matrix, tokens, gain_two,
    grad_qkv, grad_one, gain_columns, grad_all,
):
    rows, width = grad_queries.shape
    grad_all[...] = grad_own[...]
    grad_all[:HALF] += from_before[...].astype(F32)
    grad_all[rows - HALF :] += from_after[...].astype(F32)
    grad_qkv[:, :width] = grad_queries[...]
    grad_keys = turned_by(grad_all[:, :width], cosine[...], -sine[...])
    grad_qkv[:, width : 2 * width] = grad_keys.astype(BF16)
    grad_qkv[:, 2 * width :] = grad_all[:, width:].astype(BF16)
    grad = dot(grad_qkv[...], matrix[:, : 3 * width], (1, 1))
    grad_one[...] = grad.astype(BF16)
    unit, _ = unit_of(tokens[...].astype(F32))
    gain_one = jnp.sum(grad * unit, axis=0, keepdims=True)
    gain = jnp.concatenate([gain_one, gain_two[0:1, :]], axis=0)
    high = gain.astype(BF16).astype(F32)
    spare = jnp.zeros((LANES - 4, gain.shape[1]), F32)
    gain_columns[...] = jnp.concatenate([high, gain - high, spare], axis=0).T.astype(BF16)


def weight_kernel(chips, core, left_one, left_two, right_one, right_two, *refs):
    kept, away = refs[-2:]
    lower = core[0] == 0
    depth = kept.shape[1]

    def put(block, start, stop):
        kept[0, :, start:stop] = jnp.where(lower, block[:depth], block[depth:]).astype(BF16)
        away[0, :, start:stop] = jnp.where(lower, block[depth:], block[:depth]).astype(BF16)

    base = 0
    for left, right in ((left_one, right_one), (left_two, right_two)):
        width = right.shape[1]
        turned = left[...].T
        for start in range(0, width, 512):
            stop = min(width, start + 512)
            product = jnp.dot(turned, right[:, start:stop], preferred_element_type=F32)
            put(product, base + start, base + stop)
        base += width
    if len(refs) == 3:
        put(refs[0][...].astype(F32), base, base + refs[0].shape[1])


def weight_terms(ring, left_one, right_one, left_two, right_two, extra=None):
    work_rows, width = left_one.shape
    lanes = width // ring.chips
    depth = lanes // 2
    total = right_one.shape[1] + right_two.shape[1]
    more_args, more_specs = [], []
    if extra is not None:
        total += extra.shape[1]
        more_args.append(extra)
        more_specs.append(
            pl.BlockSpec((lanes, extra.shape[1]), lambda i, chips, core: (chips[i], 0))
        )

    def left_map(i, chips, core):
        return (0, chips[i])

    def whole_map(i, chips, core):
        return (0, 0)

    return pl.pallas_call(
        weight_kernel,
        grid_spec=pltpu.PrefetchScalarGridSpec(
            num_scalar_prefetch=2,
            grid=(ring.chips,),
            in_specs=[
                pl.BlockSpec((work_rows, lanes), left_map),
                pl.BlockSpec((work_rows, lanes), left_map),
                pl.BlockSpec(right_one.shape, whole_map),
                pl.BlockSpec(right_two.shape, whole_map),
                *more_specs,
            ],
            out_specs=[
                pl.BlockSpec((1, depth, total), lambda i, chips, core: (i, 0, 0)),
                pl.BlockSpec((1, depth, total), lambda i, chips, core: (i, 0, 0)),
            ],
        ),
        out_shape=[
            jax.ShapeDtypeStruct((ring.chips, depth, total), BF16),
            jax.ShapeDtypeStruct((ring.chips, depth, total), BF16),
        ],
        compiler_params=pltpu.CompilerParams(vmem_limit_bytes=40 * 1024 * 1024),
        cost_estimate=pl.CostEstimate(
            flops=2 * work_rows * width * total,
            bytes_accessed=2 * (width + work_rows) * total,
            transcendentals=0,
        ),
    )(
        ring.chips_at(ring.slots),
        ring.core.reshape(1),
        left_one,
        left_two,
        right_one,
        right_two,
        *more_args,
    )


def summed_terms(ring, name, *factors):
    if ring.short:
        return (yield from ring.scatter_sum(*weight_terms(ring, *factors), name))
    left_one, right_one, left_two, right_two, *extra = factors
    terms = [dot(left_one, right_one, (0, 0)), dot(left_two, right_two, (0, 0))]
    terms = jnp.concatenate([t.astype(BF16) for t in terms] + extra, axis=1)
    return lax.psum_scatter(terms, SEQ, scatter_dimension=0, tiled=True).astype(F32)


def norm_back(grad_rows, gain, unit_rows, inverse):
    scaled = grad_rows * gain
    centered_grad = (
        scaled
        - jnp.mean(scaled, axis=-1, keepdims=True)
        - unit_rows * jnp.mean(scaled * unit_rows, axis=-1, keepdims=True)
    )
    return inverse * centered_grad


def rotary_tables(positions):
    half_size = HD // 2
    frequency = THETA ** (-(jnp.arange(half_size, dtype=F32) * 2.0) / HD)
    angles = positions.astype(F32)[:, None] * frequency[None, :]
    cosine, sine = jnp.cos(angles), jnp.sin(angles)
    copies = LANES // HD
    return jnp.tile(cosine, (1, 2 * copies)), jnp.tile(
        jnp.concatenate([-sine, sine], axis=1), (1, copies)
    )


def pair_rows(mine):
    other = pair_swap(mine)
    first = lax.axis_index(PAIR) == 0
    return jnp.concatenate([jnp.where(first, mine, other), jnp.where(first, other, mine)], axis=0)


def own_rows(values, row_count):
    return lax.dynamic_slice_in_dim(values, lax.axis_index(PAIR) * row_count, row_count, 0)


def other_rows(values, row_count):
    return lax.dynamic_slice_in_dim(values, (1 - lax.axis_index(PAIR)) * row_count, row_count, 0)


def dot(a, b, over=(1, 0)):
    return lax.dot_general(a, b, (((over[0],), (over[1],)), ((), ())), preferred_element_type=F32)


def padded_to_lanes(values):
    return jnp.pad(values, ((0, 0), (0, -values.shape[1] % LANES)))


def local(tokens, norm1_gain, w_qkv, w_attn_out, norm2_gain, w_in, w_down, cotangent):
    row_count, model_width = tokens.shape
    ring = Ring(model_width)
    depth, _, width = w_qkv.shape
    units = w_down.shape[0]
    gains = padded_to_lanes(jnp.stack([norm1_gain, norm2_gain], axis=1))
    blob_a = jnp.concatenate([w_qkv.reshape(depth, -1), w_attn_out.T, gains], axis=1)
    blob_b = jnp.concatenate(
        [padded_to_lanes(w_in[:, 0]), padded_to_lanes(w_in[:, 1]), padded_to_lanes(w_down.T)], axis=1
    )
    units_pad = blob_b.shape[1] // 3
    steps_a = Stepped(ring.gather(blob_a, "gather_a"))
    steps_a.step()
    blob_b = steps_a.ride(blob_b)
    pieces, starts = steps_a.finish()
    steps_b = Stepped(ring.gather(blob_b, "gather_b"))

    work_rows = row_count * lax.axis_size(PAIR)
    tokens_all = pair_rows(tokens)
    cot_all = pair_rows(cotangent)
    seq = jnp.stack([lax.axis_index(SEQ), lax.axis_size(SEQ)]).astype(jnp.int32)
    cosine, sine = rotary_tables(seq[0] * work_rows + jnp.arange(work_rows, dtype=jnp.int32))

    count = len(pieces)
    tokens_all = steps_b.ride(tokens_all)
    whole_a, attn_matrix, gains, work_one, queries, kv_own, kv_first, kv_last = call(
        functools.partial(first_kernel, count, width),
        (starts, tokens_all, cosine, sine, *pieces),
        [SMEM] + [VMEM] * 3 + [ANY] * count,
        [
            shape_of(model_width, blob_a.shape[1], BF16),
            shape_of(model_width, width, BF16),
            shape_of(8, model_width, F32),
            shape_of(work_rows, model_width, BF16),
            shape_of(work_rows, width, BF16),
            shape_of(work_rows, 2 * width, BF16),
            shape_of(HALF, 2 * width, BF16),
            shape_of(HALF, 2 * width, BF16),
        ],
        [pltpu.SemaphoreType.DMA((count,))],
        flops=6 * work_rows * model_width * width,
        moved=16 * MIB,
    )
    from_before = passed_along(kv_last, SEQ, 1)
    from_after = passed_along(kv_first, SEQ, -1)
    reach_rows = work_rows + 2 * HALF
    queries = steps_b.ride(queries)
    context, attn_term = call(
        attend_kernel,
        (seq, queries, kv_own, from_before, from_after, attn_matrix),
        [SMEM] + [VMEM] * 5,
        [shape_of(work_rows, width, BF16), shape_of(work_rows, model_width, BF16)],
        [pltpu.VMEM((reach_rows, 2 * width), BF16)],
        flops=2 * work_rows * model_width * width,
        moved=16 * MIB,
    )
    attn_other = steps_b.ride(pair_swap(attn_term))

    pieces, starts = steps_b.finish()
    count = len(pieces)
    residual, work_two, hidden, grad_proj, grad_two, down_term = call(
        functools.partial(hidden_kernel, count),
        (starts, tokens_all, attn_term, attn_other, gains, cot_all, *pieces),
        [SMEM] + [VMEM] * 5 + [ANY] * count,
        [
            shape_of(work_rows, model_width, F32),
            shape_of(work_rows, model_width, BF16),
            shape_of(work_rows, units_pad, BF16),
            shape_of(work_rows, 2 * units_pad, BF16),
            shape_of(work_rows, model_width, BF16),
            shape_of(work_rows, model_width, BF16),
        ],
        [
            pltpu.VMEM((model_width, blob_b.shape[1]), BF16),
            pltpu.SemaphoreType.DMA((count,)),
        ],
        flops=12 * work_rows * model_width * units_pad,
        moved=32 * MIB,
    )
    grad_two_other = pair_swap(grad_two)
    steps_b = Stepped(summed_terms(ring, "sum_b", work_two, grad_proj, cot_all, hidden))
    steps_b.step()
    grad_two = steps_b.ride(grad_two)
    grad_residual, grad_low, gain_two, grad_queries, grad_own, to_before, to_after = call(
        attend_back_kernel,
        (
            seq, residual, gains, grad_two, grad_two_other, cot_all, attn_matrix,
            queries, kv_own, from_before, from_after, cosine, sine,
        ),
        [SMEM] + [VMEM] * 12,
        [
            shape_of(work_rows, model_width, F32),
            shape_of(work_rows, model_width, BF16),
            shape_of(8, model_width, F32),
            shape_of(work_rows, width, BF16),
            shape_of(work_rows, 2 * width, F32),
            shape_of(HALF, 2 * width, BF16),
            shape_of(HALF, 2 * width, BF16),
        ],
        [
            pltpu.VMEM((reach_rows, 2 * width), BF16),
            pltpu.VMEM((reach_rows, 2 * width), F32),
        ],
        flops=4 * work_rows * model_width * width,
        moved=24 * MIB,
    )
    from_next = passed_along(to_before, SEQ, -1)
    from_prev = passed_along(to_after, SEQ, 1)

    down_other = pair_swap(other_rows(down_term, row_count))
    output = (
        own_rows(residual, row_count)
        + (own_rows(down_term, row_count).astype(F32) + down_other.astype(F32))
    ).astype(BF16)

    grad_queries = steps_b.ride(grad_queries)
    grad_qkv, grad_one, gain_columns = call(
        last_kernel,
        (
            grad_queries, grad_own, from_prev, from_next, cosine, sine, whole_a, tokens_all,
            gain_two,
        ),
        [VMEM] * 9,
        [
            shape_of(work_rows, 3 * width, BF16),
            shape_of(work_rows, model_width, BF16),
            shape_of(model_width, LANES, BF16),
        ],
        [pltpu.VMEM((work_rows, 2 * width), F32)],
        flops=6 * work_rows * model_width * width,
        moved=16 * MIB,
    )
    one_other = pair_swap(other_rows(grad_one, row_count))
    steps_a = Stepped(summed_terms(ring, "sum_a", work_one, grad_qkv, grad_low, context, gain_columns))
    steps_a.beside(steps_b)
    steps_a.step()
    steps_a.beside(steps_b)
    share_b = steps_b.finish()
    share_a = steps_a.finish()

    gain_one = gains[0:1]
    unit_one, inverse_one = unit_of(tokens.astype(F32))
    grad_low_one = own_rows(grad_one, row_count).astype(F32) + one_other.astype(F32)
    grad_tokens = (
        own_rows(grad_residual, row_count)
        + norm_back(grad_low_one, gain_one, unit_one, inverse_one)
    ).astype(BF16)

    share_gains = share_a[:, 4 * width : 4 * width + 2] + share_a[:, 4 * width + 2 : 4 * width + 4]
    share_gain_one = share_gains[:, 0]
    share_gain_one = share_gain_one + pair_swap(share_gain_one)
    return (
        output,
        grad_tokens,
        share_gain_one,
        share_a[:, : 3 * width].reshape(depth, 3, width),
        share_a[:, 3 * width : 4 * width].T,
        share_gains[:, 1],
        jnp.stack([share_b[:, :units], share_b[:, units_pad : units_pad + units]], axis=1),
        share_b[:, 2 * units_pad : 2 * units_pad + units].T,
    )


def solution(mesh):
    return jax.shard_map(
        local,
        mesh=mesh,
        in_specs=(
            P((SEQ, PAIR), None),
            P(SEQ),
            P(SEQ, None, PAIR),
            P(PAIR, SEQ),
            P(SEQ),
            P(SEQ, None, PAIR),
            P(PAIR, SEQ),
            P((SEQ, PAIR), None),
        ),
        out_specs=(
            P((SEQ, PAIR), None),
            P((SEQ, PAIR), None),
            P(SEQ),
            P(SEQ, None, PAIR),
            P(PAIR, SEQ),
            P(SEQ),
            P(SEQ, None, PAIR),
            P(PAIR, SEQ),
        ),
        check_vma=False,
    )
```

```python
import functools
import math

import jax
import jax.numpy as jnp
import numpy as np
from jax import lax
from jax.experimental import pallas as pl
from jax.experimental.pallas import tpu as pltpu
from jax.sharding import PartitionSpec as P

HD = 64
HALF = 64
LANES = 128
COST = 1

EPSILON = 1e-05
THETA = 10000.0
SEQ = "seq"
PAIR = "fsdp"
F32 = jnp.float32
BF16 = jnp.bfloat16


def passed_along(block, axis, distance):
    devices = range(lax.axis_size(axis))
    route = [(i - distance, i) for i in devices if i - distance in devices]
    return lax.ppermute(block, axis, route)


def pair_swap(block):
    return lax.ppermute(block, PAIR, [(0, 1), (1, 0)])


class Ring:
    def __init__(self, width):
        size = lax.axis_size(SEQ)
        self.chips = size // 2
        rows = self.chips // 2
        order = [2 * z for z in range(rows)] + [2 * z + 1 for z in reversed(range(rows))]
        place = np.argsort(np.array(order))
        self.up, self.down = [], []
        for i in range(size):
            chip, core = divmod(i, 2)
            self.up.append((i, order[(place[chip] + 1) % self.chips] * 2 + core))
            self.down.append((i, order[(place[chip] - 1) % self.chips] * 2 + core))
        self.swap = [(i, i ^ 1) for i in range(size)]
        me = lax.axis_index(SEQ)
        self.core = me % 2
        self.place = jnp.asarray(place, jnp.int32)[me // 2]
        self.order = jnp.asarray(order, jnp.int32)
        self.half = self.chips // 2
        self.slots = [self.half]
        for step in range(1, self.half):
            self.slots += [self.half + step, self.half - step]
        self.slots.append(0)
        self.short = width == LANES * self.chips

    def chips_at(self, distances):
        steps = jnp.asarray(distances, jnp.int32)
        return self.order[(self.place + steps + self.chips) % self.chips]

    def go(self, block, route, name):
        with jax.named_scope(name):
            return lax.ppermute(block, SEQ, route)

    def gather(self, block, name, plan):
        if not self.short:
            whole = lax.all_gather(block, SEQ, axis=0, tiled=True)
            return [whole], jnp.zeros(1, jnp.int32)
        rows = block.shape[0]
        middle = rows // 2
        upward = downward = block
        held = {0: (block, 0)}
        swapped = {}
        for step in range(1, self.half + 1):
            if step == self.half:
                upward, downward = upward[:middle], downward[middle:]
            upward = self.go(upward, self.up, f"{name}_up_{step}")
            downward = self.go(downward, self.down, f"{name}_down_{step}")
            meanwhile = [d for d in plan[step - 1] if d in held]
            came = [self.go(held[d][0], self.swap, f"{name}_cores_{d}") for d in meanwhile]
            upward, downward, *came = yield upward, downward, *came
            swapped.update(zip(meanwhile, came))
            held[-step] = upward, 0
            held[step] = downward, middle if step == self.half else 0
        for d in held:
            if d not in swapped:
                swapped[d] = self.go(held[d][0], self.swap, f"{name}_cores_{d}")
        pieces = [held[d][0] for d in held] + [swapped[d] for d in held]
        places = [(d, 0, held[d][1]) for d in held] + [(d, 1, held[d][1]) for d in held]
        distances, others, offsets = np.array(places, np.int32).T
        cores = self.chips_at(distances) * 2 + jnp.where(others == 1, 1 - self.core, self.core)
        return pieces, cores * rows + offsets

    def scatter_sum(self, early, rest, name):
        kept_early, away_early = early
        kept_rest, away_rest = rest
        count, rows = kept_early.shape[:2]
        middle = rows // 2
        kept_early, kept_rest = yield kept_early, kept_rest
        away_early, away_rest = yield away_early, away_rest
        came_early = self.go(away_early, self.swap, f"{name}_cores_early")
        came_rest = self.go(away_rest, self.swap, f"{name}_cores_rest")

        def at(slot):
            i = self.slots.index(slot)
            if i < count:
                return kept_early[i].astype(F32) + came_early[i].astype(F32)
            return kept_rest[i - count].astype(F32) + came_rest[i - count].astype(F32)

        far = at(self.half).astype(BF16)
        upward, downward = far[:middle], far[middle:]
        for step in range(1, self.half + 1):
            upward, downward = yield upward, downward
            upward = self.go(upward, self.up, f"{name}_up_{step}").astype(F32)
            downward = self.go(downward, self.down, f"{name}_down_{step}").astype(F32)
            if step == 1:
                upward = jnp.pad(upward, ((0, rows - middle), (0, 0)))
                downward = jnp.pad(downward, ((middle, 0), (0, 0)))
            if step < self.half:
                upward = (at(self.half - step) + upward).astype(BF16)
                downward = (at(self.half + step) + downward).astype(BF16)
        return at(0) + upward + downward


class Stepped:
    def __init__(self, steps):
        self.steps, self.state, self.result = steps, None, None
        self.advance()

    def advance(self):
        try:
            if self.state is not None:
                self.state = lax.optimization_barrier(self.state)
            self.state = self.steps.send(self.state)
        except StopIteration as end:
            self.steps, self.state, self.result = None, None, end.value

    def ride(self, value):
        if self.steps is not None:
            value, self.state = lax.optimization_barrier((value, self.state))
            self.advance()
        return value

    def hold(self, value):
        if self.steps is not None:
            value, self.state = lax.optimization_barrier((value, self.state))
        return value

    def step(self):
        if self.steps is not None:
            self.advance()

    def beside(self, other):
        if self.steps is not None and other.steps is not None:
            self.state, other.state = lax.optimization_barrier((self.state, other.state))
            self.advance()
            other.advance()

    def finish(self):
        while self.steps is not None:
            self.advance()
        return self.result


VMEM = pl.BlockSpec(memory_space=pltpu.VMEM)
ANY = pl.BlockSpec(memory_space=pltpu.HBM)
SMEM = pl.BlockSpec(memory_space=pltpu.SMEM)
MIB = 1024 * 1024


def shape_of(rows, columns, kind):
    return jax.ShapeDtypeStruct((rows, columns), kind)


def call(kernel, args, specs, outs, scratch=(), flops=0, moved=0, room=20):
    return pl.pallas_call(
        kernel,
        in_specs=specs,
        out_specs=[VMEM] * len(outs),
        out_shape=outs,
        scratch_shapes=list(scratch),
        compiler_params=pltpu.CompilerParams(vmem_limit_bytes=room * MIB),
        cost_estimate=pl.CostEstimate(
            flops=flops // COST, bytes_accessed=moved // COST, transcendentals=0
        ),
    )(*args)


def placing(starts, pieces, whole, ready):
    copies = []
    for i, piece in enumerate(pieces):
        rows = piece.shape[0]
        start = pl.multiple_of(starts[i], rows)
        copies.append(
            pltpu.make_async_copy(piece, whole.at[pl.ds(start, rows), :], ready.at[i])
        )
    return copies


def lane_of(rows, width):
    return lax.broadcasted_iota(jnp.int32, (rows, width), 1)


def halves_swapped(values):
    width = values.shape[1]
    lane = lane_of(*values.shape)
    ahead = pltpu.roll(values, width - HD // 2, 1)
    behind = pltpu.roll(values, HD // 2, 1)
    return jnp.where(lane % HD < HD // 2, ahead, behind)


def turned_by(values, cosine, sine):
    copies = values.shape[1] // LANES
    cosine = jnp.concatenate([cosine] * copies, axis=1)
    sine = jnp.concatenate([sine] * copies, axis=1)
    return values * cosine + halves_swapped(values) * sine


def unit_of(values):
    average = jnp.mean(values, axis=-1, keepdims=True)
    centered = values - average
    inverse = lax.rsqrt(jnp.mean(centered * centered, axis=-1, keepdims=True) + EPSILON)
    return centered * inverse, inverse


def first_kernel(count, width, starts, tokens, before, after, cosine, sine, *refs):
    pieces = refs[:count]
    whole, matrix, gains, work, queries, keys_values, all_rows, ready = refs[count:]
    copies = placing(starts, pieces, whole, ready)
    for copy in copies:
        copy.start()
    joined_rows(before, tokens, after, all_rows)
    unit, _ = unit_of(all_rows[...].astype(F32))
    for copy in copies:
        copy.wait()
    matrix[...] = whole[:, 3 * width : 4 * width]
    gains[...] = whole[:, 4 * width :].astype(F32).T[:8]
    all_rows[...] = (unit * gains[0:1, :]).astype(BF16)
    rows = work.shape[0]
    own = slice(HALF, HALF + rows)
    work[...] = all_rows[own, :]
    for start in range(0, 3 * width, 256):
        columns = whole[:, start : start + 256]
        if start < width:
            part = dot(work[...], columns)
            queries[:, start : start + 256] = turned_by(part, cosine[own], sine[own]).astype(BF16)
        else:
            part = dot(all_rows[...], columns)
            if start < 2 * width:
                part = turned_by(part, cosine[...], sine[...])
            keys_values[:, start - width : start - width + 256] = part.astype(BF16)


def window(seq, tile, tiles):
    row = lax.broadcasted_iota(jnp.int32, (2 * LANES, 2 * LANES), 0) % LANES
    column = lax.broadcasted_iota(jnp.int32, (2 * LANES, 2 * LANES), 1)
    ahead = column - row
    inside = (ahead >= 0) & (ahead <= 2 * HALF)
    if tile == 0:
        inside &= (seq[0] > 0) | (column >= HALF)
    if tile == tiles - 1:
        inside &= (seq[0] < seq[1] - 1) | (column < 2 * LANES - HALF)
    return inside


def heads_apart(pair):
    lane = lane_of(*pair.shape)
    zero = jnp.zeros_like(pair)
    return jnp.concatenate(
        [jnp.where(lane < HD, pair, zero), jnp.where(lane < HD, zero, pair)], axis=0
    )


def heads_joined(apart):
    rows = apart.shape[0] // 2
    return jnp.where(lane_of(rows, apart.shape[1]) < HD, apart[:rows], apart[rows:])


def shares_of(apart, keys, inside):
    scores = dot(apart, keys, (1, 1)) * (1.0 / math.sqrt(HD))
    scores = jnp.where(inside, scores, -1e30)
    expo = jnp.exp(scores - jnp.max(scores, axis=-1, keepdims=True))
    return expo / jnp.sum(expo, axis=-1, keepdims=True)


def joined_rows(before, own, after, whole):
    rows = own.shape[0]
    whole[:HALF] = before[...]
    whole[HALF : HALF + rows] = own[...]
    whole[HALF + rows :] = after[...]


def attend_kernel(seq, queries, keys_values, matrix, context, term):
    rows, width = queries.shape
    tiles = rows // LANES
    for tile in range(tiles):
        inside = window(seq, tile, tiles)
        at = slice(tile * LANES, tile * LANES + LANES)
        reach = slice(tile * LANES, tile * LANES + 2 * LANES)
        for start in range(0, width, LANES):
            columns = slice(start, start + LANES)
            apart = heads_apart(queries[at, columns])
            shares = shares_of(apart, keys_values[reach, columns], inside)
            values = keys_values[reach, width + start : width + start + LANES]
            context[at, columns] = heads_joined(dot(shares.astype(BF16), values)).astype(BF16)
    term[...] = dot(context[...], matrix[...], (1, 1)).astype(BF16)


def hidden_kernel(count, spare, starts, tokens, term, term_other, gains, cot, *refs):
    pieces = refs[:count]
    residual, work, hidden, grad_proj, grad_two, down, whole, ready = refs[count:]
    copies = placing(starts, pieces, whole, ready)
    for copy in copies:
        copy.start()
    added = term[...].astype(F32) + term_other[...].astype(F32)
    residual[...] = tokens[...].astype(F32) + added
    unit, _ = unit_of(residual[...])
    work[...] = (unit * gains[1:2, :]).astype(BF16)
    for copy in copies:
        copy.wait()
    units = hidden.shape[1] - LANES

    def grads(gate, up, back):
        share = 0.5 + 0.5 * lax.erf(gate * (1.0 / math.sqrt(2.0)))
        bell = jnp.exp(-0.5 * gate * gate) * (1.0 / math.sqrt(2.0 * math.pi))
        gelu = gate * share
        return gelu * up, back * up * (share + gate * bell), back * gelu

    for start in range(0, units, 256):
        stop = min(units, start + 256)
        gate = dot(work[...], whole[:, start:stop])
        up = dot(work[...], whole[:, units + start : units + stop])
        back = dot(cot[...], whole[:, 2 * units + start : 2 * units + stop])
        here, grad_gate, grad_up = grads(gate, up, back)
        hidden[:, start:stop] = here.astype(BF16)
        grad_proj[:, start:stop] = grad_gate.astype(BF16)
        grad_proj[:, units + start : units + stop] = grad_up.astype(BF16)
    tail = whole[:, 3 * units :]
    both = dot(work[...], tail)
    back = pltpu.roll(dot(cot[...], tail), LANES - 2 * spare, 1)
    parts = grads(both, pltpu.roll(both, LANES - spare, 1), back)
    lane = lane_of(*both.shape)
    here, grad_gate, grad_up = [jnp.where(lane < spare, part, 0.0) for part in parts]
    hidden[:, units:] = pltpu.roll(here, 2 * spare, 1).astype(BF16)
    grad_proj[:, 2 * units :] = (grad_gate + pltpu.roll(grad_up, spare, 1)).astype(BF16)
    grad_two[...] = (
        dot(grad_proj[:, : 2 * units], whole[:, : 2 * units], (1, 1))
        + dot(grad_proj[:, 2 * units :], tail, (1, 1))
    ).astype(BF16)
    down[...] = dot(hidden[...], whole[:, 2 * units :], (1, 1)).astype(BF16)


def attend_back_kernel(
    seq, residual, gains, grad_two, grad_two_other, cot, matrix, queries, keys_values,
    cosine, sine, grad_residual, grad_low, gain_two, grad_queries, grad_own, to_before, to_after,
    grad_all,
):
    rows, width = queries.shape
    unit, inverse = unit_of(residual[...])
    grad = grad_two[...].astype(F32) + grad_two_other[...].astype(F32)
    gain_two[...] = jnp.broadcast_to(jnp.sum(grad * unit, axis=0, keepdims=True), gain_two.shape)
    scaled = grad * gains[1:2, :]
    middle = jnp.mean(scaled, axis=-1, keepdims=True)
    along = jnp.mean(scaled * unit, axis=-1, keepdims=True)
    total = cot[...].astype(F32) + inverse * (scaled - middle - unit * along)
    grad_residual[...] = total
    grad_low[...] = total.astype(BF16)
    grad_context = dot(grad_low[...], matrix[...]).astype(BF16)
    grad_all[...] = jnp.zeros_like(grad_all)
    scale = 1.0 / math.sqrt(HD)
    tiles = rows // LANES
    for tile in range(tiles):
        inside = window(seq, tile, tiles)
        at = slice(tile * LANES, tile * LANES + LANES)
        own_at = slice(HALF + tile * LANES, HALF + tile * LANES + LANES)
        reach = slice(tile * LANES, tile * LANES + 2 * LANES)
        for start in range(0, width, LANES):
            columns = slice(start, start + LANES)
            beside = slice(width + start, width + start + LANES)
            apart = heads_apart(queries[at, columns])
            keys = keys_values[reach, columns]
            shares = shares_of(apart, keys, inside)
            grad_apart = heads_apart(grad_context[at, columns])
            grad_shares = dot(grad_apart, keys_values[reach, beside], (1, 1))
            lost = jnp.sum(grad_shares * shares, axis=-1, keepdims=True)
            grad_scores = (shares * (grad_shares - lost)).astype(BF16)
            grad_here = heads_joined(dot(grad_scores, keys)) * scale
            grad_queries[at, columns] = turned_by(grad_here, cosine[own_at], -sine[own_at]).astype(BF16)
            grad_all[reach, columns] += dot(grad_scores, apart, (0, 0)) * scale
            grad_all[reach, beside] += dot(shares.astype(BF16), grad_apart, (0, 0))
    to_before[...] = grad_all[:HALF].astype(BF16)
    grad_own[...] = grad_all[HALF : HALF + rows]
    to_after[...] = grad_all[HALF + rows :].astype(BF16)


def last_kernel(
    grad_queries, grad_own, from_before, from_after, cosine, sine, matrix, tokens, gain_two,
    grad_qkv, grad_one, gain_columns, grad_all,
):
    rows, width = grad_queries.shape
    grad_all[...] = grad_own[...]
    grad_all[:HALF] += from_before[...].astype(F32)
    grad_all[rows - HALF :] += from_after[...].astype(F32)
    grad_qkv[:, :width] = grad_queries[...]
    own = slice(HALF, HALF + rows)
    grad_keys = turned_by(grad_all[:, :width], cosine[own], -sine[own])
    grad_qkv[:, width : 2 * width] = grad_keys.astype(BF16)
    grad_qkv[:, 2 * width :] = grad_all[:, width:].astype(BF16)
    grad = dot(grad_qkv[...], matrix[:, : 3 * width], (1, 1))
    grad_one[...] = grad.astype(BF16)
    unit, _ = unit_of(tokens[...].astype(F32))
    gain_one = jnp.sum(grad * unit, axis=0, keepdims=True)
    gain = jnp.concatenate([gain_one, gain_two[0:1, :]], axis=0)
    high = gain.astype(BF16).astype(F32)
    spare = jnp.zeros((LANES - 4, gain.shape[1]), F32)
    gain_columns[...] = jnp.concatenate([high, gain - high, spare], axis=0).T.astype(BF16)


def weight_kernel(tail, chips, core, left_one, left_two, right_one, right_two, *refs):
    kept, away = refs[-2:]
    lower = core[0] == 0
    depth = kept.shape[1]

    def put(block, start, stop):
        kept[0, :, start:stop] = jnp.where(lower, block[:depth], block[depth:]).astype(BF16)
        away[0, :, start:stop] = jnp.where(lower, block[depth:], block[:depth]).astype(BF16)

    base = 0
    rest = 0.0
    for left, right in ((left_one, right_one), (left_two, right_two)):
        width = right.shape[1] - tail
        turned = left[...].T
        for start in range(0, width, 512):
            stop = min(width, start + 512)
            product = jnp.dot(turned, right[:, start:stop], preferred_element_type=F32)
            put(product, base + start, base + stop)
        base += width
        if tail:
            rest += jnp.dot(turned, right[:, width:], preferred_element_type=F32)
    if tail:
        put(rest, base, base + tail)
    if len(refs) == 3:
        put(refs[0][...].astype(F32), base, base + refs[0].shape[1])


def weight_terms(ring, slots, left_one, right_one, left_two, right_two, extra=None, tail=0, room=20):
    work_rows, width = left_one.shape
    lanes = width // ring.chips
    depth = lanes // 2
    total = right_one.shape[1] + right_two.shape[1] - tail
    more_args, more_specs = [], []
    if extra is not None:
        total += extra.shape[1]
        more_args.append(extra)
        more_specs.append(
            pl.BlockSpec((lanes, extra.shape[1]), lambda i, chips, core: (chips[i], 0))
        )

    def left_map(i, chips, core):
        return (0, chips[i])

    def whole_map(i, chips, core):
        return (0, 0)

    return pl.pallas_call(
        functools.partial(weight_kernel, tail),
        grid_spec=pltpu.PrefetchScalarGridSpec(
            num_scalar_prefetch=2,
            grid=(len(slots),),
            in_specs=[
                pl.BlockSpec((work_rows, lanes), left_map),
                pl.BlockSpec((work_rows, lanes), left_map),
                pl.BlockSpec(right_one.shape, whole_map),
                pl.BlockSpec(right_two.shape, whole_map),
                *more_specs,
            ],
            out_specs=[
                pl.BlockSpec((1, depth, total), lambda i, chips, core: (i, 0, 0)),
                pl.BlockSpec((1, depth, total), lambda i, chips, core: (i, 0, 0)),
            ],
        ),
        out_shape=[
            pltpu.HBM((len(slots), depth, total), BF16),
            pltpu.HBM((len(slots), depth, total), BF16),
        ],
        compiler_params=pltpu.CompilerParams(vmem_limit_bytes=room * MIB),
        cost_estimate=pl.CostEstimate(
            flops=2 * work_rows * lanes * len(slots) * total // COST,
            bytes_accessed=2 * (lanes * len(slots) + work_rows) * total // COST,
            transcendentals=0,
        ),
    )(
        ring.chips_at(slots),
        ring.core.reshape(1),
        left_one,
        left_two,
        right_one,
        right_two,
        *more_args,
    )


def summed_terms(ring, name, *factors, tail=0, room=20):
    if ring.short:
        early, rest = [
            weight_terms(ring, slots, *factors, tail=tail, room=room)
            for slots in (ring.slots[:3], ring.slots[3:])
        ]
        return (yield from ring.scatter_sum(early, rest, name))
    left_one, right_one, left_two, right_two, *extra = factors
    terms = [dot(left_one, right_one, (0, 0)), dot(left_two, right_two, (0, 0))]
    if tail:
        rest = terms[0][:, -tail:] + terms[1][:, -tail:]
        terms = [terms[0][:, :-tail], terms[1][:, :-tail], rest]
    terms = jnp.concatenate([t.astype(BF16) for t in terms] + extra, axis=1)
    return lax.psum_scatter(terms, SEQ, scatter_dimension=0, tiled=True).astype(F32)


def norm_back(grad_rows, gain, unit_rows, inverse):
    scaled = grad_rows * gain
    centered_grad = (
        scaled
        - jnp.mean(scaled, axis=-1, keepdims=True)
        - unit_rows * jnp.mean(scaled * unit_rows, axis=-1, keepdims=True)
    )
    return inverse * centered_grad


def rotary_tables(positions):
    half_size = HD // 2
    frequency = THETA ** (-(jnp.arange(half_size, dtype=F32) * 2.0) / HD)
    angles = positions.astype(F32)[:, None] * frequency[None, :]
    cosine, sine = jnp.cos(angles), jnp.sin(angles)
    copies = LANES // HD
    return jnp.tile(cosine, (1, 2 * copies)), jnp.tile(
        jnp.concatenate([-sine, sine], axis=1), (1, copies)
    )


def edge_rows(block):
    blocks = range(lax.axis_size(SEQ))
    route = [(2 * i, 2 * i - 2) for i in blocks if i > 0]
    route += [(2 * i + 1, 2 * i + 3) for i in blocks if i + 1 in blocks]
    return lax.ppermute(block, (SEQ, PAIR), route)


def pair_rows(mine, other):
    first = lax.axis_index(PAIR) == 0
    return jnp.concatenate([jnp.where(first, mine, other), jnp.where(first, other, mine)], axis=0)


def own_rows(values, row_count):
    return lax.dynamic_slice_in_dim(values, lax.axis_index(PAIR) * row_count, row_count, 0)


def other_rows(values, row_count):
    return lax.dynamic_slice_in_dim(values, (1 - lax.axis_index(PAIR)) * row_count, row_count, 0)


def dot(a, b, over=(1, 0)):
    return lax.dot_general(a, b, (((over[0],), (over[1],)), ((), ())), preferred_element_type=F32)


def padded_to_lanes(values):
    return jnp.pad(values, ((0, 0), (0, -values.shape[1] % LANES)))


def local(tokens, norm1_gain, w_qkv, w_attn_out, norm2_gain, w_in, w_down, cotangent):
    row_count, model_width = tokens.shape
    ring = Ring(model_width)
    depth, _, width = w_qkv.shape
    units = w_down.shape[0]
    gains = padded_to_lanes(jnp.stack([norm1_gain, norm2_gain], axis=1))
    blob_a = jnp.concatenate([w_qkv.reshape(depth, -1), w_attn_out.T, gains], axis=1)
    whole_units = units // LANES * LANES
    spare = units - whole_units
    parts = [w_in[:, 0], w_in[:, 1], w_down.T]
    blob_b = jnp.concatenate(
        [part[:, :whole_units] for part in parts] + [part[:, whole_units:] for part in parts], axis=1
    )
    blob_b = jnp.pad(blob_b, ((0, 0), (0, LANES - 3 * spare)))
    steps_a = Stepped(ring.gather(blob_a, "gather_a", [[0], [-1, 1], [], []]))
    first = lax.axis_index(PAIR) == 0
    edge = edge_rows(jnp.where(first, tokens[:HALF], tokens[-HALF:]))
    edge = steps_a.hold(edge)
    joined = jnp.concatenate([tokens, edge], axis=0)
    other = pair_swap(joined)
    steps_a.step()
    other = steps_a.hold(other)
    tokens_all = pair_rows(tokens, other[:row_count])
    tokens_before = jnp.where(first, other[row_count:], edge)
    tokens_after = jnp.where(first, edge, other[row_count:])
    blob_b = steps_a.ride(blob_b)
    steps_b = Stepped(ring.gather(blob_b, "gather_b", [[], [0], [-1, 1], [-2, 2]]))
    steps_a.step()
    pieces, starts = steps_a.finish()

    work_rows = row_count * lax.axis_size(PAIR)
    reach_rows = work_rows + 2 * HALF
    seq = jnp.stack([lax.axis_index(SEQ), lax.axis_size(SEQ)]).astype(jnp.int32)
    cosine, sine = rotary_tables(
        seq[0] * work_rows - HALF + jnp.arange(reach_rows, dtype=jnp.int32)
    )

    tokens_all, cot_own = steps_b.ride((tokens_all, cotangent))
    cot_other = pair_swap(cot_own)
    count = len(pieces)
    whole_a, attn_matrix, gains, work_one, queries, keys_values = call(
        functools.partial(first_kernel, count, width),
        (starts, tokens_all, tokens_before, tokens_after, cosine, sine, *pieces),
        [SMEM] + [VMEM] * 5 + [ANY] * count,
        [
            shape_of(model_width, blob_a.shape[1], BF16),
            shape_of(model_width, width, BF16),
            shape_of(8, model_width, F32),
            shape_of(work_rows, model_width, BF16),
            shape_of(work_rows, width, BF16),
            shape_of(reach_rows, 2 * width, BF16),
        ],
        [pltpu.VMEM((reach_rows, model_width), BF16), pltpu.SemaphoreType.DMA((count,))],
        flops=6 * work_rows * model_width * width,
        moved=16 * MIB,
        room=60,
    )
    queries, cot_other = steps_b.ride((queries, cot_other))
    cot_all = pair_rows(cotangent, cot_other)
    context, attn_term = call(
        attend_kernel,
        (seq, queries, keys_values, attn_matrix),
        [SMEM] + [VMEM] * 3,
        [shape_of(work_rows, width, BF16), shape_of(work_rows, model_width, BF16)],
        flops=2 * work_rows * model_width * width,
        moved=16 * MIB,
    )
    attn_other = steps_b.ride(pair_swap(attn_term))

    pieces, starts = steps_b.finish()
    count = len(pieces)
    residual, work_two, hidden, grad_proj, grad_two, down_term = call(
        functools.partial(hidden_kernel, count, spare),
        (starts, tokens_all, attn_term, attn_other, gains, cot_all, *pieces),
        [SMEM] + [VMEM] * 5 + [ANY] * count,
        [
            shape_of(work_rows, model_width, F32),
            shape_of(work_rows, model_width, BF16),
            shape_of(work_rows, whole_units + LANES, BF16),
            shape_of(work_rows, 2 * whole_units + LANES, BF16),
            shape_of(work_rows, model_width, BF16),
            shape_of(work_rows, model_width, BF16),
        ],
        [
            pltpu.VMEM((model_width, blob_b.shape[1]), BF16),
            pltpu.SemaphoreType.DMA((count,)),
        ],
        flops=12 * work_rows * model_width * units,
        moved=32 * MIB,
        room=60,
    )
    grad_two_other = pair_swap(grad_two)
    steps_b = Stepped(summed_terms(ring, "sum_b", work_two, grad_proj, cot_all, hidden, tail=LANES, room=60))
    grad_two = steps_b.ride(grad_two)
    grad_residual, grad_low, gain_two, grad_queries, grad_own, to_before, to_after = call(
        attend_back_kernel,
        (
            seq, residual, gains, grad_two, grad_two_other, cot_all, attn_matrix,
            queries, keys_values, cosine, sine,
        ),
        [SMEM] + [VMEM] * 10,
        [
            shape_of(work_rows, model_width, F32),
            shape_of(work_rows, model_width, BF16),
            shape_of(8, model_width, F32),
            shape_of(work_rows, width, BF16),
            shape_of(work_rows, 2 * width, F32),
            shape_of(HALF, 2 * width, BF16),
            shape_of(HALF, 2 * width, BF16),
        ],
        [pltpu.VMEM((reach_rows, 2 * width), F32)],
        flops=4 * work_rows * model_width * width,
        moved=24 * MIB,
    )
    to_before, to_after = steps_b.ride((to_before, to_after))
    from_next = passed_along(to_before, SEQ, -1)
    from_prev = passed_along(to_after, SEQ, 1)

    down_other = pair_swap(other_rows(down_term, row_count))
    grad_queries = steps_b.ride(grad_queries)
    grad_qkv, grad_one, gain_columns = call(
        last_kernel,
        (
            grad_queries, grad_own, from_prev, from_next, cosine, sine, whole_a, tokens_all,
            gain_two,
        ),
        [VMEM] * 9,
        [
            shape_of(work_rows, 3 * width, BF16),
            shape_of(work_rows, model_width, BF16),
            shape_of(model_width, LANES, BF16),
        ],
        [pltpu.VMEM((work_rows, 2 * width), F32)],
        flops=6 * work_rows * model_width * width,
        moved=16 * MIB,
    )
    one_other = pair_swap(other_rows(grad_one, row_count))
    down_other = steps_b.hold(down_other)
    steps_a = Stepped(summed_terms(ring, "sum_a", work_one, grad_qkv, grad_low, context, gain_columns))
    steps_a.step()
    steps_a.beside(steps_b)
    one_other = steps_a.hold(one_other)
    steps_a.step()
    steps_a.beside(steps_b)
    steps_a.step()
    steps_a.beside(steps_b)
    share_b = steps_b.finish()
    share_a = steps_a.finish()

    output = (
        own_rows(residual, row_count)
        + (own_rows(down_term, row_count).astype(F32) + down_other.astype(F32))
    ).astype(BF16)

    gain_one = gains[0:1]
    unit_one, inverse_one = unit_of(tokens.astype(F32))
    grad_low_one = own_rows(grad_one, row_count).astype(F32) + one_other.astype(F32)
    grad_tokens = (
        own_rows(grad_residual, row_count)
        + norm_back(grad_low_one, gain_one, unit_one, inverse_one)
    ).astype(BF16)

    def share_b_part(part):
        tail = 3 * whole_units + part * spare
        main = share_b[:, part * whole_units : (part + 1) * whole_units]
        return jnp.concatenate([main, share_b[:, tail : tail + spare]], axis=1)

    share_gains = share_a[:, 4 * width : 4 * width + 2] + share_a[:, 4 * width + 2 : 4 * width + 4]
    share_gain_one = share_gains[:, 0]
    share_gain_one = share_gain_one + pair_swap(share_gain_one)
    return (
        output,
        grad_tokens,
        share_gain_one,
        share_a[:, : 3 * width].reshape(depth, 3, width),
        share_a[:, 3 * width : 4 * width].T,
        share_gains[:, 1],
        jnp.stack([share_b_part(0), share_b_part(1)], axis=1),
        share_b_part(2).T,
    )


def solution(mesh):
    return jax.shard_map(
        local,
        mesh=mesh,
        in_specs=(
            P((SEQ, PAIR), None),
            P(SEQ),
            P(SEQ, None, PAIR),
            P(PAIR, SEQ),
            P(SEQ),
            P(SEQ, None, PAIR),
            P(PAIR, SEQ),
            P((SEQ, PAIR), None),
        ),
        out_specs=(
            P((SEQ, PAIR), None),
            P((SEQ, PAIR), None),
            P(SEQ),
            P(SEQ, None, PAIR),
            P(PAIR, SEQ),
            P(SEQ),
            P(SEQ, None, PAIR),
            P(PAIR, SEQ),
        ),
        check_vma=False,
    )
```

```python
import functools
import math

import jax
import jax.numpy as jnp
import numpy as np
from jax import lax
from jax.experimental import pallas as pl
from jax.experimental.pallas import tpu as pltpu
from jax.sharding import PartitionSpec as P

HD = 64
HALF = 64
LANES = 128
COST = 1

EPSILON = 1e-05
THETA = 10000.0
SEQ = "seq"
PAIR = "fsdp"
F32 = jnp.float32
BF16 = jnp.bfloat16


def passed_along(block, axis, distance):
    devices = range(lax.axis_size(axis))
    route = [(i - distance, i) for i in devices if i - distance in devices]
    return lax.ppermute(block, axis, route)


def pair_swap(block):
    return lax.ppermute(block, PAIR, [(0, 1), (1, 0)])


class Ring:
    def __init__(self, width):
        size = lax.axis_size(SEQ)
        self.chips = size // 2
        rows = self.chips // 2
        order = [2 * z for z in range(rows)] + [2 * z + 1 for z in reversed(range(rows))]
        place = np.argsort(np.array(order))
        self.up, self.down = [], []
        for i in range(size):
            chip, core = divmod(i, 2)
            self.up.append((i, order[(place[chip] + 1) % self.chips] * 2 + core))
            self.down.append((i, order[(place[chip] - 1) % self.chips] * 2 + core))
        self.swap = [(i, i ^ 1) for i in range(size)]
        me = lax.axis_index(SEQ)
        self.core = me % 2
        self.place = jnp.asarray(place, jnp.int32)[me // 2]
        self.order = jnp.asarray(order, jnp.int32)
        self.half = self.chips // 2
        self.slots = [self.half]
        for step in range(1, self.half):
            self.slots += [self.half + step, self.half - step]
        self.slots.append(0)
        self.short = width == LANES * self.chips

    def chips_at(self, distances):
        steps = jnp.asarray(distances, jnp.int32)
        return self.order[(self.place + steps + self.chips) % self.chips]

    def go(self, block, route, name):
        with jax.named_scope(name):
            return lax.ppermute(block, SEQ, route)

    def gather(self, block, name, plan):
        if not self.short:
            whole = lax.all_gather(block, SEQ, axis=0, tiled=True)
            return [whole], jnp.zeros(1, jnp.int32)
        rows = block.shape[0]
        middle = rows // 2
        upward = downward = block
        order = [0]
        for step in range(1, self.half + 1):
            order += [-step, step]
        places = [(d, 0, middle if d == self.half else 0) for d in order]
        places += [(d, 1, offset) for d, _, offset in places]
        distances, others, offsets = np.array(places, np.int32).T
        cores = self.chips_at(distances) * 2 + jnp.where(others == 1, 1 - self.core, self.core)
        starts = cores * rows + offsets
        held = {0: (block, 0)}
        swapped = {}
        for step in range(1, self.half + 1):
            if step == self.half:
                upward, downward = upward[:middle], downward[middle:]
            upward = self.go(upward, self.up, f"{name}_up_{step}")
            downward = self.go(downward, self.down, f"{name}_down_{step}")
            meanwhile = [d for d in plan[step - 1] if d in held]
            came = [self.go(held[d][0], self.swap, f"{name}_cores_{d}") for d in meanwhile]
            upward, downward, starts, *came = yield upward, downward, starts, *came
            swapped.update(zip(meanwhile, came))
            held[-step] = upward, 0
            held[step] = downward, middle if step == self.half else 0
        for d in held:
            if d not in swapped:
                swapped[d] = self.go(held[d][0], self.swap, f"{name}_cores_{d}")
        pieces = [held[d][0] for d in held] + [swapped[d] for d in held]
        return pieces, starts

    def scatter_sum(self, early, rest, name):
        kept_early, away_early = early
        kept_rest, away_rest = rest
        count, rows = kept_early.shape[:2]
        middle = rows // 2
        came_early = self.go(away_early, self.swap, f"{name}_cores_early")
        came_rest = self.go(away_rest, self.swap, f"{name}_cores_rest")

        def at(slot):
            i = self.slots.index(slot)
            if i < count:
                return kept_early[i].astype(F32) + came_early[i].astype(F32)
            return kept_rest[i - count].astype(F32) + came_rest[i - count].astype(F32)

        far = at(self.half).astype(BF16)
        upward, downward = far[:middle], far[middle:]
        for step in range(1, self.half + 1):
            upward, downward = yield upward, downward
            upward = self.go(upward, self.up, f"{name}_up_{step}")
            downward = self.go(downward, self.down, f"{name}_down_{step}")
            upward, downward = yield upward, downward
            upward, downward = upward.astype(F32), downward.astype(F32)
            if step == 1:
                upward = jnp.pad(upward, ((0, rows - middle), (0, 0)))
                downward = jnp.pad(downward, ((middle, 0), (0, 0)))
            if step < self.half:
                upward = (at(self.half - step) + upward).astype(BF16)
                downward = (at(self.half + step) + downward).astype(BF16)
        return at(0) + upward + downward


class Stepped:
    def __init__(self, steps):
        self.steps, self.state, self.result = steps, None, None
        self.advance()

    def advance(self):
        try:
            if self.state is not None:
                self.state = lax.optimization_barrier(self.state)
            self.state = self.steps.send(self.state)
        except StopIteration as end:
            self.steps, self.state, self.result = None, None, end.value

    def ride(self, value):
        if self.steps is not None:
            value, self.state = lax.optimization_barrier((value, self.state))
            self.advance()
        return value

    def hold(self, value):
        if self.steps is not None:
            value, self.state = lax.optimization_barrier((value, self.state))
        return value

    def step(self):
        if self.steps is not None:
            self.advance()

    def beside(self, other):
        if self.steps is not None and other.steps is not None:
            self.state, other.state = lax.optimization_barrier((self.state, other.state))
            self.advance()
            other.advance()

    def finish(self):
        while self.steps is not None:
            self.advance()
        return self.result


VMEM = pl.BlockSpec(memory_space=pltpu.VMEM)
ANY = pl.BlockSpec(memory_space=pltpu.HBM)
SMEM = pl.BlockSpec(memory_space=pltpu.SMEM)
MIB = 1024 * 1024


def shape_of(rows, columns, kind):
    return jax.ShapeDtypeStruct((rows, columns), kind)


def call(kernel, args, specs, outs, scratch=(), flops=0, moved=0, room=20):
    return pl.pallas_call(
        kernel,
        in_specs=specs,
        out_specs=[VMEM] * len(outs),
        out_shape=outs,
        scratch_shapes=list(scratch),
        compiler_params=pltpu.CompilerParams(vmem_limit_bytes=room * MIB),
        cost_estimate=pl.CostEstimate(
            flops=flops // COST, bytes_accessed=moved // COST, transcendentals=0
        ),
    )(*args)


def placing(starts, pieces, whole, ready):
    copies = []
    for i, piece in enumerate(pieces):
        rows = piece.shape[0]
        start = pl.multiple_of(starts[i], rows)
        copies.append(
            pltpu.make_async_copy(piece, whole.at[pl.ds(start, rows), :], ready.at[i])
        )
    return copies


def lane_of(rows, width):
    return lax.broadcasted_iota(jnp.int32, (rows, width), 1)


def halves_swapped(values):
    width = values.shape[1]
    lane = lane_of(*values.shape)
    ahead = pltpu.roll(values, width - HD // 2, 1)
    behind = pltpu.roll(values, HD // 2, 1)
    return jnp.where(lane % HD < HD // 2, ahead, behind)


def turned_by(values, cosine, sine):
    copies = values.shape[1] // LANES
    cosine = jnp.concatenate([cosine] * copies, axis=1)
    sine = jnp.concatenate([sine] * copies, axis=1)
    return values * cosine + halves_swapped(values) * sine


def unit_of(values):
    average = jnp.mean(values, axis=-1, keepdims=True)
    centered = values - average
    inverse = lax.rsqrt(jnp.mean(centered * centered, axis=-1, keepdims=True) + EPSILON)
    return centered * inverse, inverse


def first_kernel(count, width, starts, tokens, before, after, cosine, sine, *refs):
    pieces = refs[:count]
    whole, matrix, gains, work, queries, keys_values, wide_cosine, wide_sine = refs[count:-2]
    all_rows, ready = refs[-2:]
    copies = placing(starts, pieces, whole, ready)
    for copy in copies:
        copy.start()
    joined_rows(before, tokens, after, all_rows)
    wide_cosine[...] = jnp.concatenate([cosine[...]] * 4, axis=1)
    wide_sine[...] = jnp.concatenate([-sine[...], sine[...]] * 2, axis=1)
    unit, _ = unit_of(all_rows[...].astype(F32))
    for copy in copies:
        copy.wait()
    matrix[...] = whole[:, 3 * width : 4 * width]
    gains[...] = whole[:, 4 * width :].astype(F32).T[:8]
    all_rows[...] = (unit * gains[0:1, :]).astype(BF16)
    rows = work.shape[0]
    own = slice(HALF, HALF + rows)
    work[...] = all_rows[own, :]
    for start in range(0, 3 * width, 256):
        columns = whole[:, start : start + 256]
        if start < width:
            part = dot(work[...], columns)
            queries[:, start : start + 256] = turned_by(part, wide_cosine[own], wide_sine[own]).astype(BF16)
        else:
            part = dot(all_rows[...], columns)
            if start < 2 * width:
                part = turned_by(part, wide_cosine[...], wide_sine[...])
            keys_values[:, start - width : start - width + 256] = part.astype(BF16)


def window(seq, tile, tiles):
    row = lax.broadcasted_iota(jnp.int32, (2 * LANES, 2 * LANES), 0) % LANES
    column = lax.broadcasted_iota(jnp.int32, (2 * LANES, 2 * LANES), 1)
    ahead = column - row
    inside = (ahead >= 0) & (ahead <= 2 * HALF)
    if tile == 0:
        inside &= (seq[0] > 0) | (column >= HALF)
    if tile == tiles - 1:
        inside &= (seq[0] < seq[1] - 1) | (column < 2 * LANES - HALF)
    return inside


def heads_apart(pair):
    lane = lane_of(*pair.shape)
    zero = jnp.zeros_like(pair)
    return jnp.concatenate(
        [jnp.where(lane < HD, pair, zero), jnp.where(lane < HD, zero, pair)], axis=0
    )


def heads_joined(apart):
    rows = apart.shape[0] // 2
    return jnp.where(lane_of(rows, apart.shape[1]) < HD, apart[:rows], apart[rows:])


def shares_of(apart, keys, inside):
    scores = dot(apart, keys, (1, 1)) * (1.0 / math.sqrt(HD))
    scores = jnp.where(inside, scores, -1e30)
    expo = jnp.exp(scores - jnp.max(scores, axis=-1, keepdims=True))
    return expo / jnp.sum(expo, axis=-1, keepdims=True)


def joined_rows(before, own, after, whole):
    rows = own.shape[0]
    whole[:HALF] = before[...]
    whole[HALF : HALF + rows] = own[...]
    whole[HALF + rows :] = after[...]


def attend_kernel(seq, queries, keys_values, matrix, context, term):
    rows, width = queries.shape
    tiles = rows // LANES
    for tile in range(tiles):
        inside = window(seq, tile, tiles)
        at = slice(tile * LANES, tile * LANES + LANES)
        reach = slice(tile * LANES, tile * LANES + 2 * LANES)
        for start in range(0, width, LANES):
            columns = slice(start, start + LANES)
            apart = heads_apart(queries[at, columns])
            shares = shares_of(apart, keys_values[reach, columns], inside)
            values = keys_values[reach, width + start : width + start + LANES]
            context[at, columns] = heads_joined(dot(shares.astype(BF16), values)).astype(BF16)
    term[...] = dot(context[...], matrix[...], (1, 1)).astype(BF16)


def hidden_kernel(count, spare, early, starts, chips, core, tokens, term, term_other, gains, cot, *refs):
    pieces = refs[:count]
    residual, work, hidden, grad_proj, grad_two, down, *terms, whole, ready = refs[count:]
    copies = placing(starts, pieces, whole, ready)
    for copy in copies:
        copy.start()
    added = term[...].astype(F32) + term_other[...].astype(F32)
    residual[...] = tokens[...].astype(F32) + added
    unit, _ = unit_of(residual[...])
    work[...] = (unit * gains[1:2, :]).astype(BF16)
    for copy in copies:
        copy.wait()
    units = hidden.shape[1] - LANES

    def grads(gate, up, back):
        share = 0.5 + 0.5 * lax.erf(gate * (1.0 / math.sqrt(2.0)))
        bell = jnp.exp(-0.5 * gate * gate) * (1.0 / math.sqrt(2.0 * math.pi))
        gelu = gate * share
        return gelu * up, back * up * (share + gate * bell), back * gelu

    for start in range(0, units, 256):
        stop = min(units, start + 256)
        gate = dot(work[...], whole[:, start:stop])
        up = dot(work[...], whole[:, units + start : units + stop])
        back = dot(cot[...], whole[:, 2 * units + start : 2 * units + stop])
        here, grad_gate, grad_up = grads(gate, up, back)
        hidden[:, start:stop] = here.astype(BF16)
        grad_proj[:, start:stop] = grad_gate.astype(BF16)
        grad_proj[:, units + start : units + stop] = grad_up.astype(BF16)
    tail = whole[:, 3 * units :]
    both = dot(work[...], tail)
    back = pltpu.roll(dot(cot[...], tail), LANES - 2 * spare, 1)
    parts = grads(both, pltpu.roll(both, LANES - spare, 1), back)
    lane = lane_of(*both.shape)
    here, grad_gate, grad_up = [jnp.where(lane < spare, part, 0.0) for part in parts]
    hidden[:, units:] = pltpu.roll(here, 2 * spare, 1).astype(BF16)
    grad_proj[:, 2 * units :] = (grad_gate + pltpu.roll(grad_up, spare, 1)).astype(BF16)
    grad_two[...] = (
        dot(grad_proj[:, : 2 * units], whole[:, : 2 * units], (1, 1))
        + dot(grad_proj[:, 2 * units :], tail, (1, 1))
    ).astype(BF16)
    down[...] = dot(hidden[...], whole[:, 2 * units :], (1, 1)).astype(BF16)
    if early:
        early_rows(early, chips, core, LANES, [(work, grad_proj), (cot, hidden)], None, *terms)


def attend_back_kernel(
    seq, residual, gains, grad_two, grad_two_other, cot, matrix, queries, keys_values,
    cosine, sine, grad_residual, grad_low, gain_two, grad_queries, grad_own, to_before, to_after,
    grad_all,
):
    rows, width = queries.shape
    unit, inverse = unit_of(residual[...])
    grad = grad_two[...].astype(F32) + grad_two_other[...].astype(F32)
    gain_two[...] = jnp.broadcast_to(jnp.sum(grad * unit, axis=0, keepdims=True), gain_two.shape)
    scaled = grad * gains[1:2, :]
    middle = jnp.mean(scaled, axis=-1, keepdims=True)
    along = jnp.mean(scaled * unit, axis=-1, keepdims=True)
    total = cot[...].astype(F32) + inverse * (scaled - middle - unit * along)
    grad_residual[...] = total
    grad_low[...] = total.astype(BF16)
    grad_context = dot(grad_low[...], matrix[...]).astype(BF16)
    grad_all[...] = jnp.zeros_like(grad_all)
    scale = 1.0 / math.sqrt(HD)
    tiles = rows // LANES
    for tile in range(tiles):
        inside = window(seq, tile, tiles)
        at = slice(tile * LANES, tile * LANES + LANES)
        own_at = slice(HALF + tile * LANES, HALF + tile * LANES + LANES)
        reach = slice(tile * LANES, tile * LANES + 2 * LANES)
        for start in range(0, width, LANES):
            columns = slice(start, start + LANES)
            beside = slice(width + start, width + start + LANES)
            apart = heads_apart(queries[at, columns])
            keys = keys_values[reach, columns]
            shares = shares_of(apart, keys, inside)
            grad_apart = heads_apart(grad_context[at, columns])
            grad_shares = dot(grad_apart, keys_values[reach, beside], (1, 1))
            lost = jnp.sum(grad_shares * shares, axis=-1, keepdims=True)
            grad_scores = (shares * (grad_shares - lost)).astype(BF16)
            grad_here = heads_joined(dot(grad_scores, keys)) * scale
            grad_queries[at, columns] = turned_by(grad_here, cosine[own_at], -sine[own_at]).astype(BF16)
            grad_all[reach, columns] += dot(grad_scores, apart, (0, 0)) * scale
            grad_all[reach, beside] += dot(shares.astype(BF16), grad_apart, (0, 0))
    to_before[...] = grad_all[:HALF].astype(BF16)
    grad_own[...] = grad_all[HALF : HALF + rows]
    to_after[...] = grad_all[HALF + rows :].astype(BF16)


def last_kernel(
    early, chips, core, grad_queries, grad_own, from_before, from_after, cosine, sine, tokens,
    gain_two, work, grad_low, context, matrix_whole, grad_qkv, grad_one, gain_columns, *refs,
):
    *parts, grad_all, matrix, ready = refs
    rows, width = grad_queries.shape
    fetch = pltpu.make_async_copy(matrix_whole.at[:, : 3 * width], matrix, ready)
    fetch.start()
    grad_all[...] = grad_own[...]
    grad_all[:HALF] += from_before[...].astype(F32)
    grad_all[rows - HALF :] += from_after[...].astype(F32)
    grad_qkv[:, :width] = grad_queries[...]
    own = slice(HALF, HALF + rows)
    grad_keys = turned_by(grad_all[:, :width], cosine[own], -sine[own])
    grad_qkv[:, width : 2 * width] = grad_keys.astype(BF16)
    grad_qkv[:, 2 * width :] = grad_all[:, width:].astype(BF16)
    fetch.wait()
    grad = dot(grad_qkv[...], matrix[...], (1, 1))
    grad_one[...] = grad.astype(BF16)
    unit, _ = unit_of(tokens[...].astype(F32))
    gain_one = jnp.sum(grad * unit, axis=0, keepdims=True)
    gain = jnp.concatenate([gain_one, gain_two[0:1, :]], axis=0)
    high = gain.astype(BF16).astype(F32)
    spare = jnp.zeros((LANES - 4, gain.shape[1]), F32)
    gain_columns[...] = jnp.concatenate([high, gain - high, spare], axis=0).T.astype(BF16)
    if early:
        pairs = [(work, grad_qkv), (grad_low, context)]
        early_rows(early, chips, core, 0, pairs, gain_columns, *parts)


def weight_rows(i, tail, lower, pairs, extra, kept, away):
    depth = kept.shape[1]

    def put(block, start, stop):
        kept[i, :, start:stop] = jnp.where(lower, block[:depth], block[depth:]).astype(BF16)
        away[i, :, start:stop] = jnp.where(lower, block[depth:], block[:depth]).astype(BF16)

    base = 0
    rest = 0.0
    for left, right in pairs:
        width = right.shape[1] - tail
        turned = left.T
        for start in range(0, width, 512):
            stop = min(width, start + 512)
            product = jnp.dot(turned, right[:, start:stop], preferred_element_type=F32)
            put(product, base + start, base + stop)
        base += width
        if tail:
            rest += jnp.dot(turned, right[:, width:], preferred_element_type=F32)
    if tail:
        put(rest, base, base + tail)
    if extra is not None:
        put(extra.astype(F32), base, base + extra.shape[1])


def early_rows(count, chips, core, tail, pairs, extra, kept, away):
    lower = core[0] == 0
    for i in range(count):
        lanes = pl.ds(pl.multiple_of(chips[i] * LANES, LANES), LANES)
        blocks = [(left[:, lanes], right) for left, right in pairs]
        more = None if extra is None else extra[lanes, :]
        weight_rows(i, tail, lower, blocks, more, kept, away)


def weight_kernel(tail, chips, core, left_one, left_two, right_one, right_two, *refs):
    pairs = [(left_one[...], right_one), (left_two[...], right_two)]
    extra = refs[0][...] if len(refs) == 3 else None
    weight_rows(0, tail, core[0] == 0, pairs, extra, *refs[-2:])


def weight_terms(ring, chips, core, skip, left_one, right_one, left_two, right_two, extra=None, tail=0, room=20):
    work_rows, width = left_one.shape
    lanes = width // ring.chips
    depth = lanes // 2
    total = right_one.shape[1] + right_two.shape[1] - tail
    more_args, more_specs = [], []
    if extra is not None:
        total += extra.shape[1]
        more_args.append(extra)
        more_specs.append(
            pl.BlockSpec((lanes, extra.shape[1]), lambda i, chips, core: (chips[i + skip], 0))
        )

    count = ring.chips - skip

    def left_map(i, chips, core):
        return (0, chips[i + skip])

    def whole_map(i, chips, core):
        return (0, 0)

    return pl.pallas_call(
        functools.partial(weight_kernel, tail),
        grid_spec=pltpu.PrefetchScalarGridSpec(
            num_scalar_prefetch=2,
            grid=(count,),
            in_specs=[
                pl.BlockSpec((work_rows, lanes), left_map),
                pl.BlockSpec((work_rows, lanes), left_map),
                pl.BlockSpec(right_one.shape, whole_map),
                pl.BlockSpec(right_two.shape, whole_map),
                *more_specs,
            ],
            out_specs=[
                pl.BlockSpec((1, depth, total), lambda i, chips, core: (i, 0, 0)),
                pl.BlockSpec((1, depth, total), lambda i, chips, core: (i, 0, 0)),
            ],
        ),
        out_shape=[
            pltpu.HBM((count, depth, total), BF16),
            pltpu.HBM((count, depth, total), BF16),
        ],
        compiler_params=pltpu.CompilerParams(vmem_limit_bytes=room * MIB),
        cost_estimate=pl.CostEstimate(
            flops=2 * work_rows * lanes * count * total // COST,
            bytes_accessed=2 * (lanes * count + work_rows) * total // COST,
            transcendentals=0,
        ),
    )(
        chips,
        core,
        left_one,
        left_two,
        right_one,
        right_two,
        *more_args,
    )


def summed_terms(left_one, right_one, left_two, right_two, extra=None, tail=0):
    yield from ()
    terms = [dot(left_one, right_one, (0, 0)), dot(left_two, right_two, (0, 0))]
    if tail:
        rest = terms[0][:, -tail:] + terms[1][:, -tail:]
        terms = [terms[0][:, :-tail], terms[1][:, :-tail], rest]
    terms = [t.astype(BF16) for t in terms] + ([] if extra is None else [extra])
    terms = jnp.concatenate(terms, axis=1)
    return lax.psum_scatter(terms, SEQ, scatter_dimension=0, tiled=True).astype(F32)


def norm_back(grad_rows, gain, unit_rows, inverse):
    scaled = grad_rows * gain
    centered_grad = (
        scaled
        - jnp.mean(scaled, axis=-1, keepdims=True)
        - unit_rows * jnp.mean(scaled * unit_rows, axis=-1, keepdims=True)
    )
    return inverse * centered_grad


def rotary_tables(positions):
    half_size = HD // 2
    frequency = THETA ** (-(jnp.arange(half_size, dtype=F32) * 2.0) / HD)
    angles = positions.astype(F32)[:, None] * frequency[None, :]
    return jnp.cos(angles), jnp.sin(angles)


def edge_rows(block):
    blocks = range(lax.axis_size(SEQ))
    route = [(2 * i, 2 * i - 2) for i in blocks if i > 0]
    route += [(2 * i + 1, 2 * i + 3) for i in blocks if i + 1 in blocks]
    return lax.ppermute(block, (SEQ, PAIR), route)


def pair_rows(mine, other):
    first = lax.axis_index(PAIR) == 0
    return jnp.concatenate([jnp.where(first, mine, other), jnp.where(first, other, mine)], axis=0)


def own_rows(values, row_count):
    return lax.dynamic_slice_in_dim(values, lax.axis_index(PAIR) * row_count, row_count, 0)


def other_rows(values, row_count):
    return lax.dynamic_slice_in_dim(values, (1 - lax.axis_index(PAIR)) * row_count, row_count, 0)


def dot(a, b, over=(1, 0)):
    return lax.dot_general(a, b, (((over[0],), (over[1],)), ((), ())), preferred_element_type=F32)


def padded_to_lanes(values):
    return jnp.pad(values, ((0, 0), (0, -values.shape[1] % LANES)))


def local(tokens, norm1_gain, w_qkv, w_attn_out, norm2_gain, w_in, w_down, cotangent):
    row_count, model_width = tokens.shape
    ring = Ring(model_width)
    early = 3 if ring.short else 0
    chips, core = ring.chips_at(ring.slots), ring.core.reshape(1)
    depth, _, width = w_qkv.shape
    units = w_down.shape[0]
    gains = padded_to_lanes(jnp.stack([norm1_gain, norm2_gain], axis=1))
    blob_a = jnp.concatenate([w_qkv.reshape(depth, -1), w_attn_out.T, gains], axis=1)
    whole_units = units // LANES * LANES
    spare = units - whole_units
    parts = [w_in[:, 0], w_in[:, 1], w_down.T]
    blob_b = jnp.concatenate(
        [part[:, :whole_units] for part in parts] + [part[:, whole_units:] for part in parts], axis=1
    )
    blob_b = jnp.pad(blob_b, ((0, 0), (0, LANES - 3 * spare)))
    steps_a = Stepped(ring.gather(blob_a, "gather_a", [[0], [-1, 1], [], [-2]]))
    first = lax.axis_index(PAIR) == 0
    edge = edge_rows(jnp.where(first, tokens[:HALF], tokens[-HALF:]))
    edge = steps_a.hold(edge)
    joined = jnp.concatenate([tokens, edge, cotangent], axis=0)
    other = pair_swap(joined)
    steps_a.step()
    blob_b = steps_a.ride(blob_b)
    steps_b = Stepped(ring.gather(blob_b, "gather_b", [[], [], [0, -1, 1], [-2, 2]]))
    other = steps_a.hold(other)
    tokens_all = pair_rows(tokens, other[:row_count])
    beside = other[row_count : row_count + HALF]
    tokens_before = jnp.where(first, beside, edge)
    tokens_after = jnp.where(first, edge, beside)
    cot_all = pair_rows(cotangent, other[row_count + HALF :])

    work_rows = row_count * lax.axis_size(PAIR)
    reach_rows = work_rows + 2 * HALF
    seq = jnp.stack([lax.axis_index(SEQ), lax.axis_size(SEQ)]).astype(jnp.int32)
    cosine, sine = rotary_tables(
        seq[0] * work_rows - HALF + jnp.arange(reach_rows, dtype=jnp.int32)
    )
    inputs = tokens_all, tokens_before, tokens_after, cot_all, seq, cosine, sine, chips, core
    inputs = steps_a.hold(inputs)
    tokens_all, tokens_before, tokens_after, cot_all, seq, cosine, sine, chips, core = inputs
    steps_a.beside(steps_b)
    pieces, starts = steps_a.finish()
    count = len(pieces)
    whole_a, attn_matrix, gains, work_one, queries, keys_values, cosine, sine = call(
        functools.partial(first_kernel, count, width),
        (starts, tokens_all, tokens_before, tokens_after, cosine, sine, *pieces),
        [SMEM] + [VMEM] * 5 + [ANY] * count,
        [
            shape_of(model_width, blob_a.shape[1], BF16),
            shape_of(model_width, width, BF16),
            shape_of(8, model_width, F32),
            shape_of(work_rows, model_width, BF16),
            shape_of(work_rows, width, BF16),
            shape_of(reach_rows, 2 * width, BF16),
            shape_of(reach_rows, LANES, F32),
            shape_of(reach_rows, LANES, F32),
        ],
        [pltpu.VMEM((reach_rows, model_width), BF16), pltpu.SemaphoreType.DMA((count,))],
        flops=6 * work_rows * model_width * width,
        moved=16 * MIB,
        room=60,
    )
    queries = steps_b.ride(queries)
    context, attn_term = call(
        attend_kernel,
        (seq, queries, keys_values, attn_matrix),
        [SMEM] + [VMEM] * 3,
        [pltpu.HBM((work_rows, width), BF16), pltpu.HBM((work_rows, model_width), BF16)],
        flops=2 * work_rows * model_width * width,
        moved=16 * MIB,
        room=60,
    )
    attn_other = steps_b.ride(pair_swap(attn_term))

    pieces, starts = steps_b.finish()
    count = len(pieces)
    residual, work_two, hidden, grad_proj, grad_two, down_term, *early_b = call(
        functools.partial(hidden_kernel, count, spare, early),
        (starts, chips, core, tokens_all, attn_term, attn_other, gains, cot_all, *pieces),
        [SMEM] * 3 + [VMEM] * 5 + [ANY] * count,
        [
            shape_of(work_rows, model_width, F32),
            shape_of(work_rows, model_width, BF16),
            shape_of(work_rows, whole_units + LANES, BF16),
            shape_of(work_rows, 2 * whole_units + LANES, BF16),
            shape_of(work_rows, model_width, BF16),
            shape_of(work_rows, model_width, BF16),
        ]
        + [pltpu.HBM((early, depth, blob_b.shape[1]), BF16)] * (2 if early else 0),
        [
            pltpu.VMEM((model_width, blob_b.shape[1]), BF16),
            pltpu.SemaphoreType.DMA((count,)),
        ],
        flops=12 * work_rows * model_width * units,
        moved=32 * MIB,
        room=60,
    )
    grad_two_other = pair_swap(grad_two)
    factors = work_two, grad_proj, cot_all, hidden
    if early:
        rest_b = weight_terms(ring, chips, core, early, *factors, tail=LANES, room=60)
        steps_b = Stepped(ring.scatter_sum(early_b, rest_b, "sum_b"))
    else:
        rest_b = ()
        steps_b = Stepped(summed_terms(*factors, tail=LANES))
    grad_two, rest_b = steps_b.ride((grad_two, rest_b))
    grad_residual, grad_low, gain_two, grad_queries, grad_own, to_before, to_after = call(
        attend_back_kernel,
        (
            seq, residual, gains, grad_two, grad_two_other, cot_all, attn_matrix,
            queries, keys_values, cosine, sine,
        ),
        [SMEM] + [VMEM] * 10,
        [
            pltpu.HBM((work_rows, model_width), F32),
            pltpu.HBM((work_rows, model_width), BF16),
            shape_of(8, model_width, F32),
            shape_of(work_rows, width, BF16),
            shape_of(work_rows, 2 * width, F32),
            pltpu.HBM((HALF, 2 * width), BF16),
            pltpu.HBM((HALF, 2 * width), BF16),
        ],
        [pltpu.VMEM((reach_rows, 2 * width), F32)],
        flops=4 * work_rows * model_width * width,
        moved=24 * MIB,
    )
    to_before, to_after = steps_b.ride((to_before, to_after))
    from_next = passed_along(to_before, SEQ, -1)
    from_prev = passed_along(to_after, SEQ, 1)

    down_other = pair_swap(other_rows(down_term, row_count))
    grad_queries = steps_b.ride(grad_queries)
    last = call(
        functools.partial(last_kernel, early),
        (
            chips, core, grad_queries, grad_own, from_prev, from_next, cosine, sine, tokens_all,
            gain_two, work_one, grad_low, context, whole_a,
        ),
        [SMEM] * 2 + [VMEM] * 11 + [ANY],
        [
            shape_of(work_rows, 3 * width, BF16),
            shape_of(work_rows, model_width, BF16),
            shape_of(model_width, LANES, BF16),
        ]
        + [pltpu.HBM((early, depth, blob_a.shape[1]), BF16)] * (2 if early else 0),
        [
            pltpu.VMEM((work_rows, 2 * width), F32),
            pltpu.VMEM((model_width, 3 * width), BF16),
            pltpu.SemaphoreType.DMA,
        ],
        flops=6 * work_rows * model_width * width,
        moved=16 * MIB,
        room=60,
    )
    grad_qkv, grad_one, gain_columns, *early_a = steps_b.ride(tuple(last))
    one_other = pair_swap(other_rows(grad_one, row_count))
    grad_qkv = steps_b.ride(grad_qkv)
    factors = work_one, grad_qkv, grad_low, context, gain_columns
    if early:
        rest_a = weight_terms(ring, chips, core, early, *factors)
        steps_a = Stepped(ring.scatter_sum(early_a, rest_a, "sum_a"))
    else:
        steps_a = Stepped(summed_terms(*factors))
    steps_a.step()
    steps_a.step()
    one_other = steps_a.hold(one_other)
    steps_a.step()
    steps_a.step()
    steps_b.step()
    down_other = steps_a.hold(down_other)
    steps_a.beside(steps_b)
    steps_a.step()
    steps_a.step()
    steps_a.beside(steps_b)
    share_b = steps_b.finish()
    share_a = steps_a.finish()

    output = (
        own_rows(residual, row_count)
        + (own_rows(down_term, row_count).astype(F32) + down_other.astype(F32))
    ).astype(BF16)

    gain_one = gains[0:1]
    unit_one, inverse_one = unit_of(tokens.astype(F32))
    grad_low_one = own_rows(grad_one, row_count).astype(F32) + one_other.astype(F32)
    grad_tokens = (
        own_rows(grad_residual, row_count)
        + norm_back(grad_low_one, gain_one, unit_one, inverse_one)
    ).astype(BF16)

    def share_b_part(part):
        tail = 3 * whole_units + part * spare
        main = share_b[:, part * whole_units : (part + 1) * whole_units]
        return jnp.concatenate([main, share_b[:, tail : tail + spare]], axis=1)

    share_gains = share_a[:, 4 * width : 4 * width + 2] + share_a[:, 4 * width + 2 : 4 * width + 4]
    share_gain_one = share_gains[:, 0]
    share_gain_one = share_gain_one + pair_swap(share_gain_one)
    return (
        output,
        grad_tokens,
        share_gain_one,
        share_a[:, : 3 * width].reshape(depth, 3, width),
        share_a[:, 3 * width : 4 * width].T,
        share_gains[:, 1],
        jnp.stack([share_b_part(0), share_b_part(1)], axis=1),
        share_b_part(2).T,
    )


def solution(mesh):
    return jax.shard_map(
        local,
        mesh=mesh,
        in_specs=(
            P((SEQ, PAIR), None),
            P(SEQ),
            P(SEQ, None, PAIR),
            P(PAIR, SEQ),
            P(SEQ),
            P(SEQ, None, PAIR),
            P(PAIR, SEQ),
            P((SEQ, PAIR), None),
        ),
        out_specs=(
            P((SEQ, PAIR), None),
            P((SEQ, PAIR), None),
            P(SEQ),
            P(SEQ, None, PAIR),
            P(PAIR, SEQ),
            P(SEQ),
            P(SEQ, None, PAIR),
            P(PAIR, SEQ),
        ),
        check_vma=False,
    )
```

```python
import functools
import math

import jax
import jax.numpy as jnp
import numpy as np
from jax import lax
from jax.experimental import pallas as pl
from jax.experimental.pallas import tpu as pltpu
from jax.sharding import PartitionSpec as P

HD = 64
HALF = 64
LANES = 128
COST = 1

EPSILON = 1e-05
THETA = 10000.0
SEQ = "seq"
PAIR = "fsdp"
F32 = jnp.float32
BF16 = jnp.bfloat16


def passed_along(block, axis, distance):
    devices = range(lax.axis_size(axis))
    route = [(i - distance, i) for i in devices if i - distance in devices]
    return lax.ppermute(block, axis, route)


def pair_swap(block):
    return lax.ppermute(block, PAIR, [(0, 1), (1, 0)])


class Ring:
    def __init__(self, width):
        size = lax.axis_size(SEQ)
        self.chips = size // 2
        rows = self.chips // 2
        order = [2 * z for z in range(rows)] + [2 * z + 1 for z in reversed(range(rows))]
        place = np.argsort(np.array(order))
        self.up, self.down = [], []
        for i in range(size):
            chip, core = divmod(i, 2)
            self.up.append((i, order[(place[chip] + 1) % self.chips] * 2 + core))
            self.down.append((i, order[(place[chip] - 1) % self.chips] * 2 + core))
        self.swap = [(i, i ^ 1) for i in range(size)]
        me = lax.axis_index(SEQ)
        self.core = me % 2
        self.place = jnp.asarray(place, jnp.int32)[me // 2]
        self.order = jnp.asarray(order, jnp.int32)
        self.half = self.chips // 2
        self.slots = [self.half]
        for step in range(1, self.half):
            self.slots += [self.half + step, self.half - step]
        self.slots.append(0)
        self.short = width == LANES * self.chips

    def chips_at(self, distances):
        steps = jnp.asarray(distances, jnp.int32)
        return self.order[(self.place + steps + self.chips) % self.chips]

    def go(self, block, route, name):
        with jax.named_scope(name):
            return lax.ppermute(block, SEQ, route)

    def gather(self, block, name, plan):
        if not self.short:
            whole = lax.all_gather(block, SEQ, axis=0, tiled=True)
            return [whole], jnp.zeros(1, jnp.int32)
        rows = block.shape[0]
        middle = rows // 2
        upward = downward = block
        order = [0]
        for step in range(1, self.half + 1):
            order += [-step, step]
        places = [(d, 0, middle if d == self.half else 0) for d in order]
        places += [(d, 1, offset) for d, _, offset in places]
        distances, others, offsets = np.array(places, np.int32).T
        cores = self.chips_at(distances) * 2 + jnp.where(others == 1, 1 - self.core, self.core)
        starts = cores * rows + offsets
        held = {0: (block, 0)}
        swapped = {}
        for step in range(1, self.half + 1):
            if step == self.half:
                upward, downward = upward[:middle], downward[middle:]
            upward = self.go(upward, self.up, f"{name}_up_{step}")
            downward = self.go(downward, self.down, f"{name}_down_{step}")
            meanwhile = [d for d in plan[step - 1] if d in held]
            came = [self.go(held[d][0], self.swap, f"{name}_cores_{d}") for d in meanwhile]
            upward, downward, starts, *came = yield upward, downward, starts, *came
            swapped.update(zip(meanwhile, came))
            held[-step] = upward, 0
            held[step] = downward, middle if step == self.half else 0
        for d in held:
            if d not in swapped:
                swapped[d] = self.go(held[d][0], self.swap, f"{name}_cores_{d}")
        pieces = [held[d][0] for d in held] + [swapped[d] for d in held]
        return pieces, starts

    def scatter_sum(self, early, rest, name):
        kept_early, away_early = early
        kept_rest, away_rest = rest
        count, rows = kept_early.shape[:2]
        middle = rows // 2
        came_early = self.go(away_early, self.swap, f"{name}_cores_early")
        came_rest = self.go(away_rest, self.swap, f"{name}_cores_rest")

        def at(slot):
            i = self.slots.index(slot)
            if i < count:
                return kept_early[i].astype(F32) + came_early[i].astype(F32)
            return kept_rest[i - count].astype(F32) + came_rest[i - count].astype(F32)

        far = at(self.half).astype(BF16)
        upward, downward = far[:middle], far[middle:]
        for step in range(1, self.half + 1):
            upward, downward = yield upward, downward
            upward = self.go(upward, self.up, f"{name}_up_{step}")
            downward = self.go(downward, self.down, f"{name}_down_{step}")
            upward, downward = yield upward, downward
            upward, downward = upward.astype(F32), downward.astype(F32)
            if step == 1:
                upward = jnp.pad(upward, ((0, rows - middle), (0, 0)))
                downward = jnp.pad(downward, ((middle, 0), (0, 0)))
            if step < self.half:
                upward = (at(self.half - step) + upward).astype(BF16)
                downward = (at(self.half + step) + downward).astype(BF16)
        return at(0) + upward + downward


class Stepped:
    def __init__(self, steps):
        self.steps, self.state, self.result = steps, None, None
        self.advance()

    def advance(self):
        try:
            if self.state is not None:
                self.state = lax.optimization_barrier(self.state)
            self.state = self.steps.send(self.state)
        except StopIteration as end:
            self.steps, self.state, self.result = None, None, end.value

    def ride(self, value):
        if self.steps is not None:
            value, self.state = lax.optimization_barrier((value, self.state))
            self.advance()
        return value

    def hold(self, value):
        if self.steps is not None:
            value, self.state = lax.optimization_barrier((value, self.state))
        return value

    def step(self):
        if self.steps is not None:
            self.advance()

    def beside(self, other):
        if self.steps is not None and other.steps is not None:
            self.state, other.state = lax.optimization_barrier((self.state, other.state))
            self.advance()
            other.advance()

    def finish(self):
        while self.steps is not None:
            self.advance()
        return self.result


VMEM = pl.BlockSpec(memory_space=pltpu.VMEM)
ANY = pl.BlockSpec(memory_space=pltpu.HBM)
SMEM = pl.BlockSpec(memory_space=pltpu.SMEM)
MIB = 1024 * 1024


def shape_of(rows, columns, kind):
    return jax.ShapeDtypeStruct((rows, columns), kind)


def call(kernel, args, specs, outs, scratch=(), flops=0, moved=0, room=20):
    return pl.pallas_call(
        kernel,
        in_specs=specs,
        out_specs=[VMEM] * len(outs),
        out_shape=outs,
        scratch_shapes=list(scratch),
        compiler_params=pltpu.CompilerParams(vmem_limit_bytes=room * MIB),
        cost_estimate=pl.CostEstimate(
            flops=flops // COST, bytes_accessed=moved // COST, transcendentals=0
        ),
    )(*args)


def placing(starts, pieces, whole, ready):
    copies = []
    for i, piece in enumerate(pieces):
        rows = piece.shape[0]
        start = pl.multiple_of(starts[i], rows)
        copies.append(
            pltpu.make_async_copy(piece, whole.at[pl.ds(start, rows), :], ready.at[i])
        )
    return copies


def lane_of(rows, width):
    return lax.broadcasted_iota(jnp.int32, (rows, width), 1)


def halves_swapped(values):
    width = values.shape[1]
    lane = lane_of(*values.shape)
    ahead = pltpu.roll(values, width - HD // 2, 1)
    behind = pltpu.roll(values, HD // 2, 1)
    return jnp.where(lane % HD < HD // 2, ahead, behind)


def turned_by(values, cosine, sine):
    copies = values.shape[1] // LANES
    cosine = jnp.concatenate([cosine] * copies, axis=1)
    sine = jnp.concatenate([sine] * copies, axis=1)
    return values * cosine + halves_swapped(values) * sine


def unit_of(values):
    average = jnp.mean(values, axis=-1, keepdims=True)
    centered = values - average
    inverse = lax.rsqrt(jnp.mean(centered * centered, axis=-1, keepdims=True) + EPSILON)
    return centered * inverse, inverse


def first_kernel(count, width, starts, seq, tokens, before, after, cosine, sine, *refs):
    pieces = refs[:count]
    whole, matrix, gains, work, queries, keys_values, wide_cosine, wide_sine = refs[count:-4]
    context, term = refs[-4:-2]
    all_rows, ready = refs[-2:]
    copies = placing(starts, pieces, whole, ready)
    for copy in copies:
        copy.start()
    joined_rows(before, tokens, after, all_rows)
    wide_cosine[...] = jnp.concatenate([cosine[...]] * 4, axis=1)
    wide_sine[...] = jnp.concatenate([-sine[...], sine[...]] * 2, axis=1)
    unit, _ = unit_of(all_rows[...].astype(F32))
    for copy in copies:
        copy.wait()
    matrix[...] = whole[:, 3 * width : 4 * width]
    gains[...] = whole[:, 4 * width :].astype(F32).T[:8]
    all_rows[...] = (unit * gains[0:1, :]).astype(BF16)
    rows = work.shape[0]
    own = slice(HALF, HALF + rows)
    work[...] = all_rows[own, :]
    for start in range(0, 3 * width, 256):
        columns = whole[:, start : start + 256]
        if start < width:
            part = dot(work[...], columns)
            queries[:, start : start + 256] = turned_by(part, wide_cosine[own], wide_sine[own]).astype(BF16)
        else:
            part = dot(all_rows[...], columns)
            if start < 2 * width:
                part = turned_by(part, wide_cosine[...], wide_sine[...])
            keys_values[:, start - width : start - width + 256] = part.astype(BF16)
    attend(seq, queries, keys_values, matrix, context, term)


def window(seq, tile, tiles):
    row = lax.broadcasted_iota(jnp.int32, (2 * LANES, 2 * LANES), 0) % LANES
    column = lax.broadcasted_iota(jnp.int32, (2 * LANES, 2 * LANES), 1)
    ahead = column - row
    inside = (ahead >= 0) & (ahead <= 2 * HALF)
    if tile == 0:
        inside &= (seq[0] > 0) | (column >= HALF)
    if tile == tiles - 1:
        inside &= (seq[0] < seq[1] - 1) | (column < 2 * LANES - HALF)
    return inside


def heads_apart(pair):
    lane = lane_of(*pair.shape)
    zero = jnp.zeros_like(pair)
    return jnp.concatenate(
        [jnp.where(lane < HD, pair, zero), jnp.where(lane < HD, zero, pair)], axis=0
    )


def heads_joined(apart):
    rows = apart.shape[0] // 2
    return jnp.where(lane_of(rows, apart.shape[1]) < HD, apart[:rows], apart[rows:])


def shares_of(apart, keys, inside):
    scores = dot(apart, keys, (1, 1)) * (1.0 / math.sqrt(HD))
    scores = jnp.where(inside, scores, -1e30)
    expo = jnp.exp(scores - jnp.max(scores, axis=-1, keepdims=True))
    return expo / jnp.sum(expo, axis=-1, keepdims=True)


def joined_rows(before, own, after, whole):
    rows = own.shape[0]
    whole[:HALF] = before[...]
    whole[HALF : HALF + rows] = own[...]
    whole[HALF + rows :] = after[...]


def attend(seq, queries, keys_values, matrix, context, term):
    rows, width = queries.shape
    tiles = rows // LANES
    for tile in range(tiles):
        inside = window(seq, tile, tiles)
        at = slice(tile * LANES, tile * LANES + LANES)
        reach = slice(tile * LANES, tile * LANES + 2 * LANES)
        for start in range(0, width, LANES):
            columns = slice(start, start + LANES)
            apart = heads_apart(queries[at, columns])
            shares = shares_of(apart, keys_values[reach, columns], inside)
            values = keys_values[reach, width + start : width + start + LANES]
            context[at, columns] = heads_joined(dot(shares.astype(BF16), values)).astype(BF16)
    term[...] = dot(context[...], matrix[...], (1, 1)).astype(BF16)


def hidden_kernel(count, spare, early, starts, chips, core, tokens, term, term_other, gains, cot, *refs):
    pieces = refs[:count]
    residual, work, hidden, grad_proj, grad_two, down, *terms, whole, ready = refs[count:]
    copies = placing(starts, pieces, whole, ready)
    for copy in copies:
        copy.start()
    added = term[...].astype(F32) + term_other[...].astype(F32)
    residual[...] = tokens[...].astype(F32) + added
    unit, _ = unit_of(residual[...])
    work[...] = (unit * gains[1:2, :]).astype(BF16)
    for copy in copies:
        copy.wait()
    units = hidden.shape[1] - LANES

    def grads(gate, up, back):
        share = 0.5 + 0.5 * lax.erf(gate * (1.0 / math.sqrt(2.0)))
        bell = jnp.exp(-0.5 * gate * gate) * (1.0 / math.sqrt(2.0 * math.pi))
        gelu = gate * share
        return gelu * up, back * up * (share + gate * bell), back * gelu

    for start in range(0, units, 256):
        stop = min(units, start + 256)
        gate = dot(work[...], whole[:, start:stop])
        up = dot(work[...], whole[:, units + start : units + stop])
        back = dot(cot[...], whole[:, 2 * units + start : 2 * units + stop])
        here, grad_gate, grad_up = grads(gate, up, back)
        hidden[:, start:stop] = here.astype(BF16)
        grad_proj[:, start:stop] = grad_gate.astype(BF16)
        grad_proj[:, units + start : units + stop] = grad_up.astype(BF16)
    tail = whole[:, 3 * units :]
    both = dot(work[...], tail)
    back = pltpu.roll(dot(cot[...], tail), LANES - 2 * spare, 1)
    parts = grads(both, pltpu.roll(both, LANES - spare, 1), back)
    lane = lane_of(*both.shape)
    here, grad_gate, grad_up = [jnp.where(lane < spare, part, 0.0) for part in parts]
    hidden[:, units:] = pltpu.roll(here, 2 * spare, 1).astype(BF16)
    grad_proj[:, 2 * units :] = (grad_gate + pltpu.roll(grad_up, spare, 1)).astype(BF16)
    grad_two[...] = (
        dot(grad_proj[:, : 2 * units], whole[:, : 2 * units], (1, 1))
        + dot(grad_proj[:, 2 * units :], tail, (1, 1))
    ).astype(BF16)
    down[...] = dot(hidden[...], whole[:, 2 * units :], (1, 1)).astype(BF16)
    if early:
        early_rows(early, chips, core, LANES, [(work, grad_proj), (cot, hidden)], None, *terms)


def attend_back_kernel(
    seq, residual, gains, grad_two, grad_two_other, cot, matrix, queries, keys_values,
    cosine, sine, grad_residual, grad_low, gain_two, grad_queries, grad_own, to_before, to_after,
    grad_all,
):
    rows, width = queries.shape
    unit, inverse = unit_of(residual[...])
    grad = grad_two[...].astype(F32) + grad_two_other[...].astype(F32)
    gain_two[...] = jnp.broadcast_to(jnp.sum(grad * unit, axis=0, keepdims=True), gain_two.shape)
    scaled = grad * gains[1:2, :]
    middle = jnp.mean(scaled, axis=-1, keepdims=True)
    along = jnp.mean(scaled * unit, axis=-1, keepdims=True)
    total = cot[...].astype(F32) + inverse * (scaled - middle - unit * along)
    grad_residual[...] = total
    grad_low[...] = total.astype(BF16)
    grad_context = dot(grad_low[...], matrix[...]).astype(BF16)
    grad_all[...] = jnp.zeros_like(grad_all)
    scale = 1.0 / math.sqrt(HD)
    tiles = rows // LANES
    for tile in range(tiles):
        inside = window(seq, tile, tiles)
        at = slice(tile * LANES, tile * LANES + LANES)
        own_at = slice(HALF + tile * LANES, HALF + tile * LANES + LANES)
        reach = slice(tile * LANES, tile * LANES + 2 * LANES)
        for start in range(0, width, LANES):
            columns = slice(start, start + LANES)
            beside = slice(width + start, width + start + LANES)
            apart = heads_apart(queries[at, columns])
            keys = keys_values[reach, columns]
            shares = shares_of(apart, keys, inside)
            grad_apart = heads_apart(grad_context[at, columns])
            grad_shares = dot(grad_apart, keys_values[reach, beside], (1, 1))
            lost = jnp.sum(grad_shares * shares, axis=-1, keepdims=True)
            grad_scores = (shares * (grad_shares - lost)).astype(BF16)
            grad_here = heads_joined(dot(grad_scores, keys)) * scale
            grad_queries[at, columns] = turned_by(grad_here, cosine[own_at], -sine[own_at]).astype(BF16)
            grad_all[reach, columns] += dot(grad_scores, apart, (0, 0)) * scale
            grad_all[reach, beside] += dot(shares.astype(BF16), grad_apart, (0, 0))
    to_before[...] = grad_all[:HALF].astype(BF16)
    grad_own[...] = grad_all[HALF : HALF + rows]
    to_after[...] = grad_all[HALF + rows :].astype(BF16)


def last_kernel(
    early, chips, core, grad_queries, grad_own, from_before, from_after, cosine, sine, tokens,
    gain_two, work, grad_low, context, matrix_whole, grad_qkv, grad_one, gain_columns, *refs,
):
    *parts, grad_all, matrix, ready = refs
    rows, width = grad_queries.shape
    fetch = pltpu.make_async_copy(matrix_whole.at[:, : 3 * width], matrix, ready)
    fetch.start()
    grad_all[...] = grad_own[...]
    grad_all[:HALF] += from_before[...].astype(F32)
    grad_all[rows - HALF :] += from_after[...].astype(F32)
    grad_qkv[:, :width] = grad_queries[...]
    own = slice(HALF, HALF + rows)
    grad_keys = turned_by(grad_all[:, :width], cosine[own], -sine[own])
    grad_qkv[:, width : 2 * width] = grad_keys.astype(BF16)
    grad_qkv[:, 2 * width :] = grad_all[:, width:].astype(BF16)
    fetch.wait()
    grad = dot(grad_qkv[...], matrix[...], (1, 1))
    grad_one[...] = grad.astype(BF16)
    unit, _ = unit_of(tokens[...].astype(F32))
    gain_one = jnp.sum(grad * unit, axis=0, keepdims=True)
    gain = jnp.concatenate([gain_one, gain_two[0:1, :]], axis=0)
    high = gain.astype(BF16).astype(F32)
    spare = jnp.zeros((LANES - 4, gain.shape[1]), F32)
    gain_columns[...] = jnp.concatenate([high, gain - high, spare], axis=0).T.astype(BF16)
    if early:
        pairs = [(work, grad_qkv), (grad_low, context)]
        early_rows(early, chips, core, 0, pairs, gain_columns, *parts)


def weight_rows(i, tail, lower, pairs, extra, kept, away):
    depth = kept.shape[1]

    def put(block, start, stop):
        kept[i, :, start:stop] = jnp.where(lower, block[:depth], block[depth:]).astype(BF16)
        away[i, :, start:stop] = jnp.where(lower, block[depth:], block[:depth]).astype(BF16)

    base = 0
    rest = 0.0
    for left, right in pairs:
        width = right.shape[1] - tail
        turned = left.T
        for start in range(0, width, 512):
            stop = min(width, start + 512)
            product = jnp.dot(turned, right[:, start:stop], preferred_element_type=F32)
            put(product, base + start, base + stop)
        base += width
        if tail:
            rest += jnp.dot(turned, right[:, width:], preferred_element_type=F32)
    if tail:
        put(rest, base, base + tail)
    if extra is not None:
        put(extra.astype(F32), base, base + extra.shape[1])


def early_rows(count, chips, core, tail, pairs, extra, kept, away):
    lower = core[0] == 0
    for i in range(count):
        lanes = pl.ds(pl.multiple_of(chips[i] * LANES, LANES), LANES)
        blocks = [(left[:, lanes], right) for left, right in pairs]
        more = None if extra is None else extra[lanes, :]
        weight_rows(i, tail, lower, blocks, more, kept, away)


def weight_kernel(tail, chips, core, left_one, left_two, right_one, right_two, *refs):
    pairs = [(left_one[...], right_one), (left_two[...], right_two)]
    extra = refs[0][...] if len(refs) == 3 else None
    weight_rows(0, tail, core[0] == 0, pairs, extra, *refs[-2:])


def weight_terms(ring, chips, core, skip, left_one, right_one, left_two, right_two, extra=None, tail=0, room=20):
    work_rows, width = left_one.shape
    lanes = width // ring.chips
    depth = lanes // 2
    total = right_one.shape[1] + right_two.shape[1] - tail
    more_args, more_specs = [], []
    if extra is not None:
        total += extra.shape[1]
        more_args.append(extra)
        more_specs.append(
            pl.BlockSpec((lanes, extra.shape[1]), lambda i, chips, core: (chips[i + skip], 0))
        )

    count = ring.chips - skip

    def left_map(i, chips, core):
        return (0, chips[i + skip])

    def whole_map(i, chips, core):
        return (0, 0)

    return pl.pallas_call(
        functools.partial(weight_kernel, tail),
        grid_spec=pltpu.PrefetchScalarGridSpec(
            num_scalar_prefetch=2,
            grid=(count,),
            in_specs=[
                pl.BlockSpec((work_rows, lanes), left_map),
                pl.BlockSpec((work_rows, lanes), left_map),
                pl.BlockSpec(right_one.shape, whole_map),
                pl.BlockSpec(right_two.shape, whole_map),
                *more_specs,
            ],
            out_specs=[
                pl.BlockSpec((1, depth, total), lambda i, chips, core: (i, 0, 0)),
                pl.BlockSpec((1, depth, total), lambda i, chips, core: (i, 0, 0)),
            ],
        ),
        out_shape=[
            pltpu.HBM((count, depth, total), BF16),
            pltpu.HBM((count, depth, total), BF16),
        ],
        compiler_params=pltpu.CompilerParams(vmem_limit_bytes=room * MIB),
        cost_estimate=pl.CostEstimate(
            flops=2 * work_rows * lanes * count * total // COST,
            bytes_accessed=2 * (lanes * count + work_rows) * total // COST,
            transcendentals=0,
        ),
    )(
        chips,
        core,
        left_one,
        left_two,
        right_one,
        right_two,
        *more_args,
    )


def summed_terms(left_one, right_one, left_two, right_two, extra=None, tail=0):
    yield from ()
    terms = [dot(left_one, right_one, (0, 0)), dot(left_two, right_two, (0, 0))]
    if tail:
        rest = terms[0][:, -tail:] + terms[1][:, -tail:]
        terms = [terms[0][:, :-tail], terms[1][:, :-tail], rest]
    terms = [t.astype(BF16) for t in terms] + ([] if extra is None else [extra])
    terms = jnp.concatenate(terms, axis=1)
    return lax.psum_scatter(terms, SEQ, scatter_dimension=0, tiled=True).astype(F32)


def norm_back(grad_rows, gain, unit_rows, inverse):
    scaled = grad_rows * gain
    centered_grad = (
        scaled
        - jnp.mean(scaled, axis=-1, keepdims=True)
        - unit_rows * jnp.mean(scaled * unit_rows, axis=-1, keepdims=True)
    )
    return inverse * centered_grad


def rotary_tables(positions):
    half_size = HD // 2
    frequency = THETA ** (-(jnp.arange(half_size, dtype=F32) * 2.0) / HD)
    angles = positions.astype(F32)[:, None] * frequency[None, :]
    return jnp.cos(angles), jnp.sin(angles)


def edge_rows(block):
    blocks = range(lax.axis_size(SEQ))
    route = [(2 * i, 2 * i - 2) for i in blocks if i > 0]
    route += [(2 * i + 1, 2 * i + 3) for i in blocks if i + 1 in blocks]
    return lax.ppermute(block, (SEQ, PAIR), route)


def pair_rows(mine, other):
    first = lax.axis_index(PAIR) == 0
    return jnp.concatenate([jnp.where(first, mine, other), jnp.where(first, other, mine)], axis=0)


def own_rows(values, row_count):
    return lax.dynamic_slice_in_dim(values, lax.axis_index(PAIR) * row_count, row_count, 0)


def other_rows(values, row_count):
    return lax.dynamic_slice_in_dim(values, (1 - lax.axis_index(PAIR)) * row_count, row_count, 0)


def dot(a, b, over=(1, 0)):
    return lax.dot_general(a, b, (((over[0],), (over[1],)), ((), ())), preferred_element_type=F32)


def padded_to_lanes(values):
    return jnp.pad(values, ((0, 0), (0, -values.shape[1] % LANES)))


def local(tokens, norm1_gain, w_qkv, w_attn_out, norm2_gain, w_in, w_down, cotangent):
    row_count, model_width = tokens.shape
    ring = Ring(model_width)
    early = 3 if ring.short else 0
    chips, core = ring.chips_at(ring.slots), ring.core.reshape(1)
    depth, _, width = w_qkv.shape
    units = w_down.shape[0]
    gains = padded_to_lanes(jnp.stack([norm1_gain, norm2_gain], axis=1))
    blob_a = jnp.concatenate([w_qkv.reshape(depth, -1), w_attn_out.T, gains], axis=1)
    whole_units = units // LANES * LANES
    spare = units - whole_units
    parts = [w_in[:, 0], w_in[:, 1], w_down.T]
    blob_b = jnp.concatenate(
        [part[:, :whole_units] for part in parts] + [part[:, whole_units:] for part in parts], axis=1
    )
    blob_b = jnp.pad(blob_b, ((0, 0), (0, LANES - 3 * spare)))
    steps_a = Stepped(ring.gather(blob_a, "gather_a", [[0], [-1, 1], [], [-2]]))
    first = lax.axis_index(PAIR) == 0
    edge = edge_rows(jnp.where(first, tokens[:HALF], tokens[-HALF:]))
    edge = steps_a.hold(edge)
    joined = jnp.concatenate([tokens, edge, cotangent], axis=0)
    other = pair_swap(joined)
    steps_a.step()
    blob_b = steps_a.ride(blob_b)
    steps_b = Stepped(ring.gather(blob_b, "gather_b", [[], [], [0, -1, 1], [-2, 2]]))
    other = steps_a.hold(other)
    tokens_all = pair_rows(tokens, other[:row_count])
    beside = other[row_count : row_count + HALF]
    tokens_before = jnp.where(first, beside, edge)
    tokens_after = jnp.where(first, edge, beside)
    cot_all = pair_rows(cotangent, other[row_count + HALF :])

    work_rows = row_count * lax.axis_size(PAIR)
    reach_rows = work_rows + 2 * HALF
    seq = jnp.stack([lax.axis_index(SEQ), lax.axis_size(SEQ)]).astype(jnp.int32)
    cosine, sine = rotary_tables(
        seq[0] * work_rows - HALF + jnp.arange(reach_rows, dtype=jnp.int32)
    )
    inputs = tokens_all, tokens_before, tokens_after, cot_all, seq, cosine, sine, chips, core
    inputs = steps_a.hold(inputs)
    tokens_all, tokens_before, tokens_after, cot_all, seq, cosine, sine, chips, core = inputs
    steps_a.beside(steps_b)
    pieces, starts = steps_a.finish()
    count = len(pieces)
    whole_a, attn_matrix, gains, work_one, queries, keys_values, *later = call(
        functools.partial(first_kernel, count, width),
        (starts, seq, tokens_all, tokens_before, tokens_after, cosine, sine, *pieces),
        [SMEM] * 2 + [VMEM] * 5 + [ANY] * count,
        [
            shape_of(model_width, blob_a.shape[1], BF16),
            shape_of(model_width, width, BF16),
            shape_of(8, model_width, F32),
            shape_of(work_rows, model_width, BF16),
            shape_of(work_rows, width, BF16),
            shape_of(reach_rows, 2 * width, BF16),
            shape_of(reach_rows, LANES, F32),
            shape_of(reach_rows, LANES, F32),
            shape_of(work_rows, width, BF16),
            shape_of(work_rows, model_width, BF16),
        ],
        [pltpu.VMEM((reach_rows, model_width), BF16), pltpu.SemaphoreType.DMA((count,))],
        flops=6 * work_rows * model_width * width,
        moved=16 * MIB,
        room=60,
    )
    cosine, sine, context, attn_term = later
    attn_term = steps_b.ride(attn_term)
    attn_other = steps_b.ride(pair_swap(attn_term))

    pieces, starts = steps_b.finish()
    count = len(pieces)
    residual, work_two, hidden, grad_proj, grad_two, down_term, *early_b = call(
        functools.partial(hidden_kernel, count, spare, early),
        (starts, chips, core, tokens_all, attn_term, attn_other, gains, cot_all, *pieces),
        [SMEM] * 3 + [VMEM] * 5 + [ANY] * count,
        [
            shape_of(work_rows, model_width, F32),
            shape_of(work_rows, model_width, BF16),
            shape_of(work_rows, whole_units + LANES, BF16),
            shape_of(work_rows, 2 * whole_units + LANES, BF16),
            shape_of(work_rows, model_width, BF16),
            shape_of(work_rows, model_width, BF16),
        ]
        + [pltpu.HBM((early, depth, blob_b.shape[1]), BF16)] * (2 if early else 0),
        [
            pltpu.VMEM((model_width, blob_b.shape[1]), BF16),
            pltpu.SemaphoreType.DMA((count,)),
        ],
        flops=12 * work_rows * model_width * units,
        moved=32 * MIB,
        room=60,
    )
    grad_two_other = pair_swap(grad_two)
    factors = work_two, grad_proj, cot_all, hidden
    if early:
        rest_b = weight_terms(ring, chips, core, early, *factors, tail=LANES, room=60)
        steps_b = Stepped(ring.scatter_sum(early_b, rest_b, "sum_b"))
    else:
        rest_b = ()
        steps_b = Stepped(summed_terms(*factors, tail=LANES))
    grad_two, rest_b = steps_b.ride((grad_two, rest_b))
    grad_residual, grad_low, gain_two, grad_queries, grad_own, to_before, to_after = call(
        attend_back_kernel,
        (
            seq, residual, gains, grad_two, grad_two_other, cot_all, attn_matrix,
            queries, keys_values, cosine, sine,
        ),
        [SMEM] + [VMEM] * 10,
        [
            pltpu.HBM((work_rows, model_width), F32),
            pltpu.HBM((work_rows, model_width), BF16),
            shape_of(8, model_width, F32),
            shape_of(work_rows, width, BF16),
            shape_of(work_rows, 2 * width, F32),
            pltpu.HBM((HALF, 2 * width), BF16),
            pltpu.HBM((HALF, 2 * width), BF16),
        ],
        [pltpu.VMEM((reach_rows, 2 * width), F32)],
        flops=4 * work_rows * model_width * width,
        moved=24 * MIB,
    )
    to_before, to_after = steps_b.ride((to_before, to_after))
    from_next = passed_along(to_before, SEQ, -1)
    from_prev = passed_along(to_after, SEQ, 1)

    down_other = pair_swap(other_rows(down_term, row_count))
    from_prev, from_next = steps_b.ride((from_prev, from_next))
    last = call(
        functools.partial(last_kernel, early),
        (
            chips, core, grad_queries, grad_own, from_prev, from_next, cosine, sine, tokens_all,
            gain_two, work_one, grad_low, context, whole_a,
        ),
        [SMEM] * 2 + [VMEM] * 11 + [ANY],
        [
            shape_of(work_rows, 3 * width, BF16),
            shape_of(work_rows, model_width, BF16),
            shape_of(model_width, LANES, BF16),
        ]
        + [pltpu.HBM((early, depth, blob_a.shape[1]), BF16)] * (2 if early else 0),
        [
            pltpu.VMEM((work_rows, 2 * width), F32),
            pltpu.VMEM((model_width, 3 * width), BF16),
            pltpu.SemaphoreType.DMA,
        ],
        flops=6 * work_rows * model_width * width,
        moved=16 * MIB,
        room=60,
    )
    grad_qkv, grad_one, gain_columns, *early_a = steps_b.ride(tuple(last))
    one_other = pair_swap(other_rows(grad_one, row_count))
    grad_qkv = steps_b.ride(grad_qkv)
    factors = work_one, grad_qkv, grad_low, context, gain_columns
    if early:
        rest_a = weight_terms(ring, chips, core, early, *factors)
        steps_a = Stepped(ring.scatter_sum(early_a, rest_a, "sum_a"))
    else:
        steps_a = Stepped(summed_terms(*factors))
    steps_a.step()
    steps_a.step()
    steps_a.step()
    steps_a.step()
    steps_b.step()
    one_other = steps_a.hold(one_other)
    steps_a.beside(steps_b)
    steps_a.step()
    down_other = steps_a.hold(down_other)
    steps_a.step()
    steps_a.beside(steps_b)
    share_b = steps_b.finish()
    share_a = steps_a.finish()

    output = (
        own_rows(residual, row_count)
        + (own_rows(down_term, row_count).astype(F32) + down_other.astype(F32))
    ).astype(BF16)

    gain_one = gains[0:1]
    unit_one, inverse_one = unit_of(tokens.astype(F32))
    grad_low_one = own_rows(grad_one, row_count).astype(F32) + one_other.astype(F32)
    grad_tokens = (
        own_rows(grad_residual, row_count)
        + norm_back(grad_low_one, gain_one, unit_one, inverse_one)
    ).astype(BF16)

    def share_b_part(part):
        tail = 3 * whole_units + part * spare
        main = share_b[:, part * whole_units : (part + 1) * whole_units]
        return jnp.concatenate([main, share_b[:, tail : tail + spare]], axis=1)

    share_gains = share_a[:, 4 * width : 4 * width + 2] + share_a[:, 4 * width + 2 : 4 * width + 4]
    share_gain_one = share_gains[:, 0]
    share_gain_one = share_gain_one + pair_swap(share_gain_one)
    return (
        output,
        grad_tokens,
        share_gain_one,
        share_a[:, : 3 * width].reshape(depth, 3, width),
        share_a[:, 3 * width : 4 * width].T,
        share_gains[:, 1],
        jnp.stack([share_b_part(0), share_b_part(1)], axis=1),
        share_b_part(2).T,
    )


def solution(mesh):
    return jax.shard_map(
        local,
        mesh=mesh,
        in_specs=(
            P((SEQ, PAIR), None),
            P(SEQ),
            P(SEQ, None, PAIR),
            P(PAIR, SEQ),
            P(SEQ),
            P(SEQ, None, PAIR),
            P(PAIR, SEQ),
            P((SEQ, PAIR), None),
        ),
        out_specs=(
            P((SEQ, PAIR), None),
            P((SEQ, PAIR), None),
            P(SEQ),
            P(SEQ, None, PAIR),
            P(PAIR, SEQ),
            P(SEQ),
            P(SEQ, None, PAIR),
            P(PAIR, SEQ),
        ),
        check_vma=False,
    )
```

```python
import functools
import math

import jax
import jax.numpy as jnp
import numpy as np
from jax import lax
from jax.experimental import pallas as pl
from jax.experimental.pallas import tpu as pltpu
from jax.sharding import PartitionSpec as P

HD = 64
HALF = 64
LANES = 128
COST = 1

EPSILON = 1e-05
THETA = 10000.0
SEQ = "seq"
PAIR = "fsdp"
F32 = jnp.float32
BF16 = jnp.bfloat16


def passed_along(block, axis, distance):
    devices = range(lax.axis_size(axis))
    route = [(i - distance, i) for i in devices if i - distance in devices]
    return lax.ppermute(block, axis, route)


def pair_swap(block):
    return lax.ppermute(block, PAIR, [(0, 1), (1, 0)])


class Ring:
    def __init__(self, width):
        size = lax.axis_size(SEQ)
        self.chips = size // 2
        rows = self.chips // 2
        order = [2 * z for z in range(rows)] + [2 * z + 1 for z in reversed(range(rows))]
        place = np.argsort(np.array(order))
        self.up, self.down = [], []
        for i in range(size):
            chip, core = divmod(i, 2)
            self.up.append((i, order[(place[chip] + 1) % self.chips] * 2 + core))
            self.down.append((i, order[(place[chip] - 1) % self.chips] * 2 + core))
        self.swap = [(i, i ^ 1) for i in range(size)]
        me = lax.axis_index(SEQ)
        self.core = me % 2
        self.place = jnp.asarray(place, jnp.int32)[me // 2]
        self.order = jnp.asarray(order, jnp.int32)
        self.half = self.chips // 2
        self.slots = [self.half]
        for step in range(1, self.half):
            self.slots += [self.half + step, self.half - step]
        self.slots.append(0)
        self.short = width == LANES * self.chips

    def chips_at(self, distances):
        steps = jnp.asarray(distances, jnp.int32)
        return self.order[(self.place + steps + self.chips) % self.chips]

    def go(self, block, route, name):
        with jax.named_scope(name):
            return lax.ppermute(block, SEQ, route)

    def gather(self, block, name, plan):
        if not self.short:
            whole = lax.all_gather(block, SEQ, axis=0, tiled=True)
            return [whole], jnp.zeros(1, jnp.int32)
        rows = block.shape[0]
        middle = rows // 2
        upward = downward = block
        order = [0]
        for step in range(1, self.half + 1):
            order += [-step, step]
        places = [(d, 0, middle if d == self.half else 0) for d in order]
        places += [(d, 1, offset) for d, _, offset in places]
        distances, others, offsets = np.array(places, np.int32).T
        cores = self.chips_at(distances) * 2 + jnp.where(others == 1, 1 - self.core, self.core)
        starts = cores * rows + offsets
        held = {0: (block, 0)}
        swapped = {}
        for step in range(1, self.half + 1):
            if step == self.half:
                upward, downward = upward[:middle], downward[middle:]
            upward = self.go(upward, self.up, f"{name}_up_{step}")
            downward = self.go(downward, self.down, f"{name}_down_{step}")
            meanwhile = [d for d in plan[step - 1] if d in held]
            came = [self.go(held[d][0], self.swap, f"{name}_cores_{d}") for d in meanwhile]
            upward, downward, starts, *came = yield upward, downward, starts, *came
            swapped.update(zip(meanwhile, came))
            held[-step] = upward, 0
            held[step] = downward, middle if step == self.half else 0
        for d in held:
            if d not in swapped:
                swapped[d] = self.go(held[d][0], self.swap, f"{name}_cores_{d}")
        pieces = [held[d][0] for d in held] + [swapped[d] for d in held]
        return pieces, starts

    def scatter_sum(self, early, rest, name):
        kept_early, away_early = early
        kept_rest, away_rest = rest
        count, rows = kept_early.shape[:2]
        middle = rows // 2
        came_early = self.go(away_early, self.swap, f"{name}_cores_early")
        came_rest = self.go(away_rest, self.swap, f"{name}_cores_rest")

        def at(slot):
            i = self.slots.index(slot)
            if i < count:
                return kept_early[i].astype(F32) + came_early[i].astype(F32)
            return kept_rest[i - count].astype(F32) + came_rest[i - count].astype(F32)

        far = at(self.half).astype(BF16)
        upward, downward = far[:middle], far[middle:]
        for step in range(1, self.half + 1):
            upward, downward = yield upward, downward
            upward = self.go(upward, self.up, f"{name}_up_{step}")
            downward = self.go(downward, self.down, f"{name}_down_{step}")
            upward, downward = yield upward, downward
            upward, downward = upward.astype(F32), downward.astype(F32)
            if step == 1:
                upward = jnp.pad(upward, ((0, rows - middle), (0, 0)))
                downward = jnp.pad(downward, ((middle, 0), (0, 0)))
            if step < self.half:
                upward = (at(self.half - step) + upward).astype(BF16)
                downward = (at(self.half + step) + downward).astype(BF16)
        return at(0) + upward + downward


class Stepped:
    def __init__(self, steps):
        self.steps, self.state, self.result = steps, None, None
        self.advance()

    def advance(self):
        try:
            if self.state is not None:
                self.state = lax.optimization_barrier(self.state)
            self.state = self.steps.send(self.state)
        except StopIteration as end:
            self.steps, self.state, self.result = None, None, end.value

    def ride(self, value):
        if self.steps is not None:
            value, self.state = lax.optimization_barrier((value, self.state))
            self.advance()
        return value

    def hold(self, value):
        if self.steps is not None:
            value, self.state = lax.optimization_barrier((value, self.state))
        return value

    def step(self):
        if self.steps is not None:
            self.advance()

    def beside(self, other):
        if self.steps is not None and other.steps is not None:
            self.state, other.state = lax.optimization_barrier((self.state, other.state))
            self.advance()
            other.advance()

    def finish(self):
        while self.steps is not None:
            self.advance()
        return self.result


VMEM = pl.BlockSpec(memory_space=pltpu.VMEM)
ANY = pl.BlockSpec(memory_space=pltpu.HBM)
SMEM = pl.BlockSpec(memory_space=pltpu.SMEM)
MIB = 1024 * 1024


def shape_of(rows, columns, kind):
    return jax.ShapeDtypeStruct((rows, columns), kind)


def call(kernel, args, specs, outs, scratch=(), flops=0, moved=0, room=20):
    return pl.pallas_call(
        kernel,
        in_specs=specs,
        out_specs=[VMEM] * len(outs),
        out_shape=outs,
        scratch_shapes=list(scratch),
        compiler_params=pltpu.CompilerParams(vmem_limit_bytes=room * MIB),
        cost_estimate=pl.CostEstimate(
            flops=flops // COST, bytes_accessed=moved // COST, transcendentals=0
        ),
    )(*args)


def placing(starts, pieces, whole, ready):
    copies = []
    for i, piece in enumerate(pieces):
        rows = piece.shape[0]
        start = pl.multiple_of(starts[i], rows)
        copies.append(
            pltpu.make_async_copy(piece, whole.at[pl.ds(start, rows), :], ready.at[i])
        )
    return copies


def lane_of(rows, width):
    return lax.broadcasted_iota(jnp.int32, (rows, width), 1)


def halves_swapped(values):
    width = values.shape[1]
    lane = lane_of(*values.shape)
    ahead = pltpu.roll(values, width - HD // 2, 1)
    behind = pltpu.roll(values, HD // 2, 1)
    return jnp.where(lane % HD < HD // 2, ahead, behind)


def turned_by(values, cosine, sine):
    copies = values.shape[1] // LANES
    cosine = jnp.concatenate([cosine] * copies, axis=1)
    sine = jnp.concatenate([sine] * copies, axis=1)
    return values * cosine + halves_swapped(values) * sine


def unit_of(values):
    average = jnp.mean(values, axis=-1, keepdims=True)
    centered = values - average
    inverse = lax.rsqrt(jnp.mean(centered * centered, axis=-1, keepdims=True) + EPSILON)
    return centered * inverse, inverse


def first_kernel(count, width, starts, seq, tokens, before, after, cosine, sine, *refs):
    pieces = refs[:count]
    whole, matrix, gains, work, queries, keys_values, wide_cosine, wide_sine = refs[count:-4]
    context, term = refs[-4:-2]
    all_rows, ready = refs[-2:]
    copies = placing(starts, pieces, whole, ready)
    for copy in copies:
        copy.start()
    joined_rows(before, tokens, after, all_rows)
    wide_cosine[...] = jnp.concatenate([cosine[...]] * 4, axis=1)
    wide_sine[...] = jnp.concatenate([-sine[...], sine[...]] * 2, axis=1)
    unit, _ = unit_of(all_rows[...].astype(F32))
    for copy in copies:
        copy.wait()
    matrix[...] = whole[:, 3 * width : 4 * width]
    gains[...] = whole[:, 4 * width :].astype(F32).T[:8]
    all_rows[...] = (unit * gains[0:1, :]).astype(BF16)
    rows = work.shape[0]
    own = slice(HALF, HALF + rows)
    work[...] = all_rows[own, :]
    for start in range(0, 3 * width, 256):
        columns = whole[:, start : start + 256]
        if start < width:
            part = dot(work[...], columns)
            queries[:, start : start + 256] = turned_by(part, wide_cosine[own], wide_sine[own]).astype(BF16)
        else:
            part = dot(all_rows[...], columns)
            if start < 2 * width:
                part = turned_by(part, wide_cosine[...], wide_sine[...])
            keys_values[:, start - width : start - width + 256] = part.astype(BF16)
    attend(seq, queries, keys_values, matrix, context, term)


def window(seq, tile, tiles):
    row = lax.broadcasted_iota(jnp.int32, (2 * LANES, 2 * LANES), 0) % LANES
    column = lax.broadcasted_iota(jnp.int32, (2 * LANES, 2 * LANES), 1)
    ahead = column - row
    inside = (ahead >= 0) & (ahead <= 2 * HALF)
    if tile == 0:
        inside &= (seq[0] > 0) | (column >= HALF)
    if tile == tiles - 1:
        inside &= (seq[0] < seq[1] - 1) | (column < 2 * LANES - HALF)
    return inside


def heads_apart(pair):
    lane = lane_of(*pair.shape)
    zero = jnp.zeros_like(pair)
    return jnp.concatenate(
        [jnp.where(lane < HD, pair, zero), jnp.where(lane < HD, zero, pair)], axis=0
    )


def heads_joined(apart):
    rows = apart.shape[0] // 2
    return jnp.where(lane_of(rows, apart.shape[1]) < HD, apart[:rows], apart[rows:])


def shares_of(apart, keys, inside):
    scores = dot(apart, keys, (1, 1)) * (1.0 / math.sqrt(HD))
    scores = jnp.where(inside, scores, -1e30)
    expo = jnp.exp(scores - jnp.max(scores, axis=-1, keepdims=True))
    return expo / jnp.sum(expo, axis=-1, keepdims=True)


def joined_rows(before, own, after, whole):
    rows = own.shape[0]
    whole[:HALF] = before[...]
    whole[HALF : HALF + rows] = own[...]
    whole[HALF + rows :] = after[...]


def attend(seq, queries, keys_values, matrix, context, term):
    rows, width = queries.shape
    tiles = rows // LANES
    for tile in range(tiles):
        inside = window(seq, tile, tiles)
        at = slice(tile * LANES, tile * LANES + LANES)
        reach = slice(tile * LANES, tile * LANES + 2 * LANES)
        for start in range(0, width, LANES):
            columns = slice(start, start + LANES)
            apart = heads_apart(queries[at, columns])
            shares = shares_of(apart, keys_values[reach, columns], inside)
            values = keys_values[reach, width + start : width + start + LANES]
            context[at, columns] = heads_joined(dot(shares.astype(BF16), values)).astype(BF16)
    term[...] = dot(context[...], matrix[...], (1, 1)).astype(BF16)


def hidden_kernel(count, spare, early, starts, chips, core, tokens, term, term_other, gains, cot, *refs):
    pieces = refs[:count]
    residual, work, hidden, grad_proj, grad_two, down, *terms, whole, ready = refs[count:]
    copies = placing(starts, pieces, whole, ready)
    for copy in copies:
        copy.start()
    added = term[...].astype(F32) + term_other[...].astype(F32)
    residual[...] = tokens[...].astype(F32) + added
    unit, _ = unit_of(residual[...])
    work[...] = (unit * gains[1:2, :]).astype(BF16)
    for copy in copies:
        copy.wait()
    units = hidden.shape[1] - LANES

    def grads(gate, up, back):
        share = 0.5 + 0.5 * lax.erf(gate * (1.0 / math.sqrt(2.0)))
        bell = jnp.exp(-0.5 * gate * gate) * (1.0 / math.sqrt(2.0 * math.pi))
        gelu = gate * share
        return gelu * up, back * up * (share + gate * bell), back * gelu

    for start in range(0, units, 256):
        stop = min(units, start + 256)
        gate = dot(work[...], whole[:, start:stop])
        up = dot(work[...], whole[:, units + start : units + stop])
        back = dot(cot[...], whole[:, 2 * units + start : 2 * units + stop])
        here, grad_gate, grad_up = grads(gate, up, back)
        hidden[:, start:stop] = here.astype(BF16)
        grad_proj[:, start:stop] = grad_gate.astype(BF16)
        grad_proj[:, units + start : units + stop] = grad_up.astype(BF16)
    tail = whole[:, 3 * units :]
    both = dot(work[...], tail)
    back = pltpu.roll(dot(cot[...], tail), LANES - 2 * spare, 1)
    parts = grads(both, pltpu.roll(both, LANES - spare, 1), back)
    lane = lane_of(*both.shape)
    here, grad_gate, grad_up = [jnp.where(lane < spare, part, 0.0) for part in parts]
    hidden[:, units:] = pltpu.roll(here, 2 * spare, 1).astype(BF16)
    grad_proj[:, 2 * units :] = (grad_gate + pltpu.roll(grad_up, spare, 1)).astype(BF16)
    grad_two[...] = (
        dot(grad_proj[:, : 2 * units], whole[:, : 2 * units], (1, 1))
        + dot(grad_proj[:, 2 * units :], tail, (1, 1))
    ).astype(BF16)
    down[...] = dot(hidden[...], whole[:, 2 * units :], (1, 1)).astype(BF16)
    if early:
        early_rows(early, chips, core, LANES, [(work, grad_proj), (cot, hidden)], None, *terms)


def attend_back_kernel(
    seq, residual, gains, grad_two, grad_two_other, cot, matrix, queries, keys_values,
    cosine, sine, grad_residual, grad_low, gain_two, grad_queries, grad_own, to_before, to_after,
    grad_all,
):
    rows, width = queries.shape
    unit, inverse = unit_of(residual[...])
    grad = grad_two[...].astype(F32) + grad_two_other[...].astype(F32)
    gain_two[...] = jnp.broadcast_to(jnp.sum(grad * unit, axis=0, keepdims=True), gain_two.shape)
    scaled = grad * gains[1:2, :]
    middle = jnp.mean(scaled, axis=-1, keepdims=True)
    along = jnp.mean(scaled * unit, axis=-1, keepdims=True)
    total = cot[...].astype(F32) + inverse * (scaled - middle - unit * along)
    grad_residual[...] = total
    grad_low[...] = total.astype(BF16)
    grad_context = dot(grad_low[...], matrix[...]).astype(BF16)
    grad_all[...] = jnp.zeros_like(grad_all)
    scale = 1.0 / math.sqrt(HD)
    tiles = rows // LANES
    for tile in range(tiles):
        inside = window(seq, tile, tiles)
        at = slice(tile * LANES, tile * LANES + LANES)
        own_at = slice(HALF + tile * LANES, HALF + tile * LANES + LANES)
        reach = slice(tile * LANES, tile * LANES + 2 * LANES)
        for start in range(0, width, LANES):
            columns = slice(start, start + LANES)
            beside = slice(width + start, width + start + LANES)
            apart = heads_apart(queries[at, columns])
            keys = keys_values[reach, columns]
            shares = shares_of(apart, keys, inside)
            grad_apart = heads_apart(grad_context[at, columns])
            grad_shares = dot(grad_apart, keys_values[reach, beside], (1, 1))
            lost = jnp.sum(grad_shares * shares, axis=-1, keepdims=True)
            grad_scores = (shares * (grad_shares - lost)).astype(BF16)
            grad_here = heads_joined(dot(grad_scores, keys)) * scale
            grad_queries[at, columns] = turned_by(grad_here, cosine[own_at], -sine[own_at]).astype(BF16)
            grad_all[reach, columns] += dot(grad_scores, apart, (0, 0)) * scale
            grad_all[reach, beside] += dot(shares.astype(BF16), grad_apart, (0, 0))
    to_before[...] = grad_all[:HALF].astype(BF16)
    grad_own[...] = grad_all[HALF : HALF + rows]
    to_after[...] = grad_all[HALF + rows :].astype(BF16)


def last_kernel(
    early, chips, core, grad_queries, grad_own, from_before, from_after, cosine, sine, tokens,
    gain_two, work, grad_low, context, matrix_whole, grad_qkv, grad_one, gain_columns, *refs,
):
    *parts, grad_all, matrix, ready = refs
    rows, width = grad_queries.shape
    fetch = pltpu.make_async_copy(matrix_whole.at[:, : 3 * width], matrix, ready)
    fetch.start()
    grad_all[...] = grad_own[...]
    grad_all[:HALF] += from_before[...].astype(F32)
    grad_all[rows - HALF :] += from_after[...].astype(F32)
    grad_qkv[:, :width] = grad_queries[...]
    own = slice(HALF, HALF + rows)
    grad_keys = turned_by(grad_all[:, :width], cosine[own], -sine[own])
    grad_qkv[:, width : 2 * width] = grad_keys.astype(BF16)
    grad_qkv[:, 2 * width :] = grad_all[:, width:].astype(BF16)
    fetch.wait()
    grad = dot(grad_qkv[...], matrix[...], (1, 1))
    grad_one[...] = grad.astype(BF16)
    unit, _ = unit_of(tokens[...].astype(F32))
    gain_one = jnp.sum(grad * unit, axis=0, keepdims=True)
    gain = jnp.concatenate([gain_one, gain_two[0:1, :]], axis=0)
    high = gain.astype(BF16).astype(F32)
    spare = jnp.zeros((LANES - 4, gain.shape[1]), F32)
    gain_columns[...] = jnp.concatenate([high, gain - high, spare], axis=0).T.astype(BF16)
    if early:
        pairs = [(work, grad_qkv), (grad_low, context)]
        early_rows(early, chips, core, 0, pairs, gain_columns, *parts)


def weight_rows(i, tail, lower, pairs, extra, kept, away):
    depth = kept.shape[1]

    def put(block, start, stop):
        kept[i, :, start:stop] = jnp.where(lower, block[:depth], block[depth:]).astype(BF16)
        away[i, :, start:stop] = jnp.where(lower, block[depth:], block[:depth]).astype(BF16)

    base = 0
    rest = 0.0
    for left, right in pairs:
        width = right.shape[1] - tail
        turned = left.T
        for start in range(0, width, 512):
            stop = min(width, start + 512)
            product = jnp.dot(turned, right[:, start:stop], preferred_element_type=F32)
            put(product, base + start, base + stop)
        base += width
        if tail:
            rest += jnp.dot(turned, right[:, width:], preferred_element_type=F32)
    if tail:
        put(rest, base, base + tail)
    if extra is not None:
        put(extra.astype(F32), base, base + extra.shape[1])


def early_rows(count, chips, core, tail, pairs, extra, kept, away):
    lower = core[0] == 0
    for i in range(count):
        lanes = pl.ds(pl.multiple_of(chips[i] * LANES, LANES), LANES)
        blocks = [(left[:, lanes], right) for left, right in pairs]
        more = None if extra is None else extra[lanes, :]
        weight_rows(i, tail, lower, blocks, more, kept, away)


def weight_kernel(tail, chips, core, left_one, left_two, right_one, right_two, *refs):
    pairs = [(left_one[...], right_one), (left_two[...], right_two)]
    extra = refs[0][...] if len(refs) == 3 else None
    weight_rows(0, tail, core[0] == 0, pairs, extra, *refs[-2:])


def weight_terms(ring, chips, core, skip, left_one, right_one, left_two, right_two, extra=None, tail=0, room=20):
    work_rows, width = left_one.shape
    lanes = width // ring.chips
    depth = lanes // 2
    total = right_one.shape[1] + right_two.shape[1] - tail
    more_args, more_specs = [], []
    if extra is not None:
        total += extra.shape[1]
        more_args.append(extra)
        more_specs.append(
            pl.BlockSpec((lanes, extra.shape[1]), lambda i, chips, core: (chips[i + skip], 0))
        )

    count = ring.chips - skip

    def left_map(i, chips, core):
        return (0, chips[i + skip])

    def whole_map(i, chips, core):
        return (0, 0)

    return pl.pallas_call(
        functools.partial(weight_kernel, tail),
        grid_spec=pltpu.PrefetchScalarGridSpec(
            num_scalar_prefetch=2,
            grid=(count,),
            in_specs=[
                pl.BlockSpec((work_rows, lanes), left_map),
                pl.BlockSpec((work_rows, lanes), left_map),
                pl.BlockSpec(right_one.shape, whole_map),
                pl.BlockSpec(right_two.shape, whole_map),
                *more_specs,
            ],
            out_specs=[
                pl.BlockSpec((1, depth, total), lambda i, chips, core: (i, 0, 0)),
                pl.BlockSpec((1, depth, total), lambda i, chips, core: (i, 0, 0)),
            ],
        ),
        out_shape=[
            pltpu.HBM((count, depth, total), BF16),
            pltpu.HBM((count, depth, total), BF16),
        ],
        compiler_params=pltpu.CompilerParams(vmem_limit_bytes=room * MIB),
        cost_estimate=pl.CostEstimate(
            flops=2 * work_rows * lanes * count * total // COST,
            bytes_accessed=2 * (lanes * count + work_rows) * total // COST,
            transcendentals=0,
        ),
    )(
        chips,
        core,
        left_one,
        left_two,
        right_one,
        right_two,
        *more_args,
    )


def summed_terms(left_one, right_one, left_two, right_two, extra=None, tail=0):
    yield from ()
    terms = [dot(left_one, right_one, (0, 0)), dot(left_two, right_two, (0, 0))]
    if tail:
        rest = terms[0][:, -tail:] + terms[1][:, -tail:]
        terms = [terms[0][:, :-tail], terms[1][:, :-tail], rest]
    terms = [t.astype(BF16) for t in terms] + ([] if extra is None else [extra])
    terms = jnp.concatenate(terms, axis=1)
    return lax.psum_scatter(terms, SEQ, scatter_dimension=0, tiled=True).astype(F32)


def norm_back(grad_rows, gain, unit_rows, inverse):
    scaled = grad_rows * gain
    centered_grad = (
        scaled
        - jnp.mean(scaled, axis=-1, keepdims=True)
        - unit_rows * jnp.mean(scaled * unit_rows, axis=-1, keepdims=True)
    )
    return inverse * centered_grad


def rotary_tables(positions):
    half_size = HD // 2
    frequency = THETA ** (-(jnp.arange(half_size, dtype=F32) * 2.0) / HD)
    angles = positions.astype(F32)[:, None] * frequency[None, :]
    return jnp.cos(angles), jnp.sin(angles)


def edge_rows(block):
    blocks = range(lax.axis_size(SEQ))
    route = [(2 * i, 2 * i - 2) for i in blocks if i > 0]
    route += [(2 * i + 1, 2 * i + 3) for i in blocks if i + 1 in blocks]
    return lax.ppermute(block, (SEQ, PAIR), route)


def pair_rows(mine, other):
    first = lax.axis_index(PAIR) == 0
    return jnp.concatenate([jnp.where(first, mine, other), jnp.where(first, other, mine)], axis=0)


def own_rows(values, row_count):
    return lax.dynamic_slice_in_dim(values, lax.axis_index(PAIR) * row_count, row_count, 0)


def other_rows(values, row_count):
    return lax.dynamic_slice_in_dim(values, (1 - lax.axis_index(PAIR)) * row_count, row_count, 0)


def dot(a, b, over=(1, 0)):
    return lax.dot_general(a, b, (((over[0],), (over[1],)), ((), ())), preferred_element_type=F32)


def padded_to_lanes(values):
    return jnp.pad(values, ((0, 0), (0, -values.shape[1] % LANES)))


def local(tokens, norm1_gain, w_qkv, w_attn_out, norm2_gain, w_in, w_down, cotangent):
    row_count, model_width = tokens.shape
    ring = Ring(model_width)
    early = 3 if ring.short else 0
    chips, core = ring.chips_at(ring.slots), ring.core.reshape(1)
    depth, _, width = w_qkv.shape
    units = w_down.shape[0]
    gains = padded_to_lanes(jnp.stack([norm1_gain, norm2_gain], axis=1))
    blob_a = jnp.concatenate([w_qkv.reshape(depth, -1), w_attn_out.T, gains], axis=1)
    whole_units = units // LANES * LANES
    spare = units - whole_units
    parts = [w_in[:, 0], w_in[:, 1], w_down.T]
    blob_b = jnp.concatenate(
        [part[:, :whole_units] for part in parts] + [part[:, whole_units:] for part in parts], axis=1
    )
    blob_b = jnp.pad(blob_b, ((0, 0), (0, LANES - 3 * spare)))
    steps_a = Stepped(ring.gather(blob_a, "gather_a", [[0], [-1, 1], [], [-2]]))
    first = lax.axis_index(PAIR) == 0
    edge = edge_rows(jnp.where(first, tokens[:HALF], tokens[-HALF:]))
    edge = steps_a.hold(edge)
    joined = jnp.concatenate([tokens, edge, cotangent], axis=0)
    other = pair_swap(joined)
    steps_a.step()
    blob_b = steps_a.ride(blob_b)
    steps_b = Stepped(ring.gather(blob_b, "gather_b", [[], [], [0, -1, 1], [-2, 2]]))
    other = steps_a.hold(other)
    tokens_all = pair_rows(tokens, other[:row_count])
    beside = other[row_count : row_count + HALF]
    tokens_before = jnp.where(first, beside, edge)
    tokens_after = jnp.where(first, edge, beside)
    cot_all = pair_rows(cotangent, other[row_count + HALF :])

    work_rows = row_count * lax.axis_size(PAIR)
    reach_rows = work_rows + 2 * HALF
    seq = jnp.stack([lax.axis_index(SEQ), lax.axis_size(SEQ)]).astype(jnp.int32)
    cosine, sine = rotary_tables(
        seq[0] * work_rows - HALF + jnp.arange(reach_rows, dtype=jnp.int32)
    )
    inputs = tokens_all, tokens_before, tokens_after, cot_all, seq, cosine, sine, chips, core
    inputs = steps_a.hold(inputs)
    tokens_all, tokens_before, tokens_after, cot_all, seq, cosine, sine, chips, core = inputs
    steps_a.step()
    steps_a.beside(steps_b)
    pieces, starts = steps_a.finish()
    count = len(pieces)
    whole_a, attn_matrix, gains, work_one, queries, keys_values, *later = call(
        functools.partial(first_kernel, count, width),
        (starts, seq, tokens_all, tokens_before, tokens_after, cosine, sine, *pieces),
        [SMEM] * 2 + [VMEM] * 5 + [ANY] * count,
        [
            shape_of(model_width, blob_a.shape[1], BF16),
            shape_of(model_width, width, BF16),
            shape_of(8, model_width, F32),
            shape_of(work_rows, model_width, BF16),
            shape_of(work_rows, width, BF16),
            shape_of(reach_rows, 2 * width, BF16),
            shape_of(reach_rows, LANES, F32),
            shape_of(reach_rows, LANES, F32),
            shape_of(work_rows, width, BF16),
            shape_of(work_rows, model_width, BF16),
        ],
        [pltpu.VMEM((reach_rows, model_width), BF16), pltpu.SemaphoreType.DMA((count,))],
        flops=6 * work_rows * model_width * width,
        moved=16 * MIB,
        room=60,
    )
    cosine, sine, context, attn_term = later
    attn_term = steps_b.ride(attn_term)
    attn_other = steps_b.ride(pair_swap(attn_term))

    pieces, starts = steps_b.finish()
    count = len(pieces)
    residual, work_two, hidden, grad_proj, grad_two, down_term, *early_b = call(
        functools.partial(hidden_kernel, count, spare, early),
        (starts, chips, core, tokens_all, attn_term, attn_other, gains, cot_all, *pieces),
        [SMEM] * 3 + [VMEM] * 5 + [ANY] * count,
        [
            shape_of(work_rows, model_width, F32),
            shape_of(work_rows, model_width, BF16),
            shape_of(work_rows, whole_units + LANES, BF16),
            shape_of(work_rows, 2 * whole_units + LANES, BF16),
            shape_of(work_rows, model_width, BF16),
            shape_of(work_rows, model_width, BF16),
        ]
        + [pltpu.HBM((early, depth, blob_b.shape[1]), BF16)] * (2 if early else 0),
        [
            pltpu.VMEM((model_width, blob_b.shape[1]), BF16),
            pltpu.SemaphoreType.DMA((count,)),
        ],
        flops=12 * work_rows * model_width * units,
        moved=32 * MIB,
        room=60,
    )
    grad_two_other = pair_swap(grad_two)
    factors = work_two, grad_proj, cot_all, hidden
    if early:
        rest_b = weight_terms(ring, chips, core, early, *factors, tail=LANES, room=60)
        steps_b = Stepped(ring.scatter_sum(early_b, rest_b, "sum_b"))
    else:
        rest_b = ()
        steps_b = Stepped(summed_terms(*factors, tail=LANES))
    grad_two, rest_b = steps_b.ride((grad_two, rest_b))
    grad_residual, grad_low, gain_two, grad_queries, grad_own, to_before, to_after = call(
        attend_back_kernel,
        (
            seq, residual, gains, grad_two, grad_two_other, cot_all, attn_matrix,
            queries, keys_values, cosine, sine,
        ),
        [SMEM] + [VMEM] * 10,
        [
            pltpu.HBM((work_rows, model_width), F32),
            pltpu.HBM((work_rows, model_width), BF16),
            shape_of(8, model_width, F32),
            shape_of(work_rows, width, BF16),
            shape_of(work_rows, 2 * width, F32),
            pltpu.HBM((HALF, 2 * width), BF16),
            pltpu.HBM((HALF, 2 * width), BF16),
        ],
        [pltpu.VMEM((reach_rows, 2 * width), F32)],
        flops=4 * work_rows * model_width * width,
        moved=24 * MIB,
    )
    to_before, to_after = steps_b.ride((to_before, to_after))
    from_next = passed_along(to_before, SEQ, -1)
    from_prev = passed_along(to_after, SEQ, 1)

    down_other = pair_swap(other_rows(down_term, row_count))
    from_prev, from_next = steps_b.ride((from_prev, from_next))
    last = call(
        functools.partial(last_kernel, early),
        (
            chips, core, grad_queries, grad_own, from_prev, from_next, cosine, sine, tokens_all,
            gain_two, work_one, grad_low, context, whole_a,
        ),
        [SMEM] * 2 + [VMEM] * 11 + [ANY],
        [
            shape_of(work_rows, 3 * width, BF16),
            shape_of(work_rows, model_width, BF16),
            shape_of(model_width, LANES, BF16),
        ]
        + [pltpu.HBM((early, depth, blob_a.shape[1]), BF16)] * (2 if early else 0),
        [
            pltpu.VMEM((work_rows, 2 * width), F32),
            pltpu.VMEM((model_width, 3 * width), BF16),
            pltpu.SemaphoreType.DMA,
        ],
        flops=6 * work_rows * model_width * width,
        moved=16 * MIB,
        room=60,
    )
    last, down_other = steps_b.ride((tuple(last), down_other))
    grad_qkv, grad_one, gain_columns, *early_a = last
    one_other = pair_swap(other_rows(grad_one, row_count))
    grad_qkv = steps_b.ride(grad_qkv)
    factors = work_one, grad_qkv, grad_low, context, gain_columns
    if early:
        rest_a = weight_terms(ring, chips, core, early, *factors)
        steps_a = Stepped(ring.scatter_sum(early_a, rest_a, "sum_a"))
    else:
        steps_a = Stepped(summed_terms(*factors))
    steps_a.step()
    steps_a.beside(steps_b)
    steps_b.step()
    steps_a.step()
    one_other = steps_a.hold(one_other)
    steps_a.step()
    steps_a.step()
    steps_a.step()
    steps_a.beside(steps_b)
    share_b = steps_b.finish()
    share_a = steps_a.finish()

    output = (
        own_rows(residual, row_count)
        + (own_rows(down_term, row_count).astype(F32) + down_other.astype(F32))
    ).astype(BF16)

    gain_one = gains[0:1]
    unit_one, inverse_one = unit_of(tokens.astype(F32))
    grad_low_one = own_rows(grad_one, row_count).astype(F32) + one_other.astype(F32)
    grad_tokens = (
        own_rows(grad_residual, row_count)
        + norm_back(grad_low_one, gain_one, unit_one, inverse_one)
    ).astype(BF16)

    def share_b_part(part):
        tail = 3 * whole_units + part * spare
        main = share_b[:, part * whole_units : (part + 1) * whole_units]
        return jnp.concatenate([main, share_b[:, tail : tail + spare]], axis=1)

    share_gains = share_a[:, 4 * width : 4 * width + 2] + share_a[:, 4 * width + 2 : 4 * width + 4]
    share_gain_one = share_gains[:, 0]
    share_gain_one = share_gain_one + pair_swap(share_gain_one)
    return (
        output,
        grad_tokens,
        share_gain_one,
        share_a[:, : 3 * width].reshape(depth, 3, width),
        share_a[:, 3 * width : 4 * width].T,
        share_gains[:, 1],
        jnp.stack([share_b_part(0), share_b_part(1)], axis=1),
        share_b_part(2).T,
    )


def solution(mesh):
    return jax.shard_map(
        local,
        mesh=mesh,
        in_specs=(
            P((SEQ, PAIR), None),
            P(SEQ),
            P(SEQ, None, PAIR),
            P(PAIR, SEQ),
            P(SEQ),
            P(SEQ, None, PAIR),
            P(PAIR, SEQ),
            P((SEQ, PAIR), None),
        ),
        out_specs=(
            P((SEQ, PAIR), None),
            P((SEQ, PAIR), None),
            P(SEQ),
            P(SEQ, None, PAIR),
            P(PAIR, SEQ),
            P(SEQ),
            P(SEQ, None, PAIR),
            P(PAIR, SEQ),
        ),
        check_vma=False,
    )
```

```python
import functools
import math

import jax
import jax.numpy as jnp
import numpy as np
from jax import lax
from jax.experimental import pallas as pl
from jax.experimental.pallas import tpu as pltpu
from jax.sharding import PartitionSpec as P

HD = 64
HALF = 64
LANES = 128
COST = 1

EPSILON = 1e-05
THETA = 10000.0
SEQ = "seq"
PAIR = "fsdp"
F32 = jnp.float32
BF16 = jnp.bfloat16


def passed_along(block, axis, distance):
    devices = range(lax.axis_size(axis))
    route = [(i - distance, i) for i in devices if i - distance in devices]
    return lax.ppermute(block, axis, route)


def pair_swap(block):
    return lax.ppermute(block, PAIR, [(0, 1), (1, 0)])


class Ring:
    def __init__(self, width):
        size = lax.axis_size(SEQ)
        self.chips = size // 2
        rows = self.chips // 2
        order = [2 * z for z in range(rows)] + [2 * z + 1 for z in reversed(range(rows))]
        place = np.argsort(np.array(order))
        self.up, self.down = [], []
        for i in range(size):
            chip, core = divmod(i, 2)
            self.up.append((i, order[(place[chip] + 1) % self.chips] * 2 + core))
            self.down.append((i, order[(place[chip] - 1) % self.chips] * 2 + core))
        self.swap = [(i, i ^ 1) for i in range(size)]
        me = lax.axis_index(SEQ)
        self.core = me % 2
        self.place = jnp.asarray(place, jnp.int32)[me // 2]
        self.order = jnp.asarray(order, jnp.int32)
        self.half = self.chips // 2
        self.own = {}
        self.slots = [self.half]
        for step in range(1, self.half):
            self.slots += [self.half + step, self.half - step]
        self.slots.append(0)
        self.short = width == LANES * self.chips

    def chips_at(self, distances):
        steps = jnp.asarray(distances, jnp.int32)
        return self.order[(self.place + steps + self.chips) % self.chips]

    def go(self, block, route, name):
        with jax.named_scope(name):
            return lax.ppermute(block, SEQ, route)

    def go_across(self, block, route, name):
        both = [(2 * i + side, 2 * j + 1 - side) for i, j in route for side in (0, 1)]
        with jax.named_scope(name):
            return lax.ppermute(block, (SEQ, PAIR), both)

    def gather(self, block, name, plan):
        if not self.short:
            whole = lax.all_gather(block, SEQ, axis=0, tiled=True)
            return [whole], jnp.zeros(1, jnp.int32)
        rows = block.shape[0]
        middle = rows // 2
        upward = downward = block
        order = [0]
        for step in range(1, self.half + 1):
            order += [-step, step]
        places = [(d, 0, middle if d == self.half else 0) for d in order]
        places += [(d, 1, offset) for d, _, offset in places]
        distances, others, offsets = np.array(places, np.int32).T
        cores = self.chips_at(distances) * 2 + jnp.where(others == 1, 1 - self.core, self.core)
        starts = cores * rows + offsets
        held = {0: (block, 0)}
        swapped = {}
        for step in range(1, self.half + 1):
            if step == self.half:
                upward, downward = upward[:middle], downward[middle:]
            upward = self.go(upward, self.up, f"{name}_up_{step}")
            downward = self.go(downward, self.down, f"{name}_down_{step}")
            meanwhile = [d for d in plan[step - 1] if d in held]
            came = [self.go(held[d][0], self.swap, f"{name}_cores_{d}") for d in meanwhile]
            upward, downward, starts, *came = yield upward, downward, starts, *came
            swapped.update(zip(meanwhile, came))
            held[-step] = upward, 0
            held[step] = downward, middle if step == self.half else 0
        for d in held:
            if d not in swapped:
                swapped[d] = self.go(held[d][0], self.swap, f"{name}_cores_{d}")
        pieces = [held[d][0] for d in held] + [swapped[d] for d in held]
        return pieces, starts

    def scatter_sum(self, early, rest, name):
        kept_early, away_early = early
        kept_rest, away_rest = rest
        count, rows = kept_early.shape[:2]
        middle = rows // 2
        came_early = self.go(away_early, self.swap, f"{name}_cores_early")
        came_rest = self.go(away_rest, self.swap, f"{name}_cores_rest")

        def at(slot):
            i = self.slots.index(slot)
            if i < count:
                return kept_early[i].astype(F32) + came_early[i].astype(F32)
            return kept_rest[i - count].astype(F32) + came_rest[i - count].astype(F32)

        far = at(self.half).astype(BF16)
        upward, downward = far[:middle], far[middle:]
        for step in range(1, self.half + 1):
            if step == self.half:
                self.own[name] = at(0)
            upward, downward = yield upward, downward
            upward = self.go(upward, self.up, f"{name}_up_{step}")
            downward = self.go(downward, self.down, f"{name}_down_{step}")
            upward, downward = yield upward, downward
            upward, downward = upward.astype(F32), downward.astype(F32)
            if step == 1:
                upward = jnp.pad(upward, ((0, rows - middle), (0, 0)))
                downward = jnp.pad(downward, ((middle, 0), (0, 0)))
            if step < self.half:
                upward = (at(self.half - step) + upward).astype(BF16)
                downward = (at(self.half + step) + downward).astype(BF16)
        return at(0) + upward + downward


class Stepped:
    def __init__(self, steps):
        self.steps, self.state, self.result = steps, None, None
        self.advance()

    def advance(self):
        try:
            if self.state is not None:
                self.state = lax.optimization_barrier(self.state)
            self.state = self.steps.send(self.state)
        except StopIteration as end:
            self.steps, self.state, self.result = None, None, end.value

    def ride(self, value):
        if self.steps is not None:
            value, self.state = lax.optimization_barrier((value, self.state))
            self.advance()
        return value

    def hold(self, value):
        if self.steps is not None:
            value, self.state = lax.optimization_barrier((value, self.state))
        return value

    def step(self):
        if self.steps is not None:
            self.advance()

    def beside(self, other):
        if self.steps is not None and other.steps is not None:
            self.state, other.state = lax.optimization_barrier((self.state, other.state))
            self.advance()
            other.advance()

    def finish(self):
        while self.steps is not None:
            self.advance()
        return self.result


VMEM = pl.BlockSpec(memory_space=pltpu.VMEM)
ANY = pl.BlockSpec(memory_space=pltpu.HBM)
SMEM = pl.BlockSpec(memory_space=pltpu.SMEM)
MIB = 1024 * 1024


def shape_of(rows, columns, kind):
    return jax.ShapeDtypeStruct((rows, columns), kind)


def call(kernel, args, specs, outs, scratch=(), flops=0, moved=0, room=20):
    return pl.pallas_call(
        kernel,
        in_specs=specs,
        out_specs=[VMEM] * len(outs),
        out_shape=outs,
        scratch_shapes=list(scratch),
        compiler_params=pltpu.CompilerParams(vmem_limit_bytes=room * MIB),
        cost_estimate=pl.CostEstimate(
            flops=flops // COST, bytes_accessed=moved // COST, transcendentals=0
        ),
    )(*args)


def placing(starts, pieces, whole, ready):
    copies = []
    for i, piece in enumerate(pieces):
        rows = piece.shape[0]
        start = pl.multiple_of(starts[i], rows)
        copies.append(
            pltpu.make_async_copy(piece, whole.at[pl.ds(start, rows), :], ready.at[i])
        )
    return copies


def lane_of(rows, width):
    return lax.broadcasted_iota(jnp.int32, (rows, width), 1)


def halves_swapped(values):
    width = values.shape[1]
    lane = lane_of(*values.shape)
    ahead = pltpu.roll(values, width - HD // 2, 1)
    behind = pltpu.roll(values, HD // 2, 1)
    return jnp.where(lane % HD < HD // 2, ahead, behind)


def turned_by(values, cosine, sine):
    copies = values.shape[1] // LANES
    cosine = jnp.concatenate([cosine] * copies, axis=1)
    sine = jnp.concatenate([sine] * copies, axis=1)
    return values * cosine + halves_swapped(values) * sine


def unit_of(values):
    average = jnp.mean(values, axis=-1, keepdims=True)
    centered = values - average
    inverse = lax.rsqrt(jnp.mean(centered * centered, axis=-1, keepdims=True) + EPSILON)
    return centered * inverse, inverse


def first_kernel(count, width, starts, seq, tokens, before, after, cosine, sine, *refs):
    pieces = refs[:count]
    whole, matrix, gains, work, queries, keys_values, wide_cosine, wide_sine = refs[count:-4]
    context, term = refs[-4:-2]
    all_rows, ready = refs[-2:]
    copies = placing(starts, pieces, whole, ready)
    for copy in copies:
        copy.start()
    joined_rows(before, tokens, after, all_rows)
    wide_cosine[...] = jnp.concatenate([cosine[...]] * 4, axis=1)
    wide_sine[...] = jnp.concatenate([-sine[...], sine[...]] * 2, axis=1)
    unit, _ = unit_of(all_rows[...].astype(F32))
    for copy in copies:
        copy.wait()
    matrix[...] = whole[:, 3 * width : 4 * width]
    gains[...] = whole[:, 4 * width :].astype(F32).T[:8]
    all_rows[...] = (unit * gains[0:1, :]).astype(BF16)
    rows = work.shape[0]
    own = slice(HALF, HALF + rows)
    work[...] = all_rows[own, :]
    for start in range(0, 3 * width, 256):
        columns = whole[:, start : start + 256]
        if start < width:
            part = dot(work[...], columns)
            queries[:, start : start + 256] = turned_by(part, wide_cosine[own], wide_sine[own]).astype(BF16)
        else:
            part = dot(all_rows[...], columns)
            if start < 2 * width:
                part = turned_by(part, wide_cosine[...], wide_sine[...])
            keys_values[:, start - width : start - width + 256] = part.astype(BF16)
    attend(seq, queries, keys_values, matrix, context, term)


def window(seq, tile, tiles):
    row = lax.broadcasted_iota(jnp.int32, (2 * LANES, 2 * LANES), 0) % LANES
    column = lax.broadcasted_iota(jnp.int32, (2 * LANES, 2 * LANES), 1)
    ahead = column - row
    inside = (ahead >= 0) & (ahead <= 2 * HALF)
    if tile == 0:
        inside &= (seq[0] > 0) | (column >= HALF)
    if tile == tiles - 1:
        inside &= (seq[0] < seq[1] - 1) | (column < 2 * LANES - HALF)
    return inside


def heads_apart(pair):
    lane = lane_of(*pair.shape)
    zero = jnp.zeros_like(pair)
    return jnp.concatenate(
        [jnp.where(lane < HD, pair, zero), jnp.where(lane < HD, zero, pair)], axis=0
    )


def heads_joined(apart):
    rows = apart.shape[0] // 2
    return jnp.where(lane_of(rows, apart.shape[1]) < HD, apart[:rows], apart[rows:])


def shares_of(apart, keys, inside):
    scores = dot(apart, keys, (1, 1)) * (1.0 / math.sqrt(HD))
    scores = jnp.where(inside, scores, -1e30)
    expo = jnp.exp(scores - jnp.max(scores, axis=-1, keepdims=True))
    return expo / jnp.sum(expo, axis=-1, keepdims=True)


def joined_rows(before, own, after, whole):
    rows = own.shape[0]
    whole[:HALF] = before[...]
    whole[HALF : HALF + rows] = own[...]
    whole[HALF + rows :] = after[...]


def attend(seq, queries, keys_values, matrix, context, term):
    rows, width = queries.shape
    tiles = rows // LANES
    for tile in range(tiles):
        inside = window(seq, tile, tiles)
        at = slice(tile * LANES, tile * LANES + LANES)
        reach = slice(tile * LANES, tile * LANES + 2 * LANES)
        for start in range(0, width, LANES):
            columns = slice(start, start + LANES)
            apart = heads_apart(queries[at, columns])
            shares = shares_of(apart, keys_values[reach, columns], inside)
            values = keys_values[reach, width + start : width + start + LANES]
            context[at, columns] = heads_joined(dot(shares.astype(BF16), values)).astype(BF16)
    term[...] = dot(context[...], matrix[...], (1, 1)).astype(BF16)


def hidden_kernel(count, spare, early, starts, chips, core, tokens, term, term_other, gains, cot, *refs):
    pieces = refs[:count]
    residual, work, hidden, grad_proj, grad_two, down, *terms, whole, ready = refs[count:]
    copies = placing(starts, pieces, whole, ready)
    for copy in copies:
        copy.start()
    added = term[...].astype(F32) + term_other[...].astype(F32)
    residual[...] = tokens[...].astype(F32) + added
    unit, _ = unit_of(residual[...])
    work[...] = (unit * gains[1:2, :]).astype(BF16)
    for copy in copies:
        copy.wait()
    units = hidden.shape[1] - LANES

    def grads(gate, up, back):
        share = 0.5 + 0.5 * lax.erf(gate * (1.0 / math.sqrt(2.0)))
        bell = jnp.exp(-0.5 * gate * gate) * (1.0 / math.sqrt(2.0 * math.pi))
        gelu = gate * share
        return gelu * up, back * up * (share + gate * bell), back * gelu

    for start in range(0, units, 256):
        stop = min(units, start + 256)
        gate = dot(work[...], whole[:, start:stop])
        up = dot(work[...], whole[:, units + start : units + stop])
        back = dot(cot[...], whole[:, 2 * units + start : 2 * units + stop])
        here, grad_gate, grad_up = grads(gate, up, back)
        hidden[:, start:stop] = here.astype(BF16)
        grad_proj[:, start:stop] = grad_gate.astype(BF16)
        grad_proj[:, units + start : units + stop] = grad_up.astype(BF16)
    tail = whole[:, 3 * units :]
    both = dot(work[...], tail)
    back = pltpu.roll(dot(cot[...], tail), LANES - 2 * spare, 1)
    parts = grads(both, pltpu.roll(both, LANES - spare, 1), back)
    lane = lane_of(*both.shape)
    here, grad_gate, grad_up = [jnp.where(lane < spare, part, 0.0) for part in parts]
    hidden[:, units:] = pltpu.roll(here, 2 * spare, 1).astype(BF16)
    grad_proj[:, 2 * units :] = (grad_gate + pltpu.roll(grad_up, spare, 1)).astype(BF16)
    grad_two[...] = (
        dot(grad_proj[:, : 2 * units], whole[:, : 2 * units], (1, 1))
        + dot(grad_proj[:, 2 * units :], tail, (1, 1))
    ).astype(BF16)
    down[...] = dot(hidden[...], whole[:, 2 * units :], (1, 1)).astype(BF16)
    if early:
        early_rows(early, chips, core, LANES, [(work, grad_proj), (cot, hidden)], None, *terms)


def attend_back_kernel(
    seq, residual, gains, grad_two, grad_two_other, cot, matrix, queries, keys_values,
    cosine, sine, grad_residual, grad_low, gain_two, grad_queries, grad_own, to_before, to_after,
    grad_all,
):
    rows, width = queries.shape
    unit, inverse = unit_of(residual[...])
    grad = grad_two[...].astype(F32) + grad_two_other[...].astype(F32)
    gain_two[...] = jnp.broadcast_to(jnp.sum(grad * unit, axis=0, keepdims=True), gain_two.shape)
    scaled = grad * gains[1:2, :]
    middle = jnp.mean(scaled, axis=-1, keepdims=True)
    along = jnp.mean(scaled * unit, axis=-1, keepdims=True)
    total = cot[...].astype(F32) + inverse * (scaled - middle - unit * along)
    grad_residual[...] = total
    grad_low[...] = total.astype(BF16)
    grad_context = dot(grad_low[...], matrix[...]).astype(BF16)
    grad_all[...] = jnp.zeros_like(grad_all)
    scale = 1.0 / math.sqrt(HD)
    tiles = rows // LANES
    for tile in range(tiles):
        inside = window(seq, tile, tiles)
        at = slice(tile * LANES, tile * LANES + LANES)
        own_at = slice(HALF + tile * LANES, HALF + tile * LANES + LANES)
        reach = slice(tile * LANES, tile * LANES + 2 * LANES)
        for start in range(0, width, LANES):
            columns = slice(start, start + LANES)
            beside = slice(width + start, width + start + LANES)
            apart = heads_apart(queries[at, columns])
            keys = keys_values[reach, columns]
            shares = shares_of(apart, keys, inside)
            grad_apart = heads_apart(grad_context[at, columns])
            grad_shares = dot(grad_apart, keys_values[reach, beside], (1, 1))
            lost = jnp.sum(grad_shares * shares, axis=-1, keepdims=True)
            grad_scores = (shares * (grad_shares - lost)).astype(BF16)
            grad_here = heads_joined(dot(grad_scores, keys)) * scale
            grad_queries[at, columns] = turned_by(grad_here, cosine[own_at], -sine[own_at]).astype(BF16)
            grad_all[reach, columns] += dot(grad_scores, apart, (0, 0)) * scale
            grad_all[reach, beside] += dot(shares.astype(BF16), grad_apart, (0, 0))
    to_before[...] = grad_all[:HALF].astype(BF16)
    grad_own[...] = grad_all[HALF : HALF + rows]
    to_after[...] = grad_all[HALF + rows :].astype(BF16)


def last_kernel(
    early, chips, core, grad_queries, grad_own, from_before, from_after, cosine, sine, tokens,
    gain_two, work, grad_low, context, matrix_whole, grad_qkv, grad_one, gain_columns, *refs,
):
    *parts, grad_all, matrix, ready = refs
    rows, width = grad_queries.shape
    fetch = pltpu.make_async_copy(matrix_whole.at[:, : 3 * width], matrix, ready)
    fetch.start()
    grad_all[...] = grad_own[...]
    grad_all[:HALF] += from_before[...].astype(F32)
    grad_all[rows - HALF :] += from_after[...].astype(F32)
    grad_qkv[:, :width] = grad_queries[...]
    own = slice(HALF, HALF + rows)
    grad_keys = turned_by(grad_all[:, :width], cosine[own], -sine[own])
    grad_qkv[:, width : 2 * width] = grad_keys.astype(BF16)
    grad_qkv[:, 2 * width :] = grad_all[:, width:].astype(BF16)
    fetch.wait()
    grad = dot(grad_qkv[...], matrix[...], (1, 1))
    grad_one[...] = grad.astype(BF16)
    unit, _ = unit_of(tokens[...].astype(F32))
    gain_one = jnp.sum(grad * unit, axis=0, keepdims=True)
    gain = jnp.concatenate([gain_one, gain_two[0:1, :]], axis=0)
    high = gain.astype(BF16).astype(F32)
    spare = jnp.zeros((LANES - 4, gain.shape[1]), F32)
    gain_columns[...] = jnp.concatenate([high, gain - high, spare], axis=0).T.astype(BF16)
    if early:
        pairs = [(work, grad_qkv), (grad_low, context)]
        early_rows(early, chips, core, 0, pairs, gain_columns, *parts)


def weight_rows(i, tail, lower, pairs, extra, kept, away):
    depth = kept.shape[1]

    def put(block, start, stop):
        kept[i, :, start:stop] = jnp.where(lower, block[:depth], block[depth:]).astype(BF16)
        away[i, :, start:stop] = jnp.where(lower, block[depth:], block[:depth]).astype(BF16)

    base = 0
    rest = 0.0
    for left, right in pairs:
        width = right.shape[1] - tail
        turned = left.T
        for start in range(0, width, 512):
            stop = min(width, start + 512)
            product = jnp.dot(turned, right[:, start:stop], preferred_element_type=F32)
            put(product, base + start, base + stop)
        base += width
        if tail:
            rest += jnp.dot(turned, right[:, width:], preferred_element_type=F32)
    if tail:
        put(rest, base, base + tail)
    if extra is not None:
        put(extra.astype(F32), base, base + extra.shape[1])


def early_rows(count, chips, core, tail, pairs, extra, kept, away):
    lower = core[0] == 0
    for i in range(count):
        lanes = pl.ds(pl.multiple_of(chips[i] * LANES, LANES), LANES)
        blocks = [(left[:, lanes], right) for left, right in pairs]
        more = None if extra is None else extra[lanes, :]
        weight_rows(i, tail, lower, blocks, more, kept, away)


def weight_kernel(tail, chips, core, left_one, left_two, right_one, right_two, *refs):
    pairs = [(left_one[...], right_one), (left_two[...], right_two)]
    extra = refs[0][...] if len(refs) == 3 else None
    weight_rows(0, tail, core[0] == 0, pairs, extra, *refs[-2:])


def weight_terms(ring, chips, core, skip, left_one, right_one, left_two, right_two, extra=None, tail=0, room=20):
    work_rows, width = left_one.shape
    lanes = width // ring.chips
    depth = lanes // 2
    total = right_one.shape[1] + right_two.shape[1] - tail
    more_args, more_specs = [], []
    if extra is not None:
        total += extra.shape[1]
        more_args.append(extra)
        more_specs.append(
            pl.BlockSpec((lanes, extra.shape[1]), lambda i, chips, core: (chips[i + skip], 0))
        )

    count = ring.chips - skip

    def left_map(i, chips, core):
        return (0, chips[i + skip])

    def whole_map(i, chips, core):
        return (0, 0)

    return pl.pallas_call(
        functools.partial(weight_kernel, tail),
        grid_spec=pltpu.PrefetchScalarGridSpec(
            num_scalar_prefetch=2,
            grid=(count,),
            in_specs=[
                pl.BlockSpec((work_rows, lanes), left_map),
                pl.BlockSpec((work_rows, lanes), left_map),
                pl.BlockSpec(right_one.shape, whole_map),
                pl.BlockSpec(right_two.shape, whole_map),
                *more_specs,
            ],
            out_specs=[
                pl.BlockSpec((1, depth, total), lambda i, chips, core: (i, 0, 0)),
                pl.BlockSpec((1, depth, total), lambda i, chips, core: (i, 0, 0)),
            ],
        ),
        out_shape=[
            pltpu.HBM((count, depth, total), BF16),
            pltpu.HBM((count, depth, total), BF16),
        ],
        compiler_params=pltpu.CompilerParams(vmem_limit_bytes=room * MIB),
        cost_estimate=pl.CostEstimate(
            flops=2 * work_rows * lanes * count * total // COST,
            bytes_accessed=2 * (lanes * count + work_rows) * total // COST,
            transcendentals=0,
        ),
    )(
        chips,
        core,
        left_one,
        left_two,
        right_one,
        right_two,
        *more_args,
    )


def summed_terms(left_one, right_one, left_two, right_two, extra=None, tail=0):
    yield from ()
    terms = [dot(left_one, right_one, (0, 0)), dot(left_two, right_two, (0, 0))]
    if tail:
        rest = terms[0][:, -tail:] + terms[1][:, -tail:]
        terms = [terms[0][:, :-tail], terms[1][:, :-tail], rest]
    terms = [t.astype(BF16) for t in terms] + ([] if extra is None else [extra])
    terms = jnp.concatenate(terms, axis=1)
    return lax.psum_scatter(terms, SEQ, scatter_dimension=0, tiled=True).astype(F32)


def norm_back(grad_rows, gain, unit_rows, inverse):
    scaled = grad_rows * gain
    centered_grad = (
        scaled
        - jnp.mean(scaled, axis=-1, keepdims=True)
        - unit_rows * jnp.mean(scaled * unit_rows, axis=-1, keepdims=True)
    )
    return inverse * centered_grad


def rotary_tables(positions):
    half_size = HD // 2
    frequency = THETA ** (-(jnp.arange(half_size, dtype=F32) * 2.0) / HD)
    angles = positions.astype(F32)[:, None] * frequency[None, :]
    return jnp.cos(angles), jnp.sin(angles)


def edge_rows(block):
    blocks = range(lax.axis_size(SEQ))
    route = [(2 * i, 2 * i - 2) for i in blocks if i > 0]
    route += [(2 * i + 1, 2 * i + 3) for i in blocks if i + 1 in blocks]
    return lax.ppermute(block, (SEQ, PAIR), route)


def pair_rows(mine, other):
    first = lax.axis_index(PAIR) == 0
    return jnp.concatenate([jnp.where(first, mine, other), jnp.where(first, other, mine)], axis=0)


def own_rows(values, row_count):
    return lax.dynamic_slice_in_dim(values, lax.axis_index(PAIR) * row_count, row_count, 0)


def other_rows(values, row_count):
    return lax.dynamic_slice_in_dim(values, (1 - lax.axis_index(PAIR)) * row_count, row_count, 0)


def dot(a, b, over=(1, 0)):
    return lax.dot_general(a, b, (((over[0],), (over[1],)), ((), ())), preferred_element_type=F32)


def padded_to_lanes(values):
    return jnp.pad(values, ((0, 0), (0, -values.shape[1] % LANES)))


def local(tokens, norm1_gain, w_qkv, w_attn_out, norm2_gain, w_in, w_down, cotangent):
    row_count, model_width = tokens.shape
    ring = Ring(model_width)
    early, early_last = (2, 3) if ring.short else (0, 0)
    chips, core = ring.chips_at(ring.slots), ring.core.reshape(1)
    depth, _, width = w_qkv.shape
    units = w_down.shape[0]
    gains = padded_to_lanes(jnp.stack([norm1_gain, norm2_gain], axis=1))
    blob_a = jnp.concatenate([w_qkv.reshape(depth, -1), w_attn_out.T, gains], axis=1)
    whole_units = units // LANES * LANES
    spare = units - whole_units
    parts = [w_in[:, 0], w_in[:, 1], w_down.T]
    blob_b = jnp.concatenate(
        [part[:, :whole_units] for part in parts] + [part[:, whole_units:] for part in parts], axis=1
    )
    blob_b = jnp.pad(blob_b, ((0, 0), (0, LANES - 3 * spare)))
    steps_a = Stepped(ring.gather(blob_a, "gather_a", [[0], [-1, 1], [], [-2]]))
    first = lax.axis_index(PAIR) == 0
    edge = edge_rows(jnp.where(first, tokens[:HALF], tokens[-HALF:]))
    edge = steps_a.hold(edge)
    joined = jnp.concatenate([tokens, edge, cotangent], axis=0)
    other = pair_swap(joined)
    steps_a.step()
    blob_b = steps_a.ride(blob_b)
    steps_b = Stepped(ring.gather(blob_b, "gather_b", [[], [], [0, -1, 1], [-2, 2]]))
    other = steps_a.hold(other)
    tokens_all = pair_rows(tokens, other[:row_count])
    beside = other[row_count : row_count + HALF]
    tokens_before = jnp.where(first, beside, edge)
    tokens_after = jnp.where(first, edge, beside)
    cot_all = pair_rows(cotangent, other[row_count + HALF :])

    work_rows = row_count * lax.axis_size(PAIR)
    reach_rows = work_rows + 2 * HALF
    seq = jnp.stack([lax.axis_index(SEQ), lax.axis_size(SEQ)]).astype(jnp.int32)
    cosine, sine = rotary_tables(
        seq[0] * work_rows - HALF + jnp.arange(reach_rows, dtype=jnp.int32)
    )
    inputs = tokens_all, tokens_before, tokens_after, cot_all, seq, cosine, sine, chips, core
    inputs = steps_a.hold(inputs)
    tokens_all, tokens_before, tokens_after, cot_all, seq, cosine, sine, chips, core = inputs
    steps_a.step()
    steps_a.beside(steps_b)
    pieces, starts = steps_a.finish()
    count = len(pieces)
    whole_a, attn_matrix, gains, work_one, queries, keys_values, *later = call(
        functools.partial(first_kernel, count, width),
        (starts, seq, tokens_all, tokens_before, tokens_after, cosine, sine, *pieces),
        [SMEM] * 2 + [VMEM] * 5 + [ANY] * count,
        [
            shape_of(model_width, blob_a.shape[1], BF16),
            shape_of(model_width, width, BF16),
            shape_of(8, model_width, F32),
            shape_of(work_rows, model_width, BF16),
            shape_of(work_rows, width, BF16),
            shape_of(reach_rows, 2 * width, BF16),
            shape_of(reach_rows, LANES, F32),
            shape_of(reach_rows, LANES, F32),
            shape_of(work_rows, width, BF16),
            shape_of(work_rows, model_width, BF16),
        ],
        [pltpu.VMEM((reach_rows, model_width), BF16), pltpu.SemaphoreType.DMA((count,))],
        flops=6 * work_rows * model_width * width,
        moved=16 * MIB,
        room=60,
    )
    cosine, sine, context, attn_term = later
    attn_term = steps_b.ride(attn_term)
    attn_other = steps_b.ride(pair_swap(attn_term))

    pieces, starts = steps_b.finish()
    count = len(pieces)
    residual, work_two, hidden, grad_proj, grad_two, down_term, *early_b = call(
        functools.partial(hidden_kernel, count, spare, early),
        (starts, chips, core, tokens_all, attn_term, attn_other, gains, cot_all, *pieces),
        [SMEM] * 3 + [VMEM] * 5 + [ANY] * count,
        [
            shape_of(work_rows, model_width, F32),
            shape_of(work_rows, model_width, BF16),
            shape_of(work_rows, whole_units + LANES, BF16),
            shape_of(work_rows, 2 * whole_units + LANES, BF16),
            shape_of(work_rows, model_width, BF16),
            shape_of(work_rows, model_width, BF16),
        ]
        + [pltpu.HBM((early, depth, blob_b.shape[1]), BF16)] * (2 if early else 0),
        [
            pltpu.VMEM((model_width, blob_b.shape[1]), BF16),
            pltpu.SemaphoreType.DMA((count,)),
        ],
        flops=12 * work_rows * model_width * units,
        moved=32 * MIB,
        room=60,
    )
    grad_two_other = pair_swap(grad_two)
    factors = work_two, grad_proj, cot_all, hidden
    if early:
        rest_b = weight_terms(ring, chips, core, early, *factors, tail=LANES, room=60)
        steps_b = Stepped(ring.scatter_sum(early_b, rest_b, "sum_b"))
    else:
        rest_b = ()
        steps_b = Stepped(summed_terms(*factors, tail=LANES))
    grad_two, rest_b = steps_b.ride((grad_two, rest_b))
    grad_residual, grad_low, gain_two, grad_queries, grad_own, to_before, to_after = call(
        attend_back_kernel,
        (
            seq, residual, gains, grad_two, grad_two_other, cot_all, attn_matrix,
            queries, keys_values, cosine, sine,
        ),
        [SMEM] + [VMEM] * 10,
        [
            pltpu.HBM((work_rows, model_width), F32),
            pltpu.HBM((work_rows, model_width), BF16),
            shape_of(8, model_width, F32),
            shape_of(work_rows, width, BF16),
            shape_of(work_rows, 2 * width, F32),
            pltpu.HBM((HALF, 2 * width), BF16),
            pltpu.HBM((HALF, 2 * width), BF16),
        ],
        [pltpu.VMEM((reach_rows, 2 * width), F32)],
        flops=4 * work_rows * model_width * width,
        moved=24 * MIB,
    )
    to_before, to_after = steps_b.ride((to_before, to_after))
    from_next = passed_along(to_before, SEQ, -1)
    from_prev = passed_along(to_after, SEQ, 1)

    down_other = pair_swap(other_rows(down_term, row_count))
    from_prev, from_next = steps_b.ride((from_prev, from_next))
    last = call(
        functools.partial(last_kernel, early_last),
        (
            chips, core, grad_queries, grad_own, from_prev, from_next, cosine, sine, tokens_all,
            gain_two, work_one, grad_low, context, whole_a,
        ),
        [SMEM] * 2 + [VMEM] * 11 + [ANY],
        [
            shape_of(work_rows, 3 * width, BF16),
            shape_of(work_rows, model_width, BF16),
            shape_of(model_width, LANES, BF16),
        ]
        + [pltpu.HBM((early_last, depth, blob_a.shape[1]), BF16)] * (2 if early else 0),
        [
            pltpu.VMEM((work_rows, 2 * width), F32),
            pltpu.VMEM((model_width, 3 * width), BF16),
            pltpu.SemaphoreType.DMA,
        ],
        flops=6 * work_rows * model_width * width,
        moved=16 * MIB,
        room=60,
    )
    last, down_other = steps_b.ride((tuple(last), down_other))
    grad_qkv, grad_one, gain_columns, *early_a = last
    one_other = pair_swap(other_rows(grad_one, row_count))
    grad_qkv = steps_b.ride(grad_qkv)
    factors = work_one, grad_qkv, grad_low, context, gain_columns
    if early:
        rest_a = weight_terms(ring, chips, core, early_last, *factors)
        steps_a = Stepped(ring.scatter_sum(early_a, rest_a, "sum_a"))
    else:
        steps_a = Stepped(summed_terms(*factors))
    steps_a.step()
    steps_a.beside(steps_b)
    steps_b.step()
    steps_a.step()
    one_other = steps_a.hold(one_other)
    steps_a.step()
    steps_a.step()
    steps_a.step()
    gain_parts = []
    if early:
        gain_parts.append(pair_swap(ring.own["sum_a"][:, 4 * width :]))
        for block, route in zip(steps_a.state, (ring.up, ring.down)):
            part = ring.go_across(block[:, 4 * width :], route, "gains_across")
            gain_parts.append(part.astype(F32))
    steps_a.beside(steps_b)
    share_b = steps_b.finish()
    share_a = steps_a.finish()

    output = (
        own_rows(residual, row_count)
        + (own_rows(down_term, row_count).astype(F32) + down_other.astype(F32))
    ).astype(BF16)

    gain_one = gains[0:1]
    unit_one, inverse_one = unit_of(tokens.astype(F32))
    grad_low_one = own_rows(grad_one, row_count).astype(F32) + one_other.astype(F32)
    grad_tokens = (
        own_rows(grad_residual, row_count)
        + norm_back(grad_low_one, gain_one, unit_one, inverse_one)
    ).astype(BF16)

    def share_b_part(part):
        tail = 3 * whole_units + part * spare
        main = share_b[:, part * whole_units : (part + 1) * whole_units]
        return jnp.concatenate([main, share_b[:, tail : tail + spare]], axis=1)

    share_gains = share_a[:, 4 * width : 4 * width + 2] + share_a[:, 4 * width + 2 : 4 * width + 4]
    share_gain_one = share_gains[:, 0]
    if early:
        others = sum(gain_parts)
        share_gain_one = share_gain_one + (others[:, 0] + others[:, 2])
    else:
        share_gain_one = share_gain_one + pair_swap(share_gain_one)
    return (
        output,
        grad_tokens,
        share_gain_one,
        share_a[:, : 3 * width].reshape(depth, 3, width),
        share_a[:, 3 * width : 4 * width].T,
        share_gains[:, 1],
        jnp.stack([share_b_part(0), share_b_part(1)], axis=1),
        share_b_part(2).T,
    )


def solution(mesh):
    return jax.shard_map(
        local,
        mesh=mesh,
        in_specs=(
            P((SEQ, PAIR), None),
            P(SEQ),
            P(SEQ, None, PAIR),
            P(PAIR, SEQ),
            P(SEQ),
            P(SEQ, None, PAIR),
            P(PAIR, SEQ),
            P((SEQ, PAIR), None),
        ),
        out_specs=(
            P((SEQ, PAIR), None),
            P((SEQ, PAIR), None),
            P(SEQ),
            P(SEQ, None, PAIR),
            P(PAIR, SEQ),
            P(SEQ),
            P(SEQ, None, PAIR),
            P(PAIR, SEQ),
        ),
        check_vma=False,
    )
```

```python
import functools
import math

import jax
import jax.numpy as jnp
import numpy as np
from jax import lax
from jax.experimental import pallas as pl
from jax.experimental.pallas import tpu as pltpu
from jax.sharding import PartitionSpec as P

HD = 64
HALF = 64
LANES = 128
COST = 1

EPSILON = 1e-05
THETA = 10000.0
SEQ = "seq"
PAIR = "fsdp"
F32 = jnp.float32
BF16 = jnp.bfloat16


def passed_along(block, axis, distance):
    devices = range(lax.axis_size(axis))
    route = [(i - distance, i) for i in devices if i - distance in devices]
    return lax.ppermute(block, axis, route)


def pair_swap(block):
    return lax.ppermute(block, PAIR, [(0, 1), (1, 0)])


class Ring:
    def __init__(self, width):
        size = lax.axis_size(SEQ)
        self.chips = size // 2
        rows = self.chips // 2
        order = [2 * z for z in range(rows)] + [2 * z + 1 for z in reversed(range(rows))]
        place = np.argsort(np.array(order))
        self.up, self.down = [], []
        for i in range(size):
            chip, core = divmod(i, 2)
            self.up.append((i, order[(place[chip] + 1) % self.chips] * 2 + core))
            self.down.append((i, order[(place[chip] - 1) % self.chips] * 2 + core))
        self.swap = [(i, i ^ 1) for i in range(size)]
        me = lax.axis_index(SEQ)
        self.core = me % 2
        self.place = jnp.asarray(place, jnp.int32)[me // 2]
        self.order = jnp.asarray(order, jnp.int32)
        self.half = self.chips // 2
        self.own = {}
        self.slots = [self.half]
        for step in range(1, self.half):
            self.slots += [self.half + step, self.half - step]
        self.slots.append(0)
        self.short = width == LANES * self.chips

    def chips_at(self, distances):
        steps = jnp.asarray(distances, jnp.int32)
        return self.order[(self.place + steps + self.chips) % self.chips]

    def go(self, block, route, name):
        with jax.named_scope(name):
            return lax.ppermute(block, SEQ, route)

    def go_across(self, block, route, name):
        both = [(2 * i + side, 2 * j + 1 - side) for i, j in route for side in (0, 1)]
        with jax.named_scope(name):
            return lax.ppermute(block, (SEQ, PAIR), both)

    def gather(self, block, name, plan):
        if not self.short:
            whole = lax.all_gather(block, SEQ, axis=0, tiled=True)
            return [whole], jnp.zeros(1, jnp.int32)
        rows = block.shape[0]
        middle = rows // 2
        upward = downward = block
        order = [0]
        for step in range(1, self.half + 1):
            order += [-step, step]
        places = [(d, 0, middle if d == self.half else 0) for d in order]
        places += [(d, 1, offset) for d, _, offset in places]
        distances, others, offsets = np.array(places, np.int32).T
        cores = self.chips_at(distances) * 2 + jnp.where(others == 1, 1 - self.core, self.core)
        starts = cores * rows + offsets
        held = {0: (block, 0)}
        swapped = {}
        for step in range(1, self.half + 1):
            if step == self.half:
                upward, downward = upward[:middle], downward[middle:]
            upward = self.go(upward, self.up, f"{name}_up_{step}")
            downward = self.go(downward, self.down, f"{name}_down_{step}")
            meanwhile = [d for d in plan[step - 1] if d in held]
            came = [self.go(held[d][0], self.swap, f"{name}_cores_{d}") for d in meanwhile]
            upward, downward, starts, *came = yield upward, downward, starts, *came
            swapped.update(zip(meanwhile, came))
            held[-step] = upward, 0
            held[step] = downward, middle if step == self.half else 0
        for d in held:
            if d not in swapped:
                swapped[d] = self.go(held[d][0], self.swap, f"{name}_cores_{d}")
        pieces = [held[d][0] for d in held] + [swapped[d] for d in held]
        return pieces, starts

    def scatter_sum(self, early, rest, name):
        kept_early, away_early = early
        kept_rest, away_rest = rest
        count, rows = kept_early.shape[:2]
        middle = rows // 2
        came_early = self.go(away_early, self.swap, f"{name}_cores_early")
        came_rest = self.go(away_rest, self.swap, f"{name}_cores_rest")

        def at(slot):
            i = self.slots.index(slot)
            if i < count:
                return kept_early[i].astype(F32) + came_early[i].astype(F32)
            return kept_rest[i - count].astype(F32) + came_rest[i - count].astype(F32)

        far = at(self.half).astype(BF16)
        upward, downward = far[:middle], far[middle:]
        for step in range(1, self.half + 1):
            if step == self.half:
                self.own[name] = at(0)
            upward, downward = yield upward, downward
            upward = self.go(upward, self.up, f"{name}_up_{step}")
            downward = self.go(downward, self.down, f"{name}_down_{step}")
            upward, downward = yield upward, downward
            upward, downward = upward.astype(F32), downward.astype(F32)
            if step == 1:
                upward = jnp.pad(upward, ((0, rows - middle), (0, 0)))
                downward = jnp.pad(downward, ((middle, 0), (0, 0)))
            if step < self.half:
                upward = (at(self.half - step) + upward).astype(BF16)
                downward = (at(self.half + step) + downward).astype(BF16)
        return at(0) + upward + downward


class Stepped:
    def __init__(self, steps):
        self.steps, self.state, self.result = steps, None, None
        self.advance()

    def advance(self):
        try:
            if self.state is not None:
                self.state = lax.optimization_barrier(self.state)
            self.state = self.steps.send(self.state)
        except StopIteration as end:
            self.steps, self.state, self.result = None, None, end.value

    def ride(self, value):
        if self.steps is not None:
            value, self.state = lax.optimization_barrier((value, self.state))
            self.advance()
        return value

    def hold(self, value):
        if self.steps is not None:
            value, self.state = lax.optimization_barrier((value, self.state))
        return value

    def step(self):
        if self.steps is not None:
            self.advance()

    def beside(self, other):
        if self.steps is not None and other.steps is not None:
            self.state, other.state = lax.optimization_barrier((self.state, other.state))
            self.advance()
            other.advance()

    def finish(self):
        while self.steps is not None:
            self.advance()
        return self.result


VMEM = pl.BlockSpec(memory_space=pltpu.VMEM)
ANY = pl.BlockSpec(memory_space=pltpu.HBM)
SMEM = pl.BlockSpec(memory_space=pltpu.SMEM)
MIB = 1024 * 1024


def shape_of(rows, columns, kind):
    return jax.ShapeDtypeStruct((rows, columns), kind)


def call(kernel, args, specs, outs, scratch=(), flops=0, moved=0, room=20):
    return pl.pallas_call(
        kernel,
        in_specs=specs,
        out_specs=[VMEM] * len(outs),
        out_shape=outs,
        scratch_shapes=list(scratch),
        compiler_params=pltpu.CompilerParams(vmem_limit_bytes=room * MIB),
        cost_estimate=pl.CostEstimate(
            flops=flops // COST, bytes_accessed=moved // COST, transcendentals=0
        ),
    )(*args)


def placing(starts, pieces, whole, ready):
    copies = []
    for i, piece in enumerate(pieces):
        rows = piece.shape[0]
        start = pl.multiple_of(starts[i], rows)
        copies.append(
            pltpu.make_async_copy(piece, whole.at[pl.ds(start, rows), :], ready.at[i])
        )
    return copies


def lane_of(rows, width):
    return lax.broadcasted_iota(jnp.int32, (rows, width), 1)


def halves_swapped(values):
    width = values.shape[1]
    lane = lane_of(*values.shape)
    ahead = pltpu.roll(values, width - HD // 2, 1)
    behind = pltpu.roll(values, HD // 2, 1)
    return jnp.where(lane % HD < HD // 2, ahead, behind)


def turned_by(values, cosine, sine):
    copies = values.shape[1] // LANES
    cosine = jnp.concatenate([cosine] * copies, axis=1)
    sine = jnp.concatenate([sine] * copies, axis=1)
    return values * cosine + halves_swapped(values) * sine


def unit_of(values):
    average = jnp.mean(values, axis=-1, keepdims=True)
    centered = values - average
    inverse = lax.rsqrt(jnp.mean(centered * centered, axis=-1, keepdims=True) + EPSILON)
    return centered * inverse, inverse


def first_kernel(count, width, starts, seq, tokens, before, after, cosine, sine, *refs):
    pieces = refs[:count]
    whole, matrix, gains, work, queries, keys_values, wide_cosine, wide_sine = refs[count:-4]
    context, term = refs[-4:-2]
    all_rows, ready = refs[-2:]
    copies = placing(starts, pieces, whole, ready)
    for copy in copies:
        copy.start()
    joined_rows(before, tokens, after, all_rows)
    wide_cosine[...] = jnp.concatenate([cosine[...]] * 4, axis=1)
    wide_sine[...] = jnp.concatenate([-sine[...], sine[...]] * 2, axis=1)
    unit, _ = unit_of(all_rows[...].astype(F32))
    for copy in copies:
        copy.wait()
    matrix[...] = whole[:, 3 * width : 4 * width]
    gains[...] = whole[:, 4 * width :].astype(F32).T[:8]
    all_rows[...] = (unit * gains[0:1, :]).astype(BF16)
    rows = work.shape[0]
    own = slice(HALF, HALF + rows)
    work[...] = all_rows[own, :]
    for start in range(0, 3 * width, 256):
        columns = whole[:, start : start + 256]
        if start < width:
            part = dot(work[...], columns)
            queries[:, start : start + 256] = turned_by(part, wide_cosine[own], wide_sine[own]).astype(BF16)
        else:
            part = dot(all_rows[...], columns)
            if start < 2 * width:
                part = turned_by(part, wide_cosine[...], wide_sine[...])
            keys_values[:, start - width : start - width + 256] = part.astype(BF16)
    attend(seq, queries, keys_values, matrix, context, term)


def window(seq, tile, tiles):
    row = lax.broadcasted_iota(jnp.int32, (2 * LANES, 2 * LANES), 0) % LANES
    column = lax.broadcasted_iota(jnp.int32, (2 * LANES, 2 * LANES), 1)
    ahead = column - row
    inside = (ahead >= 0) & (ahead <= 2 * HALF)
    if tile == 0:
        inside &= (seq[0] > 0) | (column >= HALF)
    if tile == tiles - 1:
        inside &= (seq[0] < seq[1] - 1) | (column < 2 * LANES - HALF)
    return inside


def heads_apart(pair):
    lane = lane_of(*pair.shape)
    zero = jnp.zeros_like(pair)
    return jnp.concatenate(
        [jnp.where(lane < HD, pair, zero), jnp.where(lane < HD, zero, pair)], axis=0
    )


def heads_joined(apart):
    rows = apart.shape[0] // 2
    return jnp.where(lane_of(rows, apart.shape[1]) < HD, apart[:rows], apart[rows:])


def shares_of(apart, keys, inside):
    scores = dot(apart, keys, (1, 1)) * (1.0 / math.sqrt(HD))
    scores = jnp.where(inside, scores, -1e30)
    expo = jnp.exp(scores - jnp.max(scores, axis=-1, keepdims=True))
    return expo / jnp.sum(expo, axis=-1, keepdims=True)


def joined_rows(before, own, after, whole):
    rows = own.shape[0]
    whole[:HALF] = before[...]
    whole[HALF : HALF + rows] = own[...]
    whole[HALF + rows :] = after[...]


def attend(seq, queries, keys_values, matrix, context, term):
    rows, width = queries.shape
    tiles = rows // LANES
    for tile in range(tiles):
        inside = window(seq, tile, tiles)
        at = slice(tile * LANES, tile * LANES + LANES)
        reach = slice(tile * LANES, tile * LANES + 2 * LANES)
        for start in range(0, width, LANES):
            columns = slice(start, start + LANES)
            apart = heads_apart(queries[at, columns])
            shares = shares_of(apart, keys_values[reach, columns], inside)
            values = keys_values[reach, width + start : width + start + LANES]
            context[at, columns] = heads_joined(dot(shares.astype(BF16), values)).astype(BF16)
    term[...] = dot(context[...], matrix[...], (1, 1)).astype(BF16)


def hidden_kernel(count, spare, early, starts, chips, core, tokens, term, term_other, gains, cot, *refs):
    pieces = refs[:count]
    residual, work, hidden, grad_proj, grad_two, down, *terms, whole, ready = refs[count:]
    copies = placing(starts, pieces, whole, ready)
    for copy in copies:
        copy.start()
    added = term[...].astype(F32) + term_other[...].astype(F32)
    residual[...] = tokens[...].astype(F32) + added
    unit, _ = unit_of(residual[...])
    work[...] = (unit * gains[1:2, :]).astype(BF16)
    for copy in copies:
        copy.wait()
    units = hidden.shape[1] - LANES

    def grads(gate, up, back):
        share = 0.5 + 0.5 * lax.erf(gate * (1.0 / math.sqrt(2.0)))
        bell = jnp.exp(-0.5 * gate * gate) * (1.0 / math.sqrt(2.0 * math.pi))
        gelu = gate * share
        return gelu * up, back * up * (share + gate * bell), back * gelu

    for start in range(0, units, 256):
        stop = min(units, start + 256)
        gate = dot(work[...], whole[:, start:stop])
        up = dot(work[...], whole[:, units + start : units + stop])
        back = dot(cot[...], whole[:, 2 * units + start : 2 * units + stop])
        here, grad_gate, grad_up = grads(gate, up, back)
        hidden[:, start:stop] = here.astype(BF16)
        grad_proj[:, start:stop] = grad_gate.astype(BF16)
        grad_proj[:, units + start : units + stop] = grad_up.astype(BF16)
    tail = whole[:, 3 * units :]
    both = dot(work[...], tail)
    back = pltpu.roll(dot(cot[...], tail), LANES - 2 * spare, 1)
    parts = grads(both, pltpu.roll(both, LANES - spare, 1), back)
    lane = lane_of(*both.shape)
    here, grad_gate, grad_up = [jnp.where(lane < spare, part, 0.0) for part in parts]
    hidden[:, units:] = pltpu.roll(here, 2 * spare, 1).astype(BF16)
    grad_proj[:, 2 * units :] = (grad_gate + pltpu.roll(grad_up, spare, 1)).astype(BF16)
    grad_two[...] = (
        dot(grad_proj[:, : 2 * units], whole[:, : 2 * units], (1, 1))
        + dot(grad_proj[:, 2 * units :], tail, (1, 1))
    ).astype(BF16)
    down[...] = dot(hidden[...], whole[:, 2 * units :], (1, 1)).astype(BF16)
    if early:
        early_rows(early, chips, core, LANES, [(work, grad_proj), (cot, hidden)], None, *terms)


def attend_back_kernel(
    seq, residual, gains, grad_two, grad_two_other, cot, matrix, queries, keys_values,
    cosine, sine, grad_residual, grad_low, gain_two, grad_queries, grad_own, to_before, to_after,
    grad_all,
):
    rows, width = queries.shape
    unit, inverse = unit_of(residual[...])
    grad = grad_two[...].astype(F32) + grad_two_other[...].astype(F32)
    gain_two[...] = jnp.broadcast_to(jnp.sum(grad * unit, axis=0, keepdims=True), gain_two.shape)
    scaled = grad * gains[1:2, :]
    middle = jnp.mean(scaled, axis=-1, keepdims=True)
    along = jnp.mean(scaled * unit, axis=-1, keepdims=True)
    total = cot[...].astype(F32) + inverse * (scaled - middle - unit * along)
    grad_residual[...] = total
    grad_low[...] = total.astype(BF16)
    grad_context = dot(grad_low[...], matrix[...]).astype(BF16)
    grad_all[...] = jnp.zeros_like(grad_all)
    scale = 1.0 / math.sqrt(HD)
    tiles = rows // LANES
    for tile in range(tiles):
        inside = window(seq, tile, tiles)
        at = slice(tile * LANES, tile * LANES + LANES)
        own_at = slice(HALF + tile * LANES, HALF + tile * LANES + LANES)
        reach = slice(tile * LANES, tile * LANES + 2 * LANES)
        for start in range(0, width, LANES):
            columns = slice(start, start + LANES)
            beside = slice(width + start, width + start + LANES)
            apart = heads_apart(queries[at, columns])
            keys = keys_values[reach, columns]
            shares = shares_of(apart, keys, inside)
            grad_apart = heads_apart(grad_context[at, columns])
            grad_shares = dot(grad_apart, keys_values[reach, beside], (1, 1))
            lost = jnp.sum(grad_shares * shares, axis=-1, keepdims=True)
            grad_scores = (shares * (grad_shares - lost)).astype(BF16)
            grad_here = heads_joined(dot(grad_scores, keys)) * scale
            grad_queries[at, columns] = turned_by(grad_here, cosine[own_at], -sine[own_at]).astype(BF16)
            grad_all[reach, columns] += dot(grad_scores, apart, (0, 0)) * scale
            grad_all[reach, beside] += dot(shares.astype(BF16), grad_apart, (0, 0))
    to_before[...] = grad_all[:HALF].astype(BF16)
    grad_own[...] = grad_all[HALF : HALF + rows]
    to_after[...] = grad_all[HALF + rows :].astype(BF16)


def last_kernel(
    early, chips, core, grad_queries, grad_own, from_before, from_after, cosine, sine, tokens,
    gain_two, work, grad_low, context, matrix_whole, grad_qkv, grad_one, gain_columns, *refs,
):
    *parts, grad_all, matrix, ready = refs
    rows, width = grad_queries.shape
    fetch = pltpu.make_async_copy(matrix_whole.at[:, : 3 * width], matrix, ready)
    fetch.start()
    grad_all[...] = grad_own[...]
    grad_all[:HALF] += from_before[...].astype(F32)
    grad_all[rows - HALF :] += from_after[...].astype(F32)
    grad_qkv[:, :width] = grad_queries[...]
    own = slice(HALF, HALF + rows)
    grad_keys = turned_by(grad_all[:, :width], cosine[own], -sine[own])
    grad_qkv[:, width : 2 * width] = grad_keys.astype(BF16)
    grad_qkv[:, 2 * width :] = grad_all[:, width:].astype(BF16)
    fetch.wait()
    grad = dot(grad_qkv[...], matrix[...], (1, 1))
    grad_one[...] = grad.astype(BF16)
    unit, _ = unit_of(tokens[...].astype(F32))
    gain_one = jnp.sum(grad * unit, axis=0, keepdims=True)
    gain = jnp.concatenate([gain_one, gain_two[0:1, :]], axis=0)
    high = gain.astype(BF16).astype(F32)
    spare = jnp.zeros((LANES - 4, gain.shape[1]), F32)
    gain_columns[...] = jnp.concatenate([high, gain - high, spare], axis=0).T.astype(BF16)
    if early:
        pairs = [(work, grad_qkv), (grad_low, context)]
        early_rows(early, chips, core, 0, pairs, gain_columns, *parts)


def weight_rows(i, tail, lower, pairs, extra, kept, away):
    depth = kept.shape[1]

    def put(block, start, stop):
        kept[i, :, start:stop] = jnp.where(lower, block[:depth], block[depth:]).astype(BF16)
        away[i, :, start:stop] = jnp.where(lower, block[depth:], block[:depth]).astype(BF16)

    base = 0
    rest = 0.0
    for left, right in pairs:
        width = right.shape[1] - tail
        turned = left.T
        for start in range(0, width, 512):
            stop = min(width, start + 512)
            product = jnp.dot(turned, right[:, start:stop], preferred_element_type=F32)
            put(product, base + start, base + stop)
        base += width
        if tail:
            rest += jnp.dot(turned, right[:, width:], preferred_element_type=F32)
    if tail:
        put(rest, base, base + tail)
    if extra is not None:
        put(extra.astype(F32), base, base + extra.shape[1])


def early_rows(count, chips, core, tail, pairs, extra, kept, away):
    lower = core[0] == 0
    for i in range(count):
        lanes = pl.ds(pl.multiple_of(chips[i] * LANES, LANES), LANES)
        blocks = [(left[:, lanes], right) for left, right in pairs]
        more = None if extra is None else extra[lanes, :]
        weight_rows(i, tail, lower, blocks, more, kept, away)


def weight_kernel(tail, chips, core, left_one, left_two, right_one, right_two, *refs):
    pairs = [(left_one[...], right_one), (left_two[...], right_two)]
    extra = refs[0][...] if len(refs) == 3 else None
    weight_rows(0, tail, core[0] == 0, pairs, extra, *refs[-2:])


def weight_terms(ring, chips, core, skip, left_one, right_one, left_two, right_two, extra=None, tail=0, room=20):
    work_rows, width = left_one.shape
    lanes = width // ring.chips
    depth = lanes // 2
    total = right_one.shape[1] + right_two.shape[1] - tail
    more_args, more_specs = [], []
    if extra is not None:
        total += extra.shape[1]
        more_args.append(extra)
        more_specs.append(
            pl.BlockSpec((lanes, extra.shape[1]), lambda i, chips, core: (chips[i + skip], 0))
        )

    count = ring.chips - skip

    def left_map(i, chips, core):
        return (0, chips[i + skip])

    def whole_map(i, chips, core):
        return (0, 0)

    return pl.pallas_call(
        functools.partial(weight_kernel, tail),
        grid_spec=pltpu.PrefetchScalarGridSpec(
            num_scalar_prefetch=2,
            grid=(count,),
            in_specs=[
                pl.BlockSpec((work_rows, lanes), left_map),
                pl.BlockSpec((work_rows, lanes), left_map),
                pl.BlockSpec(right_one.shape, whole_map),
                pl.BlockSpec(right_two.shape, whole_map),
                *more_specs,
            ],
            out_specs=[
                pl.BlockSpec((1, depth, total), lambda i, chips, core: (i, 0, 0)),
                pl.BlockSpec((1, depth, total), lambda i, chips, core: (i, 0, 0)),
            ],
        ),
        out_shape=[
            pltpu.HBM((count, depth, total), BF16),
            pltpu.HBM((count, depth, total), BF16),
        ],
        compiler_params=pltpu.CompilerParams(vmem_limit_bytes=room * MIB),
        cost_estimate=pl.CostEstimate(
            flops=2 * work_rows * lanes * count * total // COST,
            bytes_accessed=2 * (lanes * count + work_rows) * total // COST,
            transcendentals=0,
        ),
    )(
        chips,
        core,
        left_one,
        left_two,
        right_one,
        right_two,
        *more_args,
    )


def summed_terms(left_one, right_one, left_two, right_two, extra=None, tail=0):
    yield from ()
    terms = [dot(left_one, right_one, (0, 0)), dot(left_two, right_two, (0, 0))]
    if tail:
        rest = terms[0][:, -tail:] + terms[1][:, -tail:]
        terms = [terms[0][:, :-tail], terms[1][:, :-tail], rest]
    terms = [t.astype(BF16) for t in terms] + ([] if extra is None else [extra])
    terms = jnp.concatenate(terms, axis=1)
    return lax.psum_scatter(terms, SEQ, scatter_dimension=0, tiled=True).astype(F32)


def norm_back(grad_rows, gain, unit_rows, inverse):
    scaled = grad_rows * gain
    centered_grad = (
        scaled
        - jnp.mean(scaled, axis=-1, keepdims=True)
        - unit_rows * jnp.mean(scaled * unit_rows, axis=-1, keepdims=True)
    )
    return inverse * centered_grad


def rotary_tables(positions):
    half_size = HD // 2
    frequency = THETA ** (-(jnp.arange(half_size, dtype=F32) * 2.0) / HD)
    angles = positions.astype(F32)[:, None] * frequency[None, :]
    return jnp.cos(angles), jnp.sin(angles)


def edge_rows(block):
    blocks = range(lax.axis_size(SEQ))
    route = [(2 * i, 2 * i - 2) for i in blocks if i > 0]
    route += [(2 * i + 1, 2 * i + 3) for i in blocks if i + 1 in blocks]
    return lax.ppermute(block, (SEQ, PAIR), route)


def pair_rows(mine, other):
    first = lax.axis_index(PAIR) == 0
    return jnp.concatenate([jnp.where(first, mine, other), jnp.where(first, other, mine)], axis=0)


def own_rows(values, row_count):
    return lax.dynamic_slice_in_dim(values, lax.axis_index(PAIR) * row_count, row_count, 0)


def other_rows(values, row_count):
    return lax.dynamic_slice_in_dim(values, (1 - lax.axis_index(PAIR)) * row_count, row_count, 0)


def dot(a, b, over=(1, 0)):
    return lax.dot_general(a, b, (((over[0],), (over[1],)), ((), ())), preferred_element_type=F32)


def padded_to_lanes(values):
    return jnp.pad(values, ((0, 0), (0, -values.shape[1] % LANES)))


def local(tokens, norm1_gain, w_qkv, w_attn_out, norm2_gain, w_in, w_down, cotangent):
    row_count, model_width = tokens.shape
    ring = Ring(model_width)
    early, early_last = (2, 3) if ring.short else (0, 0)
    chips, core = ring.chips_at(ring.slots), ring.core.reshape(1)
    depth, _, width = w_qkv.shape
    units = w_down.shape[0]
    gains = padded_to_lanes(jnp.stack([norm1_gain, norm2_gain], axis=1))
    blob_a = jnp.concatenate([w_qkv.reshape(depth, -1), w_attn_out.T, gains], axis=1)
    whole_units = units // LANES * LANES
    spare = units - whole_units
    parts = [w_in[:, 0], w_in[:, 1], w_down.T]
    blob_b = jnp.concatenate(
        [part[:, :whole_units] for part in parts] + [part[:, whole_units:] for part in parts], axis=1
    )
    blob_b = jnp.pad(blob_b, ((0, 0), (0, LANES - 3 * spare)))
    steps_a = Stepped(ring.gather(blob_a, "gather_a", [[0], [-1, 1], [], [-2]]))
    first = lax.axis_index(PAIR) == 0
    edge = edge_rows(jnp.where(first, tokens[:HALF], tokens[-HALF:]))
    edge = steps_a.hold(edge)
    joined = jnp.concatenate([tokens, edge, cotangent], axis=0)
    other = pair_swap(joined)
    steps_a.step()
    blob_b = steps_a.ride(blob_b)
    steps_b = Stepped(ring.gather(blob_b, "gather_b", [[], [], [0, -1, 1], [-2, 2]]))
    other = steps_a.hold(other)
    tokens_all = pair_rows(tokens, other[:row_count])
    beside = other[row_count : row_count + HALF]
    tokens_before = jnp.where(first, beside, edge)
    tokens_after = jnp.where(first, edge, beside)
    cot_all = pair_rows(cotangent, other[row_count + HALF :])

    work_rows = row_count * lax.axis_size(PAIR)
    reach_rows = work_rows + 2 * HALF
    seq = jnp.stack([lax.axis_index(SEQ), lax.axis_size(SEQ)]).astype(jnp.int32)
    cosine, sine = rotary_tables(
        seq[0] * work_rows - HALF + jnp.arange(reach_rows, dtype=jnp.int32)
    )
    inputs = tokens_all, tokens_before, tokens_after, cot_all, seq, cosine, sine, chips, core
    inputs = steps_a.hold(inputs)
    tokens_all, tokens_before, tokens_after, cot_all, seq, cosine, sine, chips, core = inputs
    steps_a.step()
    steps_a.beside(steps_b)
    pieces, starts = steps_a.finish()
    count = len(pieces)
    whole_a, attn_matrix, gains, work_one, queries, keys_values, *later = call(
        functools.partial(first_kernel, count, width),
        (starts, seq, tokens_all, tokens_before, tokens_after, cosine, sine, *pieces),
        [SMEM] * 2 + [VMEM] * 5 + [ANY] * count,
        [
            shape_of(model_width, blob_a.shape[1], BF16),
            shape_of(model_width, width, BF16),
            shape_of(8, model_width, F32),
            shape_of(work_rows, model_width, BF16),
            shape_of(work_rows, width, BF16),
            shape_of(reach_rows, 2 * width, BF16),
            shape_of(reach_rows, LANES, F32),
            shape_of(reach_rows, LANES, F32),
            shape_of(work_rows, width, BF16),
            shape_of(work_rows, model_width, BF16),
        ],
        [pltpu.VMEM((reach_rows, model_width), BF16), pltpu.SemaphoreType.DMA((count,))],
        flops=6 * work_rows * model_width * width,
        moved=16 * MIB,
        room=60,
    )
    cosine, sine, context, attn_term = later
    attn_term = steps_b.ride(attn_term)
    attn_other = steps_b.ride(pair_swap(attn_term))

    pieces, starts = steps_b.finish()
    count = len(pieces)
    residual, work_two, hidden, grad_proj, grad_two, down_term, *early_b = call(
        functools.partial(hidden_kernel, count, spare, early),
        (starts, chips, core, tokens_all, attn_term, attn_other, gains, cot_all, *pieces),
        [SMEM] * 3 + [VMEM] * 5 + [ANY] * count,
        [
            shape_of(work_rows, model_width, F32),
            shape_of(work_rows, model_width, BF16),
            shape_of(work_rows, whole_units + LANES, BF16),
            shape_of(work_rows, 2 * whole_units + LANES, BF16),
            shape_of(work_rows, model_width, BF16),
            shape_of(work_rows, model_width, BF16),
        ]
        + [pltpu.HBM((early, depth, blob_b.shape[1]), BF16)] * (2 if early else 0),
        [
            pltpu.VMEM((model_width, blob_b.shape[1]), BF16),
            pltpu.SemaphoreType.DMA((count,)),
        ],
        flops=12 * work_rows * model_width * units,
        moved=32 * MIB,
        room=60,
    )
    grad_two_other = pair_swap(grad_two)
    factors = work_two, grad_proj, cot_all, hidden
    if early:
        rest_b = weight_terms(ring, chips, core, early, *factors, tail=LANES, room=60)
        steps_b = Stepped(ring.scatter_sum(early_b, rest_b, "sum_b"))
    else:
        rest_b = ()
        steps_b = Stepped(summed_terms(*factors, tail=LANES))
    grad_two, rest_b = steps_b.ride((grad_two, rest_b))
    grad_residual, grad_low, gain_two, grad_queries, grad_own, to_before, to_after = call(
        attend_back_kernel,
        (
            seq, residual, gains, grad_two, grad_two_other, cot_all, attn_matrix,
            queries, keys_values, cosine, sine,
        ),
        [SMEM] + [VMEM] * 10,
        [
            pltpu.HBM((work_rows, model_width), F32),
            pltpu.HBM((work_rows, model_width), BF16),
            shape_of(8, model_width, F32),
            shape_of(work_rows, width, BF16),
            shape_of(work_rows, 2 * width, F32),
            pltpu.HBM((HALF, 2 * width), BF16),
            pltpu.HBM((HALF, 2 * width), BF16),
        ],
        [pltpu.VMEM((reach_rows, 2 * width), F32)],
        flops=4 * work_rows * model_width * width,
        moved=24 * MIB,
    )
    to_before, to_after = steps_b.ride((to_before, to_after))
    from_next = passed_along(to_before, SEQ, -1)
    from_prev = passed_along(to_after, SEQ, 1)

    down_other = pair_swap(other_rows(down_term, row_count))
    from_prev, from_next = steps_b.ride((from_prev, from_next))
    last = call(
        functools.partial(last_kernel, early_last),
        (
            chips, core, grad_queries, grad_own, from_prev, from_next, cosine, sine, tokens_all,
            gain_two, work_one, grad_low, context, whole_a,
        ),
        [SMEM] * 2 + [VMEM] * 11 + [ANY],
        [
            shape_of(work_rows, 3 * width, BF16),
            shape_of(work_rows, model_width, BF16),
            shape_of(model_width, LANES, BF16),
        ]
        + [pltpu.HBM((early_last, depth, blob_a.shape[1]), BF16)] * (2 if early else 0),
        [
            pltpu.VMEM((work_rows, 2 * width), F32),
            pltpu.VMEM((model_width, 3 * width), BF16),
            pltpu.SemaphoreType.DMA,
        ],
        flops=6 * work_rows * model_width * width,
        moved=16 * MIB,
        room=28,
    )
    last, down_other = steps_b.ride((tuple(last), down_other))
    grad_qkv, grad_one, gain_columns, *early_a = last
    one_other = pair_swap(other_rows(grad_one, row_count))
    grad_qkv = steps_b.ride(grad_qkv)
    factors = work_one, grad_qkv, grad_low, context, gain_columns
    if early:
        rest_a = weight_terms(ring, chips, core, early_last, *factors)
        steps_a = Stepped(ring.scatter_sum(early_a, rest_a, "sum_a"))
    else:
        steps_a = Stepped(summed_terms(*factors))
    steps_a.step()
    steps_a.beside(steps_b)
    steps_b.step()
    steps_a.step()
    one_other = steps_a.hold(one_other)
    steps_a.step()
    steps_a.step()
    steps_a.step()
    gain_parts = []
    if early:
        gain_parts.append(pair_swap(ring.own["sum_a"][:, 4 * width :]))
        for block, route in zip(steps_a.state, (ring.up, ring.down)):
            part = ring.go_across(block[:, 4 * width :], route, "gains_across")
            gain_parts.append(part.astype(F32))
    steps_a.beside(steps_b)
    share_b = steps_b.finish()
    share_a = steps_a.finish()

    output = (
        own_rows(residual, row_count)
        + (own_rows(down_term, row_count).astype(F32) + down_other.astype(F32))
    ).astype(BF16)

    gain_one = gains[0:1]
    unit_one, inverse_one = unit_of(tokens.astype(F32))
    grad_low_one = own_rows(grad_one, row_count).astype(F32) + one_other.astype(F32)
    grad_tokens = (
        own_rows(grad_residual, row_count)
        + norm_back(grad_low_one, gain_one, unit_one, inverse_one)
    ).astype(BF16)

    def share_b_part(part):
        tail = 3 * whole_units + part * spare
        main = share_b[:, part * whole_units : (part + 1) * whole_units]
        return jnp.concatenate([main, share_b[:, tail : tail + spare]], axis=1)

    share_gains = share_a[:, 4 * width : 4 * width + 2] + share_a[:, 4 * width + 2 : 4 * width + 4]
    share_gain_one = share_gains[:, 0]
    if early:
        others = sum(gain_parts)
        share_gain_one = share_gain_one + (others[:, 0] + others[:, 2])
    else:
        share_gain_one = share_gain_one + pair_swap(share_gain_one)
    return (
        output,
        grad_tokens,
        share_gain_one,
        share_a[:, : 3 * width].reshape(depth, 3, width),
        share_a[:, 3 * width : 4 * width].T,
        share_gains[:, 1],
        jnp.stack([share_b_part(0), share_b_part(1)], axis=1),
        share_b_part(2).T,
    )


def solution(mesh):
    return jax.shard_map(
        local,
        mesh=mesh,
        in_specs=(
            P((SEQ, PAIR), None),
            P(SEQ),
            P(SEQ, None, PAIR),
            P(PAIR, SEQ),
            P(SEQ),
            P(SEQ, None, PAIR),
            P(PAIR, SEQ),
            P((SEQ, PAIR), None),
        ),
        out_specs=(
            P((SEQ, PAIR), None),
            P((SEQ, PAIR), None),
            P(SEQ),
            P(SEQ, None, PAIR),
            P(PAIR, SEQ),
            P(SEQ),
            P(SEQ, None, PAIR),
            P(PAIR, SEQ),
        ),
        check_vma=False,
    )
```
